32 devices in a mesh: dp: 16 (over z, y, x), table: 2 (over core).
Axes of the slice: x: 2, y: 2, z: 4, core: 2. Of those that a mesh axis runs over, the one named last changes fastest.
Arguments:
- item_table: bfloat16 [131072, 512], P(('dp', 'table')), may hold values from -6 to 6
- token_request_slot: int32 [8192], P(('dp', 'table')), may hold values from 0 to 255
- request_rows: int32 [32, 32, 8], P(('dp', 'table')), may hold values from 0 to 4095, as said below
- lengths: int32 [2, 64], P('table'), may hold values from 0 to 256, as said below
- assignment: int32 [2, 64], P('table'), may hold values from 0 to 15
- timestamps: int32 [8192], P(('dp', 'table')), may hold values from 1 to 524288, as said below
- item_counts: int32 [131072], P(('dp', 'table')), may hold values from 0 to 3
- first_norm_gain: float32 [512], replicated, may hold values from 0.5 to 1.5
- w_uvqk: bfloat16 [512, 2048], replicated, may hold values from -0.25 to 0.25
- b_uvqk: float32 [2048], replicated, may hold values from -2 to 2
- norm2_gain: float32 [512], replicated, may hold values from 0.5 to 1.5
- w_out: bfloat16 [512, 512], replicated, may hold values from -0.25 to 0.25
- b_out: float32 [512], replicated, may hold values from -2 to 2
- pos_weight: float32 [8, 10], replicated, may hold values from -2 to 2
- time_weight: float32 [8, 10], replicated, may hold values from -2 to 2
- out_grad: bfloat16 [8192, 512], P(('dp', 'table')), may hold values from -6 to 6
Outputs:
- layer_out: bfloat16 [8192, 512], P(('dp', 'table'))
- table_grad: float32 [131072, 512], P(('dp', 'table'))
- norm1_gain_grad: float32 [512], replicated
- w_uvqk_grad: float32 [512, 2048], replicated
- b_uvqk_grad: float32 [2048], replicated
- norm2_gain_grad: float32 [512], replicated
- w_out_grad: float32 [512, 512], replicated
- b_out_grad: float32 [512], replicated
- pos_weight_grad: float32 [8, 10], replicated
- time_weight_grad: float32 [8, 10], replicated
- new_counts: int32 [131072], P(('dp', 'table'))
- log_q: float32 [131072], P(('dp', 'table'))
The draws below stay inside these ranges and needn't reach their ends.
Inputs may be any that keep to these rules, and one draw needn't show every extreme that they name: `lengths`: in each table group the histories given to one dp index sum to at most 256 rows; each group has one history of 256 rows; 0 marks an unused entry. `request_rows`: the rows one device requests from one owner are distinct. `timestamps`: Non-decreasing within each device's 256 rows; both ends of the range are reached.
All inputs are finite; a program needn't handle non-finite values.
Results may differ from the reference program's by a relative error of at most 0.0079.
Values may be sent and summed in bfloat16 or wider, within the bound.
No kernel may reach another device: no remote copies, remote signals or barrier semaphores. Data moves between devices by JAX's collectives and lax.ppermute only.
A program may use at most 128 MiB of HBM per device.

```python
import math
import jax
import jax.numpy as jnp
import numpy as np
from jax import lax

D = 512
HEADS = 8
HEAD_DIM = 64
ROWS_DEV = 4096
SLOTS = 256
HPD = 4
NB = 10
NHIST = 64
CAP = 8
TOKENS = 8192
ITEMS = 131072
N_DP = 16
N_TABLE = 2
DEVICES = 32


def shuffle_one(key):
    return jax.random.permutation(key, NHIST).astype(jnp.int32)


def history_plan(key):
    keys = jax.random.split(key, 4)
    totals = jax.random.randint(keys[0], (N_TABLE, N_DP), SLOTS // 2, SLOTS + 1)
    cuts = jax.random.randint(keys[1], (N_TABLE, N_DP, HPD - 1), 0, SLOTS + 1)
    cuts = jnp.sort(jnp.minimum(cuts, totals[:, :, None]), axis=-1)
    full = jax.random.randint(keys[2], (N_TABLE, 1), 0, N_DP)
    whole = jnp.arange(N_DP, dtype=jnp.int32)[None, :] == full
    totals = jnp.where(whole, SLOTS, totals)
    cuts = jnp.where(whole[:, :, None], 0, cuts)
    edges = jnp.concatenate([jnp.zeros((N_TABLE, N_DP, 1), jnp.int32), cuts.astype(jnp.int32), totals[:, :, None].astype(jnp.int32)], axis=-1)
    entry_len = (edges[:, :, 1:] - edges[:, :, :-1]).reshape(N_TABLE, NHIST)
    orders = jax.vmap(shuffle_one)(jax.random.split(keys[3], N_TABLE))
    return (jnp.take_along_axis(entry_len, orders, axis=1).astype(jnp.int32), (orders // HPD).astype(jnp.int32))


def draw_lengths(key, part):
    return history_plan(key)[0]


def draw_assignment(key, part):
    return history_plan(key)[1]


def draw_request_rows(key, part):
    key = jax.random.fold_in(key, 3)
    first, second = jax.random.split(key)
    stride = ROWS_DEV // CAP
    base = jnp.arange(CAP, dtype=jnp.int32) * stride
    offset = jax.random.randint(first, (DEVICES, DEVICES, CAP), 1, stride)
    common = jax.random.randint(second, (DEVICES, DEVICES, CAP), 0, 4) == 0
    return (base[None, None, :] + jnp.where(common, 0, offset)).astype(jnp.int32)


def draw_timestamps(key, part):
    key = jax.random.fold_in(key, 5)
    powers = jax.random.randint(key, (DEVICES, SLOTS), 0, 12)
    gaps = jnp.left_shift(jnp.ones_like(powers), powers)
    times = jnp.cumsum(gaps, axis=1).astype(jnp.int32)
    times = times - jnp.min(times) + 1
    last = jnp.arange(SLOTS, dtype=jnp.int32)[None, :] == SLOTS - 1
    first_dev = jnp.arange(DEVICES, dtype=jnp.int32)[:, None] == 0
    times = jnp.where(last & first_dev, SLOTS * 2048, times)
    return times.reshape(TOKENS).astype(jnp.int32)


def with_ends(array, own_key, low, high):
    shape = array.shape
    spot = [jax.random.randint(jax.random.fold_in(own_key, axis), (), 0, shape[axis]) for axis in range(len(shape))]
    array = array.at[tuple(spot)].set(low)
    longest = shape.index(max(shape))
    spot[longest] = (spot[longest] + 1) % shape[longest]
    return array.at[tuple(spot)].set(high)


def levels(rng, extent, cuts, least, high):
    gain = 1.0
    for position, blocks in cuts:
        heights = jax.random.uniform(jax.random.fold_in(jax.random.fold_in(rng, 6), position), (blocks,), jnp.float32, least / len(cuts), high / len(cuts))
        gain = gain * jnp.repeat(jnp.exp(heights), extent[position] // blocks).reshape((-1,) + (1,) * (len(extent) - 1 - position))
    return gain


def cumulative_ranks(count, skew):
    portions = [(1 << 20) // math.isqrt(grade ** skew) + 1 for grade in range(1, count + 1)]
    scale = 1 + sum(portions) // (1 << 30)
    return np.cumsum(np.array([max(1, weight // scale) for weight in portions]))


def ranked_ids(stream_key, extent, amount, skew):
    grid = cumulative_ranks(amount, skew)
    ticket = jax.random.randint(jax.random.fold_in(stream_key, 1), extent, 0, int(grid[amount - 1]))
    standing = jnp.searchsorted(jnp.asarray(grid, jnp.int32), ticket, side="right")
    return jax.random.permutation(jax.random.fold_in(stream_key, 2), amount)[standing].astype(jnp.int32)


def gaussian(rng, extent, width, bound, pieces=(), held_as=jnp.bfloat16):
    values = jax.random.normal(rng, extent, jnp.float32) * width
    if len(pieces) > 0:
        values = levels(rng, extent, pieces, -0.22, 0.18) * values
    return jnp.clip(values, min=-bound, max=bound).astype(held_as)


def setup_inputs(seed: int = 0) -> dict:
    arg_keys = jax.random.split(jax.random.key(seed), 17)
    return {
        "item_table": gaussian(arg_keys[0], (ITEMS, D), 1.0, 6.0, ((0, 32),)),
        "token_request_slot": with_ends(ranked_ids(arg_keys[1], (TOKENS,), DEVICES * CAP, 1), jax.random.fold_in(arg_keys[1], 3), 0, (DEVICES * CAP) - 1).astype(jnp.int32),
        "request_rows": draw_request_rows(jax.random.fold_in(arg_keys[16], 71), 0),
        "lengths": draw_lengths(jax.random.fold_in(arg_keys[16], 71), 0),
        "assignment": draw_assignment(jax.random.fold_in(arg_keys[16], 71), 0),
        "timestamps": draw_timestamps(jax.random.fold_in(arg_keys[16], 71), 0),
        "item_counts": with_ends(jax.random.randint(arg_keys[6], (ITEMS,), 0, 4), jax.random.fold_in(arg_keys[6], 1), 0, 3).astype(jnp.int32),
        "first_norm_gain": jnp.clip(1.0 + 0.1 * jax.random.normal(arg_keys[7], (D,), jnp.float32), 0.5, 1.5),
        "w_uvqk": gaussian(arg_keys[8], (D, 4 * D), D ** -0.5, 0.25),
        "b_uvqk": gaussian(arg_keys[9], (4 * D,), 0.3, 2.0, (), jnp.float32),
        "norm2_gain": jnp.clip(1.0 + 0.1 * jax.random.normal(arg_keys[10], (D,), jnp.float32), 0.5, 1.5),
        "w_out": gaussian(arg_keys[11], (D, D), D ** -0.5, 0.25),
        "b_out": gaussian(arg_keys[12], (D,), 0.3, 2.0, (), jnp.float32),
        "pos_weight": gaussian(arg_keys[13], (HEADS, NB), 0.3, 2.0, (), jnp.float32),
        "time_weight": gaussian(arg_keys[14], (HEADS, NB), 0.3, 2.0, (), jnp.float32),
        "out_grad": gaussian(arg_keys[15], (TOKENS, D), 1.0, 6.0, ((0, 32),)),
    }


@jax.custom_vjp
def low(v):
    return lax.optimization_barrier(v.astype(jnp.bfloat16)).astype(jnp.float32)

@jax.custom_vjp
def low_back(v):
    return v

def low_keep(v):
    return (low(v), None)

def low_pass(kept, grad):
    return (grad,)

def back_keep(v):
    return (v, None)

def back_low(kept, grad):
    return (low(grad),)
low.defvjp(low_keep, low_pass)
low_back.defvjp(back_keep, back_low)
EPSILON = 1e-05
HIGH = lax.Precision.HIGHEST

def apply_rownorm(value):
    centered = value - lax.optimization_barrier(jnp.mean(value, axis=-1, keepdims=True))
    return centered * lax.rsqrt(lax.optimization_barrier(jnp.mean(centered * centered, axis=-1, keepdims=True)) + EPSILON)

def segments_of(hist_len, hist_dest, dest):
    mine = jnp.where(hist_dest == dest, hist_len, 0).astype(jnp.int32)
    ends = jnp.cumsum(mine).astype(jnp.int32)
    starts = ends - mine
    places = jnp.arange(SLOTS, dtype=jnp.int32)
    inside = (starts[None, :] <= places[:, None]) & (places[:, None] < ends[None, :])
    labels = jnp.arange(1, NHIST + 1, dtype=jnp.int32)
    return lax.optimization_barrier(jnp.sum(jnp.where(inside, labels[None, :], 0), axis=1)).astype(jnp.int32) - 1

def bias_of(stamps, pos_w, time_w):
    places = jnp.arange(SLOTS, dtype=jnp.int32)
    dist = places[:, None] - places[None, :]
    delta = stamps[:, None] - stamps[None, :]
    bias = jnp.zeros((HEADS, SLOTS, SLOTS), jnp.float32)
    for m in range(NB):
        near = (dist >= max(1, SLOTS // 2 ** (NB - m))).astype(jnp.float32)
        later = (delta >= 4 ** m).astype(jnp.float32)
        bias = bias + pos_w[:, m, None, None] * near[None] + time_w[:, m, None, None] * later[None]
    return (bias, dist)

def layer_device(params, xd, segd, stamps, vd):
    g1, w1, b1, g2, w2, b2, pos_w, time_w = params
    n1 = low(apply_rownorm(xd) * g1)
    pre = low_back(jnp.dot(n1, w1, precision=HIGH) + b1)
    act = jax.nn.silu(pre)
    gate_u = act[:, :D]
    values = low(act[:, D:2 * D]).reshape(SLOTS, HEADS, HEAD_DIM)
    queries = low(act[:, 2 * D:3 * D]).reshape(SLOTS, HEADS, HEAD_DIM)
    keys = low(act[:, 3 * D:]).reshape(SLOTS, HEADS, HEAD_DIM)
    bias, dist = bias_of(stamps, pos_w, time_w)
    mask = ((segd[:, None] == segd[None, :]) & (segd[:, None] >= 0) & (dist >= 0)).astype(jnp.float32)
    scores = low_back(jnp.einsum('qhd,khd->hqk', queries, keys, precision=HIGH) * 0.125 + bias)
    weights = low(jax.nn.silu(scores) * mask[None])
    attn = low_back(jnp.einsum('hqk,khd->qhd', weights, values, precision=HIGH).reshape(SLOTS, D))
    mixed = low(apply_rownorm(attn) * g2 * gate_u)
    return vd[:, None] * (xd + (jnp.dot(mixed, w2, precision=HIGH) + b2))

def reference(item_table, token_request_slot, request_rows, lengths, assignment, timestamps, item_counts, first_norm_gain, w_uvqk, b_uvqk, norm2_gain, w_out, b_out, pos_weight, time_weight, out_grad):
    groups = N_TABLE
    devices = N_DP * N_TABLE
    piece = SLOTS // N_DP
    rows = jnp.arange(TOKENS, dtype=jnp.int32)
    dest = rows // SLOTS
    place = rows % SLOTS
    dp_idx = dest // groups
    grp = dest % groups
    home_dev = place // piece * groups + grp
    home = home_dev * SLOTS + dp_idx * piece + place % piece
    slot = token_request_slot[home]
    owner = slot // CAP
    item = (owner * ROWS_DEV + request_rows[home_dev, owner, slot % CAP]).astype(jnp.int32)
    device_ids = jnp.arange(devices, dtype=jnp.int32)
    segment = jax.vmap(segments_of)(lengths[device_ids % groups], assignment[device_ids % groups], device_ids // groups)
    valid = (segment >= 0).astype(jnp.float32)
    stamps = timestamps.reshape(devices, SLOTS)

    def forward(table_f, g1, w1, b1, g2, w2, b2, pos_w, time_w):
        params = (g1, w1, b1, g2, w2, b2, pos_w, time_w)
        x = low_back(table_f[item]).reshape(devices, SLOTS, D)

        def one_device(pack):
            return layer_device(params, pack[0], pack[1], pack[2], pack[3])
        return lax.map(jax.checkpoint(one_device), (x, segment, stamps, valid)).reshape(TOKENS, D)
    layer_out, pullback = jax.vjp(forward, item_table.astype(jnp.float32), first_norm_gain, w_uvqk.astype(jnp.float32), b_uvqk, norm2_gain, w_out.astype(jnp.float32), b_out, pos_weight, time_weight)
    grads = pullback(out_grad.astype(jnp.float32))
    added = jax.ops.segment_sum(valid.reshape(TOKENS).astype(jnp.int32), item, num_segments=ITEMS)
    new_counts = (item_counts + added).astype(jnp.int32)
    total = jnp.sum(new_counts.astype(jnp.float32))
    log_q = jnp.log(new_counts.astype(jnp.float32) + 1.0) - jnp.log(total + ITEMS)
    return (layer_out.astype(jnp.bfloat16), grads[0], grads[1], grads[2], grads[3], grads[4], grads[5], grads[6], grads[7], grads[8], new_counts, log_q)
```

```python
import functools

import jax
import jax.numpy as jnp
from jax import lax
from jax.experimental import pallas as pl
from jax.experimental.pallas import tpu as pltpu
from jax.sharding import PartitionSpec as P

EPSILON = 1e-05
MASKED = -1e30
F32 = jnp.float32
BF16 = jnp.bfloat16
I32 = jnp.int32
BOTH = ("dp", "table")
LANES = 128
VMEM = pl.BlockSpec(memory_space=pltpu.VMEM)
SMEM = pl.BlockSpec(memory_space=pltpu.SMEM)
PARAMS = pltpu.CompilerParams(vmem_limit_bytes=48 * 1024 * 1024)


def dot_nn(a, b):
    return lax.dot_general(a, b, (((1,), (0,)), ((), ())), preferred_element_type=F32)


def dot_nt(a, b):
    return lax.dot_general(a, b, (((1,), (1,)), ((), ())), preferred_element_type=F32)


def dot_tn(a, b):
    return lax.dot_general(a, b, (((0,), (0,)), ((), ())), preferred_element_type=F32)


def dot_exact(a, b):
    return lax.dot_general(
        a, b, (((1,), (0,)), ((), ())), precision=lax.Precision.HIGHEST, preferred_element_type=F32
    )


def iota(shape, dim):
    return lax.broadcasted_iota(I32, shape, dim)


def shape_of(shape, dtype):
    return jax.ShapeDtypeStruct(shape, dtype)


def cost(flops, moved):
    return pl.CostEstimate(flops=int(flops), bytes_accessed=int(moved), transcendentals=0)


def call(body, outs, specs, flops, moved, scratch=()):
    many = isinstance(outs, tuple)
    return pl.pallas_call(
        body,
        out_shape=outs,
        in_specs=specs,
        out_specs=tuple(VMEM for _ in outs) if many else VMEM,
        scratch_shapes=list(scratch),
        compiler_params=PARAMS,
        cost_estimate=cost(flops, moved),
    )


def request_kernel(piece, cap, rows_ref, slot_ref, len_ref, dest_ref, counts_ref, msg_ref):
    owners = rows_ref.shape[0]
    tokens = slot_ref.shape[1]
    replicas = tokens // piece
    my_dp = lax.axis_index("dp")
    lens = len_ref[...].astype(F32)
    takes = dest_ref[...] == iota((replicas, dest_ref.shape[1]), 0)
    totals = jnp.sum(jnp.where(takes, lens, 0.0), axis=1, keepdims=True)
    token = iota((replicas, tokens), 1)
    target = iota((replicas, tokens), 0)
    place = (my_dp * piece + token - target * piece).astype(F32)
    here = (token >= target * piece) & (token < (target + 1) * piece) & (place < totals)
    valid = jnp.sum(jnp.where(here, 1.0, 0.0), axis=0, keepdims=True)
    slot = slot_ref[...]
    by_owner = jnp.where(slot // cap == iota((owners, tokens), 0), valid, 0.0).astype(BF16)
    by_slot = jnp.where(slot % cap + cap == iota((LANES, tokens), 0), 1.0, 0.0).astype(BF16)
    counts = dot_nt(by_owner, by_slot)
    old = jnp.sum(counts_ref[...].astype(F32), axis=0, keepdims=True)
    total = jnp.sum(old, axis=1, keepdims=True) + jnp.sum(valid, axis=1, keepdims=True)
    lane = iota((owners, LANES), 1)
    msg_ref[...] = jnp.where(lane == 2 * cap, total, counts).astype(I32)
    msg_ref[:, 0:cap] = rows_ref[...]


def asked_column(cap, asked_ref, first):
    askers = asked_ref.shape[0]
    total = askers * cap
    spread = jnp.where(iota((total, askers), 0) // cap == iota((total, askers), 1), 1.0, 0.0)
    each = dot_exact(spread, asked_ref[...].astype(F32))
    pick = iota((total, LANES), 1) == iota((total, LANES), 0) % cap + first
    return jnp.sum(jnp.where(pick, each, 0.0), axis=1, keepdims=True)


def serve_kernel(cap, asked_ref, table_ref, served_ref):
    rows = asked_column(cap, asked_ref, 0)
    total = rows.shape[0]
    step = min(512, table_ref.shape[0])
    lane = iota((total, step), 1).astype(F32)
    acc = None
    for base in range(0, table_ref.shape[0], step):
        pick = jnp.where(rows - float(base) == lane, 1.0, 0.0).astype(BF16)
        part = dot_nn(pick, table_ref[base : base + step, :])
        acc = part if acc is None else acc + part
    served_ref[...] = acc.astype(BF16)


def counts_kernel(cap, items, asked_ref, counts_ref, new_ref, log_ref, row_ref):
    rows = asked_column(cap, asked_ref, 0)
    added = asked_column(cap, asked_ref, cap)
    total = rows.shape[0]
    lines = counts_ref.shape[0]
    line = jnp.floor(rows * (1.0 / LANES))
    lane = rows - line * LANES
    by_line = jnp.where(line == iota((total, lines), 1).astype(F32), added, 0.0).astype(BF16)
    by_lane = jnp.where(lane == iota((total, LANES), 1).astype(F32), 1.0, 0.0).astype(BF16)
    new = counts_ref[...].astype(F32) + dot_tn(by_line, by_lane)
    whole = jnp.sum(asked_ref[:, 2 * cap : 2 * cap + 1].astype(F32), axis=0, keepdims=True)
    new_ref[...] = new.astype(I32)
    log_ref[...] = jnp.log(new + 1.0) - jnp.log(whole + float(items))
    row_ref[...] = jnp.transpose(jnp.broadcast_to(rows, (total, LANES)))[0:8, :]


def take_kernel(slot_ref, fetched_ref, home_ref):
    total = fetched_ref.shape[0]
    pick = jnp.where(slot_ref[...] == iota((total, slot_ref.shape[1]), 0), 1.0, 0.0).astype(BF16)
    home_ref[...] = dot_tn(pick, fetched_ref[...]).astype(BF16)


def slot_sum_kernel(slot_ref, back_ref, sums_ref):
    total = sums_ref.shape[0]
    pick = jnp.where(slot_ref[...] == iota((total, slot_ref.shape[1]), 0), 1.0, 0.0).astype(BF16)
    sums_ref[...] = dot_nn(pick, back_ref[...]).astype(BF16)


def scatter_kernel(row_ref, got_ref, out_ref):
    block = out_ref.shape[0]
    total = got_ref.shape[0]
    here = row_ref[0:1, :] - (pl.program_id(0) * block).astype(F32)
    pick = jnp.where(here == iota((block, total), 0).astype(F32), 1.0, 0.0).astype(BF16)
    out_ref[...] = dot_nn(pick, got_ref[...])


def before_kernel(
    len_ref, dest_ref, time_ref, og_ref, wo_ref, pos_ref, timew_ref, bias_ref, go_ref, dmix_ref, valid_ref
):
    rows = time_ref.shape[1]
    heads, count = pos_ref.shape
    nhist = len_ref.shape[1]
    my_dp = lax.axis_index("dp")
    mine = jnp.where(dest_ref[...] == my_dp, len_ref[...], 0).astype(F32)
    later = iota((nhist, nhist), 0)
    other = iota((nhist, nhist), 1)
    ends = jnp.sum(jnp.where(other <= later, mine, 0.0), axis=1, keepdims=True)
    starts = jnp.sum(jnp.where(other < later, mine, 0.0), axis=1, keepdims=True)
    place = iota((nhist, rows), 1).astype(F32)
    label = iota((nhist, rows), 0).astype(F32) + 1.0
    inside = (starts <= place) & (place < ends)
    seg = jnp.sum(jnp.where(inside, label, 0.0), axis=0, keepdims=True) - 1.0
    seg_across = jnp.broadcast_to(seg, (rows, rows))
    seg_down = jnp.transpose(seg_across)
    stamp = jnp.broadcast_to(time_ref[...].astype(F32), (rows, rows))
    delta = jnp.transpose(stamp) - stamp
    dist = iota((rows, rows), 0) - iota((rows, rows), 1)
    mask = (seg_across == seg_down) & (seg_down >= 0.0) & (dist >= 0)
    valid = jnp.where(seg_down[:, 0:LANES] >= 0.0, 1.0, 0.0)
    valid_ref[...] = valid
    wide = og_ref.shape[1] // LANES
    go = og_ref[...].astype(F32) * jnp.concatenate([valid] * wide, axis=1)
    gob = go.astype(BF16)
    go_ref[...] = gob
    dmix_ref[...] = dot_nt(gob, wo_ref[...])
    for g in range(heads):
        bias = jnp.zeros((rows, rows), F32)
        for m in range(count):
            bias = bias + jnp.where(dist >= max(1, rows // 2 ** (count - m)), pos_ref[g, m], 0.0)
            bias = bias + jnp.where(delta >= float(4**m), timew_ref[g, m], 0.0)
        bias_ref[g] = jnp.where(mask, bias, MASKED)


def norm_of(value):
    centered = value - jnp.mean(value, axis=1, keepdims=True)
    scale = lax.rsqrt(jnp.mean(centered * centered, axis=1, keepdims=True) + EPSILON)
    return centered * scale, scale


def norm_back(grad_hat, normed, scale):
    first = jnp.mean(grad_hat, axis=1, keepdims=True)
    second = jnp.mean(grad_hat * normed, axis=1, keepdims=True)
    return scale * (grad_hat - first - normed * second)


def sigmoid(value):
    return 1.0 / (1.0 + jnp.exp(-value))


def layer_kernel(
    staged,
    x_ref,
    w_ref,
    b_ref,
    g1_ref,
    g2_ref,
    wo_ref,
    bo_ref,
    bias_ref,
    dmix_ref,
    valid_ref,
    lo_ref,
    n1_ref,
    y_ref,
    dh_ref,
    ds_ref,
    g2g_ref,
    msg_ref,
    h_ref,
    slope_ref,
    a_ref,
):
    rows, width = x_ref.shape
    heads = bias_ref.shape[0]
    pairs = heads // 2
    x = x_ref[...].astype(F32)
    xhat, _ = norm_of(x)
    n1 = (xhat * g1_ref[...]).astype(BF16)
    n1_ref[...] = n1
    acts = []
    for part in range(4):
        cols = slice(part * width, (part + 1) * width)
        h = dot_nn(n1, w_ref[:, cols]) + b_ref[:, cols]
        sig = sigmoid(h)
        acts.append(h * sig)
        h_ref[:, cols] = sig * (1.0 + h * (1.0 - sig))
    u = acts[0]
    v, q, k = (a.astype(BF16) for a in acts[1:])
    lane = iota((rows, LANES), 1)
    low = lane < LANES // 2
    zero = jnp.zeros((rows, LANES), BF16)

    def half(value, parity):
        return jnp.where(low if parity == 0 else ~low, value, zero)

    outs = []
    for pair in range(pairs):
        cols = slice(pair * LANES, (pair + 1) * LANES)
        total = None
        for parity in range(2):
            g = pair * 2 + parity
            s = dot_nt(half(q[:, cols], parity), k[:, cols]) * 0.125 + bias_ref[g]
            sig = sigmoid(s)
            a = (s * sig).astype(BF16)
            a_ref[g] = a
            slope_ref[g] = sig * (1.0 + s * (1.0 - sig))
            part = dot_nn(a, half(v[:, cols], parity))
            total = part if total is None else total + part
        outs.append(total)
    o = jnp.concatenate(outs, axis=1)
    ohat, scale2 = norm_of(o)
    g2 = g2_ref[...]
    n2 = ohat * g2
    y = (n2 * u).astype(BF16)
    y_ref[...] = y
    branch = dot_nn(y, wo_ref[...]) + bo_ref[...]
    valid = valid_ref[...]
    lo_ref[...] = (jnp.concatenate([valid] * (width // LANES), axis=1) * (x + branch)).astype(BF16)
    dmix = dmix_ref[...]
    du = dmix * n2
    e2 = dmix * u
    g2g_ref[...] = jnp.sum(e2 * ohat, axis=0, keepdims=True)
    do = norm_back(e2 * g2, ohat, scale2).astype(BF16)
    dh_ref[:, 0:width] = (du * h_ref[:, 0:width]).astype(BF16)
    for pair in range(pairs):
        cols = slice(pair * LANES, (pair + 1) * LANES)
        dv, dq, dk = None, None, None
        for parity in range(2):
            g = pair * 2 + parity
            dom = half(do[:, cols], parity)
            da = dot_nt(dom, v[:, cols])
            ds = (da * slope_ref[g]).astype(BF16)
            ds_ref[g] = ds
            parts = (
                dot_tn(a_ref[g], dom),
                dot_nn(ds, half(k[:, cols], parity)),
                dot_tn(ds, half(q[:, cols], parity)),
            )
            if parity == 0:
                dv, dq, dk = parts
            else:
                dv, dq, dk = dv + parts[0], dq + parts[1], dk + parts[2]
        for part, value in ((1, dv), (2, dq * 0.125), (3, dk * 0.125)):
            at = slice(part * width + pair * LANES, part * width + (pair + 1) * LANES)
            dh_ref[:, at] = (value * h_ref[:, at]).astype(BF16)
    if staged:
        other = 1 - lax.axis_index("table")
        half_cols = 2 * width
        msg_ref[:, 0:half_cols] = dh_ref[:, pl.ds(pl.multiple_of(other * half_cols, half_cols), half_cols)]
        msg_ref[:, half_cols : half_cols + width] = n1
        half_y = width // 2
        msg_ref[:, half_cols + width :] = y_ref[:, pl.ds(pl.multiple_of(other * half_y, half_y), half_y)]
    else:
        msg_ref[...] = jnp.zeros_like(msg_ref)


def dx_kernel(dh_ref, w_ref, x_ref, g1_ref, go_ref, dx_ref, g1g_ref):
    xhat, scale = norm_of(x_ref[...].astype(F32))
    dn1 = dot_nt(dh_ref[...], w_ref[...])
    g1g_ref[...] = jnp.sum(dn1 * xhat, axis=0, keepdims=True)
    dx = norm_back(dn1 * g1_ref[...], xhat, scale) + go_ref[...].astype(F32)
    dx_ref[...] = dx.astype(BF16)


SMALL_ROWS = 48


def small_kernel(count, ds_ref, time_ref, dh_ref, go_ref, g1g_ref, g2g_ref, out_ref):
    heads, rows, _ = ds_ref.shape
    width = go_ref.shape[1]
    stamp = jnp.broadcast_to(time_ref[...].astype(F32), (rows, rows))
    delta = jnp.transpose(stamp) - stamp
    dist = iota((rows, rows), 0) - iota((rows, rows), 1)
    out_ref[...] = jnp.zeros_like(out_ref)
    b_grad = jnp.sum(dh_ref[...].astype(F32), axis=0, keepdims=True)
    go_sum = jnp.sum(go_ref[...].astype(F32), axis=0, keepdims=True)
    at = 0
    for value in (b_grad, g1g_ref[...], g2g_ref[...], go_sum):
        for col in range(0, value.shape[1], LANES):
            out_ref[at : at + 1, :] = value[:, col : col + LANES]
            at += 1
    at = (at + 7) // 8 * 8
    lane = iota((heads, LANES), 1)
    for base, which, bounds in (
        (at, dist, [max(1, rows // 2 ** (count - m)) for m in range(count)]),
        (at + heads, delta, [float(4**m) for m in range(count)]),
    ):
        result = jnp.zeros((heads, LANES), F32)
        done = {}
        for m, bound in enumerate(bounds):
            if bound not in done:
                sums = [
                    jnp.sum(jnp.where(which >= bound, ds_ref[g].astype(F32), 0.0), axis=0, keepdims=True)
                    for g in range(heads)
                ]
                done[bound] = jnp.sum(jnp.concatenate(sums, axis=0), axis=1, keepdims=True)
            result = jnp.where(lane == m, done[bound], result)
        out_ref[base : base + heads, :] = result


def pack_kernel(
    planes, columns, dh_ref, n1_ref, y_ref, go_ref, got_ref, got_go_ref, small_ref, *rest
):
    outs, (uv_ref, wo_ref) = rest[:columns], rest[columns:]
    rows, width = n1_ref.shape
    core = lax.axis_index("table")
    my_dp = lax.axis_index("dp")
    my_xy = lax.rem(my_dp, columns)
    my_z = lax.div(my_dp, columns)
    half_cols = 2 * width
    half_y = width // 2
    dh = jnp.concatenate(
        [dh_ref[:, pl.ds(pl.multiple_of(core * half_cols, half_cols), half_cols)], got_ref[:, 0:half_cols]],
        axis=0,
    )
    n1 = jnp.concatenate([n1_ref[...], got_ref[:, half_cols : half_cols + width]], axis=0)
    y = jnp.concatenate(
        [y_ref[:, pl.ds(pl.multiple_of(core * half_y, half_y), half_y)], got_ref[:, half_cols + width :]],
        axis=0,
    )
    go = jnp.concatenate([go_ref[...], got_go_ref[...]], axis=0)
    uv_ref[...] = dot_tn(n1, dh)
    wo_ref[...] = dot_tn(y, go)
    chunks = planes * columns
    tall = width // chunks
    short = tall // 2
    for rel_xy in range(columns):
        xy = jnp.bitwise_xor(my_xy, rel_xy)
        for rel_z in range(planes):
            z = jnp.bitwise_xor(my_z, rel_z)
            chunk = xy * planes + z
            at = pl.multiple_of(chunk * tall, tall)
            out = outs[rel_xy].at[rel_z]
            out[:, 0:half_cols] = uv_ref[pl.ds(at, short), :].astype(BF16)
            out[:, half_cols : 2 * half_cols] = uv_ref[
                pl.ds(pl.multiple_of(at + short, short), short), :
            ].astype(BF16)
            at = pl.multiple_of(chunk * short, short)
            out[:, 2 * half_cols : 2 * half_cols + width] = wo_ref[pl.ds(at, short), :].astype(BF16)
            out[:, 2 * half_cols + width :] = small_ref[pl.ds(at, short), :].astype(BF16)


def unpack_kernel(
    planes,
    columns,
    mine_ref,
    theirs_ref,
    uvqk_ref,
    wout_ref,
    b_ref,
    g1_ref,
    g2_ref,
    bo_ref,
    pos_ref,
    time_ref,
    small_ref,
):
    width = wout_ref.shape[0]
    core = lax.axis_index("table")
    my_dp = lax.axis_index("dp")
    my_xy = lax.rem(my_dp, columns)
    my_z = lax.div(my_dp, columns)
    half_cols = 2 * width
    half_y = width // 2
    tall = width // (planes * columns)
    short = tall // 2
    for rel_xy in range(columns):
        xy = jnp.bitwise_xor(my_xy, rel_xy)
        for rel_z in range(planes):
            z = jnp.bitwise_xor(my_z, rel_z)
            chunk = xy * planes + z
            at = pl.multiple_of(chunk * short, short)
            last = slice(2 * half_cols + width, 2 * half_cols + width + LANES)
            small_ref[pl.ds(at, short), :] = (
                mine_ref[rel_xy, rel_z, :, last].astype(F32) + theirs_ref[rel_xy, rel_z, :, last].astype(F32)
            )
            for ref, side in ((mine_ref, core), (theirs_ref, 1 - core)):
                cols = pl.ds(pl.multiple_of(side * half_cols, half_cols), half_cols)
                at = pl.multiple_of(chunk * tall, tall)
                uvqk_ref[pl.ds(at, short), cols] = ref[rel_xy, rel_z, :, 0:half_cols].astype(F32)
                at = pl.multiple_of(chunk * tall + short, short)
                uvqk_ref[pl.ds(at, short), cols] = ref[
                    rel_xy, rel_z, :, half_cols : 2 * half_cols
                ].astype(F32)
                at = pl.multiple_of(side * half_y + chunk * short, short)
                wout_ref[pl.ds(at, short), :] = ref[
                    rel_xy, rel_z, :, 2 * half_cols : 2 * half_cols + width
                ].astype(F32)
    at = 0
    for out in (b_ref, g1_ref, g2_ref, bo_ref):
        for col in range(0, out.shape[1], LANES):
            out[:, col : col + LANES] = small_ref[at : at + 1, :]
            at += 1
    at = (at + 7) // 8 * 8
    heads, count = pos_ref.shape
    pos_ref[...] = small_ref[at : at + heads, 0:count]
    time_ref[...] = small_ref[at + heads : at + 2 * heads, 0:count]


def add_up(first, *rest):
    total = first.astype(F32)
    for other in rest:
        total = total + other.astype(F32)
    return total.astype(BF16)


def xor_step(value, size, step):
    return lax.ppermute(value, "dp", [(i, i ^ step) for i in range(size)])


def staged_sum(pieces, planes, columns):
    size = planes * columns
    got = [xor_step(pieces[k], size, k) for k in range(1, columns)]
    line = add_up(pieces[0], *got)
    got = [xor_step(line[k], size, k * columns) for k in range(1, planes)]
    own = add_up(line[0], *got)
    line = jnp.stack([own] + [xor_step(own, size, k * columns) for k in range(1, planes)])
    return jnp.stack([line] + [xor_step(line, size, k) for k in range(1, columns)])


def swap_cores(value):
    return lax.ppermute(value, "table", [(0, 1), (1, 0)])


def on_device(
    item_table,
    token_request_slot,
    request_rows,
    lengths,
    assignment,
    timestamps,
    item_counts,
    first_norm_gain,
    w_uvqk,
    b_uvqk,
    norm2_gain,
    w_out,
    b_out,
    pos_weight,
    time_weight,
    out_grad,
):
    rows = token_request_slot.shape[0]
    rows_dev, width = item_table.shape
    replicas = lax.axis_size("dp")
    groups = lax.axis_size("table")
    devices = replicas * groups
    cap = request_rows.shape[2]
    piece = rows // replicas
    heads, count = pos_weight.shape
    slots = devices * cap
    columns = 4
    planes = replicas // columns
    staged = (
        groups == 2
        and replicas in (4, 8, 16)
        and width % (32 * replicas) == 0
        and (2 * heads + SMALL_ROWS - 16) <= width // 2
    )
    mb = 1 << 20

    slot_row = token_request_slot.reshape(1, rows)
    time_row = timestamps.reshape(1, rows)
    counts_2d = item_counts.reshape(rows_dev // LANES, LANES)
    msg = call(
        functools.partial(request_kernel, piece, cap),
        shape_of((devices, LANES), I32),
        [VMEM] * 5,
        mb,
        mb // 8,
    )(request_rows.reshape(devices, cap), slot_row, lengths, assignment, counts_2d)
    asked = lax.all_to_all(msg.reshape(devices, 1, LANES), BOTH, 0, 0, tiled=True).reshape(devices, LANES)
    bias, go, dmix, valid = call(
        before_kernel,
        (
            shape_of((heads, rows, rows), F32),
            shape_of((rows, width), BF16),
            shape_of((rows, width), F32),
            shape_of((rows, LANES), F32),
        ),
        [VMEM] * 5 + [SMEM] * 2,
        1 << 30,
        4 * mb,
    )(lengths, assignment, time_row, out_grad, w_out, pos_weight, time_weight)
    served = call(
        functools.partial(serve_kernel, cap), shape_of((slots, width), BF16), [VMEM] * 2, 1 << 30, 5 * mb
    )(asked, item_table)
    fetched = lax.all_to_all(served.reshape(devices, cap, width), BOTH, 0, 0, tiled=True)
    new_counts, log_q, asked_row = call(
        functools.partial(counts_kernel, cap, rows_dev * devices),
        (
            shape_of((rows_dev // LANES, LANES), I32),
            shape_of((rows_dev // LANES, LANES), F32),
            shape_of((8, slots), F32),
        ),
        [VMEM] * 2,
        64 * mb,
        mb,
    )(asked, counts_2d)
    home = call(take_kernel, shape_of((rows, width), BF16), [VMEM] * 2, 64 * mb, mb)(
        slot_row, fetched.reshape(slots, width)
    )
    x = lax.all_to_all(home.reshape(replicas, piece, width), "dp", 0, 0, tiled=True).reshape(rows, width)

    half_cols = 2 * width
    g1, g2 = first_norm_gain.reshape(1, width), norm2_gain.reshape(1, width)
    msg_cols = half_cols + width + width // 2 if staged else LANES
    layer_out, n1, y, dh, ds, g2_grad, to_core = call(
        functools.partial(layer_kernel, staged),
        (
            shape_of((rows, width), BF16),
            shape_of((rows, width), BF16),
            shape_of((rows, width), BF16),
            shape_of((rows, 4 * width), BF16),
            shape_of((heads, rows, rows), BF16),
            shape_of((1, width), F32),
            shape_of((rows, msg_cols), BF16),
        ),
        [VMEM] * 10,
        2 << 30,
        8 * mb,
        scratch=(
            pltpu.VMEM((rows, 4 * width), F32),
            pltpu.VMEM((heads, rows, rows), F32),
            pltpu.VMEM((heads, rows, rows), BF16),
        ),
    )(
        x,
        w_uvqk,
        b_uvqk.reshape(1, 4 * width),
        g1,
        g2,
        w_out,
        b_out.reshape(1, width),
        bias,
        dmix,
        valid,
    )
    if staged:
        got_go = swap_cores(go)
        got = swap_cores(to_core)
    dx, g1_grad = call(
        dx_kernel, (shape_of((rows, width), BF16), shape_of((1, width), F32)), [VMEM] * 5, 1 << 29, 4 * mb
    )(dh, w_uvqk, x, g1, go)
    back = lax.all_to_all(dx.reshape(replicas, piece, width), "dp", 0, 0, tiled=True).reshape(rows, width)
    small = call(
        functools.partial(small_kernel, count),
        shape_of((width // 2, LANES), F32),
        [VMEM] * 6,
        1 << 28,
        2 * mb,
    )(ds, time_row, dh, go, g1_grad, g2_grad)
    if staged:
        short = width // replicas // 2
        pack_cols = 2 * half_cols + width + LANES
        pieces = call(
            functools.partial(pack_kernel, planes, columns),
            tuple(shape_of((planes, short, pack_cols), BF16) for _ in range(columns)),
            [VMEM] * 7,
            1 << 30,
            6 * mb,
            scratch=(pltpu.VMEM((width, half_cols), F32), pltpu.VMEM((width // 2, width), F32)),
        )(dh, n1, y, go, got, got_go, small)
        mine = staged_sum(pieces, planes, columns)
        theirs = swap_cores(mine)
        w_uvqk_sum, w_out_sum, b_sum, g1_sum, g2_sum, bo_sum, pos_sum, time_sum = call(
            functools.partial(unpack_kernel, planes, columns),
            (
                shape_of((width, 4 * width), F32),
                shape_of((width, width), F32),
                shape_of((1, 4 * width), F32),
                shape_of((1, width), F32),
                shape_of((1, width), F32),
                shape_of((1, width), F32),
                shape_of((heads, count), F32),
                shape_of((heads, count), F32),
            ),
            [VMEM] * 2,
            mb,
            8 * mb,
            scratch=(pltpu.VMEM((width // 2, LANES), F32),),
        )(mine, theirs)
    else:
        w_uvqk_sum, w_out_sum, parts = lax.psum((dot_tn(n1, dh), dot_tn(y, go), small[0:SMALL_ROWS]), BOTH)
        at = 4 * width // LANES
        step = width // LANES
        b_sum = parts[0:at]
        g1_sum, g2_sum, bo_sum = (parts[at + n * step : at + (n + 1) * step] for n in range(3))
        at = (at + 3 * step + 7) // 8 * 8
        pos_sum = parts[at : at + heads, 0:count]
        time_sum = parts[at + heads : at + 2 * heads, 0:count]
    sums = call(slot_sum_kernel, shape_of((slots, width), BF16), [VMEM] * 2, 64 * mb, mb)(slot_row, back)
    got_sums = lax.all_to_all(sums.reshape(devices, cap, width), BOTH, 0, 0, tiled=True).reshape(slots, width)
    block = min(512, rows_dev)
    table_grad = pl.pallas_call(
        scatter_kernel,
        grid=(rows_dev // block,),
        out_shape=shape_of((rows_dev, width), F32),
        in_specs=[pl.BlockSpec((8, slots), lambda i: (0, 0)), pl.BlockSpec((slots, width), lambda i: (0, 0))],
        out_specs=pl.BlockSpec((block, width), lambda i: (i, 0)),
        compiler_params=PARAMS,
        cost_estimate=cost(1 << 30, 8 * mb),
    )(asked_row, got_sums)
    return (
        layer_out,
        table_grad,
        g1_sum.reshape(width),
        w_uvqk_sum,
        b_sum.reshape(4 * width),
        g2_sum.reshape(width),
        w_out_sum,
        bo_sum.reshape(width),
        pos_sum,
        time_sum,
        new_counts.reshape(rows_dev),
        log_q.reshape(rows_dev),
    )


def solution(mesh):
    split = P(("dp", "table"))
    rows_split = P(("dp", "table"), None)
    placed = (
        rows_split,
        split,
        P(("dp", "table"), None, None),
        P("table", None),
        P("table", None),
        split,
        split,
        P(),
        P(),
        P(),
        P(),
        P(),
        P(),
        P(),
        P(),
        rows_split,
    )
    return jax.shard_map(
        on_device,
        mesh=mesh,
        in_specs=placed,
        out_specs=(rows_split, rows_split, P(), P(), P(), P(), P(), P(), P(), P(), split, split),
        check_vma=False,
    )
```

```python
import functools

import jax
import jax.numpy as jnp
from jax import lax
from jax.experimental import pallas as pl
from jax.experimental.pallas import tpu as pltpu
from jax.sharding import PartitionSpec as P

EPSILON = 1e-05
MASKED = -1e30
F32 = jnp.float32
BF16 = jnp.bfloat16
I32 = jnp.int32
BOTH = ("dp", "table")
LANES = 128
VMEM = pl.BlockSpec(memory_space=pltpu.VMEM)
SMEM = pl.BlockSpec(memory_space=pltpu.SMEM)
HBM = pl.BlockSpec(memory_space=pltpu.HBM)
MIB = 1 << 20


def dot_nn(a, b):
    return lax.dot_general(a, b, (((1,), (0,)), ((), ())), preferred_element_type=F32)


def dot_nt(a, b):
    return lax.dot_general(a, b, (((1,), (1,)), ((), ())), preferred_element_type=F32)


def dot_tn(a, b):
    return lax.dot_general(a, b, (((0,), (0,)), ((), ())), preferred_element_type=F32)


def dot_exact(a, b):
    return lax.dot_general(
        a, b, (((1,), (0,)), ((), ())), precision=lax.Precision.HIGHEST, preferred_element_type=F32
    )


def iota(shape, dim):
    return lax.broadcasted_iota(I32, shape, dim)


def shape_of(shape, dtype):
    return jax.ShapeDtypeStruct(shape, dtype)


def cost(flops, moved):
    return pl.CostEstimate(flops=int(flops), bytes_accessed=int(moved), transcendentals=0)


def params(mib):
    return pltpu.CompilerParams(vmem_limit_bytes=mib * MIB)


def call(body, outs, specs, flops, moved, scratch=(), room=16, out_specs=None):
    if out_specs is None:
        out_specs = tuple(VMEM for _ in outs) if isinstance(outs, tuple) else VMEM
    return pl.pallas_call(
        body,
        out_shape=outs,
        in_specs=specs,
        out_specs=out_specs,
        scratch_shapes=list(scratch),
        compiler_params=params(room),
        cost_estimate=cost(flops, moved),
    )


def start_all(sources, targets, sems):
    copies = [pltpu.make_async_copy(a, b, sems.at[n]) for n, (a, b) in enumerate(zip(sources, targets))]
    for copy in copies:
        copy.start()
    return copies


def request_kernel(piece, cap, *refs):
    sources, msg_ref, held, sems = refs[:5], refs[5], refs[6:11], refs[11]
    for copy in start_all(sources, held, sems):
        copy.wait()
    rows_ref, slot_ref, len_ref, dest_ref, counts_ref = held
    owners = rows_ref.shape[1]
    tokens = slot_ref.shape[1]
    replicas = tokens // piece
    my_dp = lax.axis_index("dp")
    lens = len_ref[...].astype(F32)
    takes = dest_ref[...] == iota((replicas, dest_ref.shape[1]), 0)
    totals = jnp.sum(jnp.where(takes, lens, 0.0), axis=1, keepdims=True)
    token = iota((replicas, tokens), 1)
    target = iota((replicas, tokens), 0)
    place = (my_dp * piece + token - target * piece).astype(F32)
    here = (token >= target * piece) & (token < (target + 1) * piece) & (place < totals)
    valid = jnp.sum(jnp.where(here, 1.0, 0.0), axis=0, keepdims=True)
    slot = slot_ref[...]
    by_owner = jnp.where(slot // cap == iota((owners, tokens), 0), valid, 0.0).astype(BF16)
    by_slot = jnp.where(slot % cap + cap == iota((LANES, tokens), 0), 1.0, 0.0).astype(BF16)
    counts = dot_nt(by_owner, by_slot)
    old = jnp.sum(counts_ref[...].astype(F32), axis=0, keepdims=True)
    total = jnp.sum(old, axis=1, keepdims=True) + jnp.sum(valid, axis=1, keepdims=True)
    lane = iota((owners, LANES), 1)
    place = jnp.where(iota((cap, LANES), 0) == iota((cap, LANES), 1), 1.0, 0.0)
    wanted = dot_exact(jnp.transpose(rows_ref[...].astype(F32)), place)
    msg_ref[...] = (jnp.where(lane == 2 * cap, total, counts) + wanted).astype(I32)


def asked_column(cap, asked_ref, first):
    askers = asked_ref.shape[0]
    total = askers * cap
    spread = jnp.where(iota((total, askers), 0) // cap == iota((total, askers), 1), 1.0, 0.0)
    each = dot_exact(spread, asked_ref[...].astype(F32))
    pick = iota((total, LANES), 1) == iota((total, LANES), 0) % cap + first
    return jnp.sum(jnp.where(pick, each, 0.0), axis=1, keepdims=True)


def serve_kernel(cap, asked_ref, table_ref, served_ref):
    rows = asked_column(cap, asked_ref, 0)
    total = rows.shape[0]
    step = min(512, table_ref.shape[0])
    lane = iota((total, step), 1).astype(F32)
    acc = None
    for base in range(0, table_ref.shape[0], step):
        pick = jnp.where(rows - float(base) == lane, 1.0, 0.0).astype(BF16)
        part = dot_nn(pick, table_ref[base : base + step, :])
        acc = part if acc is None else acc + part
    served_ref[...] = acc.astype(BF16)


def counts_kernel(cap, items, asked_ref, counts_ref, new_ref, log_ref, row_ref):
    rows = asked_column(cap, asked_ref, 0)
    added = asked_column(cap, asked_ref, cap)
    total = rows.shape[0]
    lines = counts_ref.shape[0]
    line = jnp.floor(rows * (1.0 / LANES))
    lane = rows - line * LANES
    by_line = jnp.where(line == iota((total, lines), 1).astype(F32), added, 0.0).astype(BF16)
    by_lane = jnp.where(lane == iota((total, LANES), 1).astype(F32), 1.0, 0.0).astype(BF16)
    new = counts_ref[...].astype(F32) + dot_tn(by_line, by_lane)
    whole = jnp.sum(asked_ref[:, 2 * cap : 2 * cap + 1].astype(F32), axis=0, keepdims=True)
    new_ref[...] = new.astype(I32)
    log_ref[...] = jnp.log(new + 1.0) - jnp.log(whole + float(items))
    row_ref[...] = jnp.transpose(jnp.broadcast_to(rows, (total, LANES)))[0:8, :]


def take_kernel(slot_ref, fetched_ref, home_ref):
    total = fetched_ref.shape[0]
    pick = jnp.where(slot_ref[...] == iota((total, slot_ref.shape[1]), 0), 1.0, 0.0).astype(BF16)
    home_ref[...] = dot_tn(pick, fetched_ref[...]).astype(BF16)


def slot_sum_kernel(slot_ref, back_ref, sums_ref):
    total = sums_ref.shape[0]
    pick = jnp.where(slot_ref[...] == iota((total, slot_ref.shape[1]), 0), 1.0, 0.0).astype(BF16)
    sums_ref[...] = dot_nn(pick, back_ref[...]).astype(BF16)


def scatter_kernel(row_ref, got_ref, out_ref):
    block = out_ref.shape[0]
    total = got_ref.shape[0]
    here = row_ref[0:1, :] - (pl.program_id(0) * block).astype(F32)
    pick = jnp.where(here == iota((block, total), 0).astype(F32), 1.0, 0.0).astype(BF16)
    out_ref[...] = dot_nn(pick, got_ref[...])


def segments(len_ref, dest_ref, rows):
    nhist = len_ref.shape[1]
    mine = jnp.where(dest_ref[...] == lax.axis_index("dp"), len_ref[...], 0).astype(F32)
    later = iota((nhist, nhist), 0)
    other = iota((nhist, nhist), 1)
    ends = jnp.sum(jnp.where(other <= later, mine, 0.0), axis=1, keepdims=True)
    starts = jnp.sum(jnp.where(other < later, mine, 0.0), axis=1, keepdims=True)
    place = iota((nhist, rows), 1).astype(F32)
    label = iota((nhist, rows), 0).astype(F32) + 1.0
    return jnp.sum(jnp.where((starts <= place) & (place < ends), label, 0.0), axis=0, keepdims=True)


def valid_rows(seg, rows):
    return jnp.transpose(jnp.broadcast_to(jnp.where(seg > 0.0, 1.0, 0.0), (LANES, rows)))


def masked_grad(og_ref, valid):
    wide = og_ref.shape[1] // LANES
    return (og_ref[...].astype(F32) * jnp.concatenate([valid] * wide, axis=1)).astype(BF16)


def go_kernel(len_ref, dest_ref, og_ref, go_ref):
    rows = og_ref.shape[0]
    go_ref[...] = masked_grad(og_ref, valid_rows(segments(len_ref, dest_ref, rows), rows))


def hold_kernel(table_ref, held_ref, sems):
    parts = sems.shape[0]
    step = table_ref.shape[0] // parts
    blocks = [pl.ds(n * step, step) for n in range(parts)]
    for copy in start_all([table_ref.at[b, :] for b in blocks], [held_ref.at[b, :] for b in blocks], sems):
        copy.wait()


def pos_bounds(rows, count):
    return [max(1, rows // 2 ** (count - m)) for m in range(count)]


def time_bounds(count):
    return [float(4**m) for m in range(count)]


def time_gaps(time_ref, rows):
    stamp = jnp.broadcast_to(time_ref[...].astype(F32), (rows, rows))
    return jnp.transpose(stamp) - stamp


def steps_passed(value, bounds):
    total = jnp.where(value >= bounds[0], 1, 0)
    for bound in bounds[1:]:
        total = total + jnp.where(value >= bound, 1, 0)
    return total


def bias_index(seg, time_ref, rows, count):
    across = jnp.broadcast_to(seg, (rows, rows))
    down = jnp.transpose(across)
    dist = iota((rows, rows), 0) - iota((rows, rows), 1)
    near = steps_passed(dist, pos_bounds(rows, count))
    late = steps_passed(time_gaps(time_ref, rows), time_bounds(count))
    mask = (across == down) & (down > 0.0) & (dist >= 0)
    return jnp.where(mask, near * (count + 1) + late, LANES - 1)


def bias_table(pos_ref, timew_ref):
    heads, count = pos_ref.shape
    entry = iota((heads, LANES), 1)
    near = entry // (count + 1)
    late = entry - near * (count + 1)
    table = jnp.zeros((heads, LANES), F32)
    for m in range(count):
        table = table + jnp.where(near > m, pos_ref[:, m : m + 1], 0.0)
        table = table + jnp.where(late > m, timew_ref[:, m : m + 1], 0.0)
    return jnp.where(entry == LANES - 1, MASKED, table)


def look_up(table_row, index):
    rows, cols = index.shape
    spread = jnp.broadcast_to(table_row, (rows, LANES))
    return jnp.concatenate(
        [jnp.take_along_axis(spread, index[:, at : at + LANES], axis=1) for at in range(0, cols, LANES)], axis=1
    )


def norm_of(value):
    centered = value - jnp.mean(value, axis=1, keepdims=True)
    scale = lax.rsqrt(jnp.mean(centered * centered, axis=1, keepdims=True) + EPSILON)
    return centered * scale, scale


def norm_back(grad_hat, normed, scale):
    first = jnp.mean(grad_hat, axis=1, keepdims=True)
    second = jnp.mean(grad_hat * normed, axis=1, keepdims=True)
    return scale * (grad_hat - first - normed * second)


def sigmoid(value):
    return 1.0 / (1.0 + jnp.exp(-value))


def layer_kernel(
    staged,
    x_ref,
    w_ref,
    b_ref,
    g1_ref,
    g2_ref,
    wo_ref,
    bo_ref,
    len_ref,
    dest_ref,
    time_ref,
    og_ref,
    pos_ref,
    timew_ref,
    lo_ref,
    n1_ref,
    y_ref,
    dh_ref,
    ds_ref,
    g2g_ref,
    msg_ref,
    h_ref,
    slope_ref,
    a_ref,
):
    rows, width = x_ref.shape
    heads, count = pos_ref.shape
    pairs = heads // 2
    seg = segments(len_ref, dest_ref, rows)
    valid = valid_rows(seg, rows)
    dmix = dot_nt(masked_grad(og_ref, valid), wo_ref[...])
    index = bias_index(seg, time_ref, rows, count)
    table = bias_table(pos_ref, timew_ref)
    x = x_ref[...].astype(F32)
    xhat, _ = norm_of(x)
    n1 = (xhat * g1_ref[...]).astype(BF16)
    n1_ref[...] = n1
    acts = []
    for part in range(4):
        cols = slice(part * width, (part + 1) * width)
        h = dot_nn(n1, w_ref[:, cols]) + b_ref[:, cols]
        sig = sigmoid(h)
        acts.append(h * sig)
        h_ref[:, cols] = sig * (1.0 + h * (1.0 - sig))
    u = acts[0]
    v, q, k = (a.astype(BF16) for a in acts[1:])
    lane = iota((rows, LANES), 1)
    low = lane < LANES // 2
    zero = jnp.zeros((rows, LANES), BF16)

    def half(value, parity):
        return jnp.where(low if parity == 0 else ~low, value, zero)

    outs = []
    for pair in range(pairs):
        cols = slice(pair * LANES, (pair + 1) * LANES)
        total = None
        for parity in range(2):
            g = pair * 2 + parity
            s = dot_nt(half(q[:, cols], parity), k[:, cols]) * 0.125 + look_up(table[g : g + 1, :], index)
            sig = sigmoid(s)
            a = (s * sig).astype(BF16)
            a_ref[g] = a
            slope_ref[g] = sig * (1.0 + s * (1.0 - sig))
            part = dot_nn(a, half(v[:, cols], parity))
            total = part if total is None else total + part
        outs.append(total)
    o = jnp.concatenate(outs, axis=1)
    ohat, scale2 = norm_of(o)
    g2 = g2_ref[...]
    n2 = ohat * g2
    y = (n2 * u).astype(BF16)
    y_ref[...] = y
    branch = dot_nn(y, wo_ref[...]) + bo_ref[...]
    lo_ref[...] = (jnp.concatenate([valid] * (width // LANES), axis=1) * (x + branch)).astype(BF16)
    du = dmix * n2
    e2 = dmix * u
    g2g_ref[...] = jnp.sum(e2 * ohat, axis=0, keepdims=True)
    do = norm_back(e2 * g2, ohat, scale2).astype(BF16)
    dh_ref[:, 0:width] = (du * h_ref[:, 0:width]).astype(BF16)
    for pair in range(pairs):
        cols = slice(pair * LANES, (pair + 1) * LANES)
        dv, dq, dk = None, None, None
        for parity in range(2):
            g = pair * 2 + parity
            dom = half(do[:, cols], parity)
            da = dot_nt(dom, v[:, cols])
            ds = (da * slope_ref[g]).astype(BF16)
            ds_ref[g] = ds
            parts = (
                dot_tn(a_ref[g], dom),
                dot_nn(ds, half(k[:, cols], parity)),
                dot_tn(ds, half(q[:, cols], parity)),
            )
            if parity == 0:
                dv, dq, dk = parts
            else:
                dv, dq, dk = dv + parts[0], dq + parts[1], dk + parts[2]
        for part, value in ((1, dv), (2, dq * 0.125), (3, dk * 0.125)):
            at = slice(part * width + pair * LANES, part * width + (pair + 1) * LANES)
            dh_ref[:, at] = (value * h_ref[:, at]).astype(BF16)
    if staged:
        other = 1 - lax.axis_index("table")
        half_cols = 2 * width
        msg_ref[:, 0:half_cols] = dh_ref[:, pl.ds(pl.multiple_of(other * half_cols, half_cols), half_cols)]
        msg_ref[:, half_cols : half_cols + width] = n1
        half_y = width // 2
        msg_ref[:, half_cols + width :] = y_ref[:, pl.ds(pl.multiple_of(other * half_y, half_y), half_y)]
    else:
        msg_ref[...] = jnp.zeros_like(msg_ref)


def dx_kernel(dh_ref, w_ref, x_ref, g1_ref, go_ref, dx_ref, g1g_ref):
    xhat, scale = norm_of(x_ref[...].astype(F32))
    dn1 = dot_nt(dh_ref[...], w_ref[...])
    g1g_ref[...] = jnp.sum(dn1 * xhat, axis=0, keepdims=True)
    dx = norm_back(dn1 * g1_ref[...], xhat, scale) + go_ref[...].astype(F32)
    dx_ref[...] = dx.astype(BF16)


SMALL_ROWS = 48


def small_kernel(count, ds_ref, time_ref, dh_ref, go_ref, g1g_ref, g2g_ref, out_ref):
    heads, rows, _ = ds_ref.shape
    width = go_ref.shape[1]
    delta = time_gaps(time_ref, rows)
    dist = iota((rows, rows), 0) - iota((rows, rows), 1)
    out_ref[...] = jnp.zeros_like(out_ref)
    b_grad = jnp.sum(dh_ref[...].astype(F32), axis=0, keepdims=True)
    go_sum = jnp.sum(go_ref[...].astype(F32), axis=0, keepdims=True)
    at = 0
    for value in (b_grad, g1g_ref[...], g2g_ref[...], go_sum):
        for col in range(0, value.shape[1], LANES):
            out_ref[at : at + 1, :] = value[:, col : col + LANES]
            at += 1
    at = (at + 7) // 8 * 8
    lane = iota((heads, LANES), 1)
    for base, which, bounds in (
        (at, dist, pos_bounds(rows, count)),
        (at + heads, delta, time_bounds(count)),
    ):
        result = jnp.zeros((heads, LANES), F32)
        done = {}
        for m, bound in enumerate(bounds):
            if bound not in done:
                sums = [
                    jnp.sum(jnp.where(which >= bound, ds_ref[g].astype(F32), 0.0), axis=0, keepdims=True)
                    for g in range(heads)
                ]
                done[bound] = jnp.sum(jnp.concatenate(sums, axis=0), axis=1, keepdims=True)
            result = jnp.where(lane == m, done[bound], result)
        out_ref[base : base + heads, :] = result


def place_of(columns):
    my_dp = lax.axis_index("dp")
    return lax.rem(my_dp, columns), lax.div(my_dp, columns)


def pack_kernel(planes, columns, dh_ref, n1_ref, y_ref, go_ref, got_ref, got_go_ref, small_ref, *rest):
    outs, (uv_ref, wo_ref) = rest[:columns], rest[columns:]
    width = n1_ref.shape[1]
    core = lax.axis_index("table")
    my_xy, my_z = place_of(columns)
    half_cols = 2 * width
    half_y = width // 2
    dh = jnp.concatenate(
        [dh_ref[:, pl.ds(pl.multiple_of(core * half_cols, half_cols), half_cols)], got_ref[:, 0:half_cols]],
        axis=0,
    )
    n1 = jnp.concatenate([n1_ref[...], got_ref[:, half_cols : half_cols + width]], axis=0)
    y = jnp.concatenate(
        [y_ref[:, pl.ds(pl.multiple_of(core * half_y, half_y), half_y)], got_ref[:, half_cols + width :]],
        axis=0,
    )
    go = jnp.concatenate([go_ref[...], got_go_ref[...]], axis=0)
    uv_ref[...] = dot_tn(n1, dh)
    wo_ref[...] = dot_tn(y, go)
    short = half_y // (planes * columns)
    for rel_xy in range(columns):
        for rel_z in range(planes):
            chunk = jnp.bitwise_xor(my_xy, rel_xy) * planes + jnp.bitwise_xor(my_z, rel_z)
            out = outs[rel_xy].at[rel_z]
            for part in range(2):
                at = pl.multiple_of((2 * chunk + part) * short, short)
                out[:, part * half_cols : (part + 1) * half_cols] = uv_ref[pl.ds(at, short), :].astype(BF16)
            at = pl.multiple_of(chunk * short, short)
            out[:, 2 * half_cols : 2 * half_cols + width] = wo_ref[pl.ds(at, short), :].astype(BF16)
            out[:, 2 * half_cols + width :] = small_ref[pl.ds(at, short), :].astype(BF16)


def unpack_kernel(planes, columns, *refs):
    pieces = refs[: 2 * columns]
    uvqk_ref, wout_ref, b_ref, g1_ref, g2_ref, bo_ref, pos_ref, time_ref, small_ref = refs[2 * columns :]
    width = wout_ref.shape[0]
    core = lax.axis_index("table")
    my_xy, my_z = place_of(columns)
    half_cols = 2 * width
    half_y = width // 2
    short = half_y // (planes * columns)
    wout_lanes = slice(2 * half_cols, 2 * half_cols + width)
    small_lanes = slice(2 * half_cols + width, 2 * half_cols + width + LANES)
    for rel_xy in range(columns):
        for rel_z in range(planes):
            chunk = jnp.bitwise_xor(my_xy, rel_xy) * planes + jnp.bitwise_xor(my_z, rel_z)
            mine, theirs = (pieces[which * columns + rel_xy].at[rel_z] for which in range(2))
            for ref, side in ((mine, core), (theirs, 1 - core)):
                cols = pl.ds(pl.multiple_of(side * half_cols, half_cols), half_cols)
                for part in range(2):
                    at = pl.multiple_of((2 * chunk + part) * short, short)
                    uvqk_ref[pl.ds(at, short), cols] = ref[
                        :, part * half_cols : (part + 1) * half_cols
                    ].astype(F32)
                at = pl.multiple_of(side * half_y + chunk * short, short)
                wout_ref[pl.ds(at, short), :] = ref[:, wout_lanes].astype(F32)
            small_ref[pl.ds(pl.multiple_of(chunk * short, short), short), :] = mine[:, small_lanes].astype(
                F32
            ) + theirs[:, small_lanes].astype(F32)
    at = 0
    for out in (b_ref, g1_ref, g2_ref, bo_ref):
        for col in range(0, out.shape[1], LANES):
            out[:, col : col + LANES] = small_ref[at : at + 1, :]
            at += 1
    at = (at + 7) // 8 * 8
    heads, count = pos_ref.shape
    pos_ref[...] = small_ref[at : at + heads, 0:count]
    time_ref[...] = small_ref[at + heads : at + 2 * heads, 0:count]


def add_up(first, *rest):
    total = first.astype(F32)
    for other in rest:
        total = total + other.astype(F32)
    return total.astype(BF16)


def xor_step(value, size, step):
    return lax.ppermute(value, "dp", [(i, i ^ step) for i in range(size)])


def reduce_step(pieces, size, stride):
    return add_up(pieces[0], *(xor_step(pieces[k], size, k * stride) for k in range(1, len(pieces))))


def gather_step(own, size, stride, peers):
    return [own] + [xor_step(own, size, k * stride) for k in range(1, peers)]


def swap_cores(value):
    return lax.ppermute(value, "table", [(0, 1), (1, 0)])


def on_device(
    item_table,
    token_request_slot,
    request_rows,
    lengths,
    assignment,
    timestamps,
    item_counts,
    first_norm_gain,
    w_uvqk,
    b_uvqk,
    norm2_gain,
    w_out,
    b_out,
    pos_weight,
    time_weight,
    out_grad,
):
    rows = token_request_slot.shape[0]
    rows_dev, width = item_table.shape
    replicas = lax.axis_size("dp")
    groups = lax.axis_size("table")
    devices = replicas * groups
    cap = request_rows.shape[2]
    piece = rows // replicas
    heads, count = pos_weight.shape
    slots = devices * cap
    columns = 4
    planes = replicas // columns
    staged = (
        groups == 2
        and replicas in (4, 8, 16)
        and width % (32 * replicas) == 0
        and (2 * heads + SMALL_ROWS - 16) <= width // 2
    )
    mb = MIB

    slot_row = token_request_slot.reshape(1, rows)
    time_row = timestamps.reshape(1, rows)
    counts_2d = item_counts.reshape(rows_dev // LANES, LANES)
    msg = call(
        functools.partial(request_kernel, piece, cap),
        shape_of((devices, LANES), I32),
        [HBM] * 5,
        mb,
        mb // 8,
        scratch=(
            pltpu.VMEM((cap, devices), I32),
            pltpu.VMEM((1, rows), I32),
            pltpu.VMEM(lengths.shape, I32),
            pltpu.VMEM(lengths.shape, I32),
            pltpu.VMEM(counts_2d.shape, I32),
            pltpu.SemaphoreType.DMA((5,)),
        ),
        room=64,
    )(request_rows.transpose(0, 2, 1).reshape(cap, devices), slot_row, lengths, assignment, counts_2d)
    asked = lax.all_to_all(msg.reshape(devices, 1, LANES), BOTH, 0, 0, tiled=True).reshape(devices, LANES)
    held = call(
        hold_kernel,
        shape_of(item_table.shape, BF16),
        [HBM],
        0,
        8 * mb,
        scratch=(pltpu.SemaphoreType.DMA((8,)),),
    )(item_table)
    asked, held = lax.optimization_barrier((asked, held))
    served = call(
        functools.partial(serve_kernel, cap), shape_of((slots, width), BF16), [VMEM] * 2, 1 << 30, 5 * mb
    )(asked, held)
    go = call(go_kernel, shape_of((rows, width), BF16), [VMEM] * 3, 64 * mb, mb)(lengths, assignment, out_grad)
    fetched = lax.all_to_all(served.reshape(devices, cap, width), BOTH, 0, 0, tiled=True)
    new_counts, log_q, asked_row = call(
        functools.partial(counts_kernel, cap, rows_dev * devices),
        (
            shape_of((rows_dev // LANES, LANES), I32),
            shape_of((rows_dev // LANES, LANES), F32),
            shape_of((8, slots), F32),
        ),
        [VMEM] * 2,
        64 * mb,
        mb,
    )(asked, counts_2d)
    home = call(take_kernel, shape_of((rows, width), BF16), [VMEM] * 2, 64 * mb, mb)(
        slot_row, fetched.reshape(slots, width)
    )
    if staged:
        got_go = swap_cores(go)
    x = lax.all_to_all(home.reshape(replicas, piece, width), "dp", 0, 0, tiled=True).reshape(rows, width)
    if staged:
        x, got_go = lax.optimization_barrier((x, got_go))

    half_cols = 2 * width
    g1, g2 = first_norm_gain.reshape(1, width), norm2_gain.reshape(1, width)
    msg_cols = half_cols + width + width // 2 if staged else LANES
    layer_out, n1, y, dh, ds, g2_grad, to_core = call(
        functools.partial(layer_kernel, staged),
        (
            shape_of((rows, width), BF16),
            shape_of((rows, width), BF16),
            shape_of((rows, width), BF16),
            shape_of((rows, 4 * width), BF16),
            shape_of((heads, rows, rows), BF16),
            shape_of((1, width), F32),
            shape_of((rows, msg_cols), BF16),
        ),
        [VMEM] * 13,
        2 << 30,
        8 * mb,
        scratch=(
            pltpu.VMEM((rows, 4 * width), F32),
            pltpu.VMEM((heads, rows, rows), F32),
            pltpu.VMEM((heads, rows, rows), BF16),
        ),
        room=24,
    )(
        x,
        w_uvqk,
        b_uvqk.reshape(1, 4 * width),
        g1,
        g2,
        w_out,
        b_out.reshape(1, width),
        lengths,
        assignment,
        time_row,
        out_grad,
        pos_weight,
        time_weight,
    )
    def home_again(dx):
        return lax.all_to_all(dx.reshape(replicas, piece, width), "dp", 0, 0, tiled=True).reshape(rows, width)

    def to_owners(back):
        sums = call(slot_sum_kernel, shape_of((slots, width), BF16), [VMEM] * 2, 64 * mb, mb)(slot_row, back)
        sums = lax.all_to_all(sums.reshape(devices, cap, width), BOTH, 0, 0, tiled=True)
        return sums.reshape(slots, width)

    def into_table(got_sums):
        block = min(512, rows_dev)
        return pl.pallas_call(
            scatter_kernel,
            grid=(rows_dev // block,),
            out_shape=shape_of((rows_dev, width), F32),
            in_specs=[pl.BlockSpec((8, slots), lambda i: (0, 0)), pl.BlockSpec((slots, width), lambda i: (0, 0))],
            out_specs=pl.BlockSpec((block, width), lambda i: (i, 0)),
            compiler_params=params(16),
            cost_estimate=cost(1 << 30, 8 * mb),
        )(asked_row, got_sums)

    if staged:
        got = swap_cores(to_core)
    dx, g1_grad = call(
        dx_kernel, (shape_of((rows, width), BF16), shape_of((1, width), F32)), [VMEM] * 5, 1 << 29, 4 * mb
    )(dh, w_uvqk, x, g1, go)
    small = call(
        functools.partial(small_kernel, count),
        shape_of((width // 2, LANES), F32),
        [VMEM] * 6,
        1 << 28,
        2 * mb,
    )(ds, time_row, dh, go, g1_grad, g2_grad)
    if staged:
        short = width // replicas // 2
        pieces = call(
            functools.partial(pack_kernel, planes, columns),
            tuple(shape_of((planes, short, 5 * width + LANES), BF16) for _ in range(columns)),
            [VMEM] * 7,
            1 << 30,
            6 * mb,
            scratch=(pltpu.VMEM((width, half_cols), F32), pltpu.VMEM((width // 2, width), F32)),
        )(dh, n1, y, go, got, got_go, small)
        dx, *pieces = lax.optimization_barrier((dx, *pieces))
        back = home_again(dx)
        line = reduce_step(pieces, replicas, 1)
        line, back = lax.optimization_barrier((line, back))
        got_sums = to_owners(back)
        own = reduce_step(line, replicas, columns)
        line = jnp.stack(gather_step(own, replicas, columns, planes))
        line, got_sums = lax.optimization_barrier((line, got_sums))
        table_grad = into_table(got_sums)
        mine = gather_step(line, replicas, 1, columns)
        theirs = [swap_cores(line)]
        mine, theirs, table_grad = lax.optimization_barrier((mine, theirs, table_grad))
        theirs += [swap_cores(piece) for piece in mine[1:]]
        w_uvqk_sum, w_out_sum, b_sum, g1_sum, g2_sum, bo_sum, pos_sum, time_sum = call(
            functools.partial(unpack_kernel, planes, columns),
            (
                shape_of((width, 4 * width), F32),
                shape_of((width, width), F32),
                shape_of((1, 4 * width), F32),
                shape_of((1, width), F32),
                shape_of((1, width), F32),
                shape_of((1, width), F32),
                shape_of((heads, count), F32),
                shape_of((heads, count), F32),
            ),
            [VMEM] * (2 * columns),
            mb,
            8 * mb,
            scratch=(pltpu.VMEM((width // 2, LANES), F32),),
        )(*mine, *theirs)
    else:
        table_grad = into_table(to_owners(home_again(dx)))
        w_uvqk_sum, w_out_sum, parts = lax.psum((dot_tn(n1, dh), dot_tn(y, go), small[0:SMALL_ROWS]), BOTH)
        at = 4 * width // LANES
        step = width // LANES
        b_sum = parts[0:at]
        g1_sum, g2_sum, bo_sum = (parts[at + n * step : at + (n + 1) * step] for n in range(3))
        at = (at + 3 * step + 7) // 8 * 8
        pos_sum = parts[at : at + heads, 0:count]
        time_sum = parts[at + heads : at + 2 * heads, 0:count]
    return (
        layer_out,
        table_grad,
        g1_sum.reshape(width),
        w_uvqk_sum,
        b_sum.reshape(4 * width),
        g2_sum.reshape(width),
        w_out_sum,
        bo_sum.reshape(width),
        pos_sum,
        time_sum,
        new_counts.reshape(rows_dev),
        log_q.reshape(rows_dev),
    )


def solution(mesh):
    split = P(("dp", "table"))
    rows_split = P(("dp", "table"), None)
    placed = (
        rows_split,
        split,
        P(("dp", "table"), None, None),
        P("table", None),
        P("table", None),
        split,
        split,
        P(),
        P(),
        P(),
        P(),
        P(),
        P(),
        P(),
        P(),
        rows_split,
    )
    return jax.shard_map(
        on_device,
        mesh=mesh,
        in_specs=placed,
        out_specs=(rows_split, rows_split, P(), P(), P(), P(), P(), P(), P(), P(), split, split),
        check_vma=False,
    )
```

```python
import functools

import jax
import jax.numpy as jnp
from jax import lax
from jax.experimental import pallas as pl
from jax.experimental.pallas import tpu as pltpu
from jax.sharding import PartitionSpec as P

EPSILON = 1e-05
MASKED = -1e30
F32 = jnp.float32
BF16 = jnp.bfloat16
I32 = jnp.int32
BOTH = ("dp", "table")
LANES = 128
VMEM = pl.BlockSpec(memory_space=pltpu.VMEM)
SMEM = pl.BlockSpec(memory_space=pltpu.SMEM)
HBM = pl.BlockSpec(memory_space=pltpu.HBM)
MIB = 1 << 20


def dot_nn(a, b):
    return lax.dot_general(a, b, (((1,), (0,)), ((), ())), preferred_element_type=F32)


def dot_nt(a, b):
    return lax.dot_general(a, b, (((1,), (1,)), ((), ())), preferred_element_type=F32)


def dot_tn(a, b):
    return lax.dot_general(a, b, (((0,), (0,)), ((), ())), preferred_element_type=F32)


def dot_exact(a, b):
    return lax.dot_general(
        a, b, (((1,), (0,)), ((), ())), precision=lax.Precision.HIGHEST, preferred_element_type=F32
    )


def iota(shape, dim):
    return lax.broadcasted_iota(I32, shape, dim)


def shape_of(shape, dtype):
    return jax.ShapeDtypeStruct(shape, dtype)


def cost(flops, moved):
    return pl.CostEstimate(flops=int(flops), bytes_accessed=int(moved), transcendentals=0)


def params(mib):
    return pltpu.CompilerParams(vmem_limit_bytes=mib * MIB)


def call(body, outs, specs, flops, moved, scratch=(), room=16, out_specs=None, aliases=None):
    if out_specs is None:
        out_specs = tuple(VMEM for _ in outs) if isinstance(outs, tuple) else VMEM
    return pl.pallas_call(
        body,
        out_shape=outs,
        in_specs=specs,
        out_specs=out_specs,
        scratch_shapes=list(scratch),
        input_output_aliases=aliases or {},
        compiler_params=params(room),
        cost_estimate=cost(flops, moved),
    )


def start_all(sources, targets, sems):
    copies = [pltpu.make_async_copy(a, b, sems.at[n]) for n, (a, b) in enumerate(zip(sources, targets))]
    for copy in copies:
        copy.start()
    return copies


def request_kernel(piece, cap, *refs):
    sources, msg_ref, held, sems = refs[:5], refs[5], refs[6:11], refs[11]
    for copy in start_all(sources, held, sems):
        copy.wait()
    rows_ref, slot_ref, len_ref, dest_ref, counts_ref = held
    owners = rows_ref.shape[1]
    tokens = slot_ref.shape[1]
    replicas = tokens // piece
    my_dp = lax.axis_index("dp")
    lens = len_ref[...].astype(F32)
    takes = dest_ref[...] == iota((replicas, dest_ref.shape[1]), 0)
    totals = jnp.sum(jnp.where(takes, lens, 0.0), axis=1, keepdims=True)
    token = iota((replicas, tokens), 1)
    target = iota((replicas, tokens), 0)
    place = (my_dp * piece + token - target * piece).astype(F32)
    here = (token >= target * piece) & (token < (target + 1) * piece) & (place < totals)
    valid = jnp.sum(jnp.where(here, 1.0, 0.0), axis=0, keepdims=True)
    slot = slot_ref[...]
    by_owner = jnp.where(slot // cap == iota((owners, tokens), 0), valid, 0.0).astype(BF16)
    by_slot = jnp.where(slot % cap + cap == iota((LANES, tokens), 0), 1.0, 0.0).astype(BF16)
    counts = dot_nt(by_owner, by_slot)
    old = jnp.sum(counts_ref[...].astype(F32), axis=0, keepdims=True)
    total = jnp.sum(old, axis=1, keepdims=True) + jnp.sum(valid, axis=1, keepdims=True)
    lane = iota((owners, LANES), 1)
    place = jnp.where(iota((cap, LANES), 0) == iota((cap, LANES), 1), 1.0, 0.0)
    wanted = dot_exact(jnp.transpose(rows_ref[...].astype(F32)), place)
    msg_ref[...] = (jnp.where(lane == 2 * cap, total, counts) + wanted).astype(I32)


def asked_column(cap, asked_ref, first):
    askers = asked_ref.shape[0]
    total = askers * cap
    spread = jnp.where(iota((total, askers), 0) // cap == iota((total, askers), 1), 1.0, 0.0)
    each = dot_exact(spread, asked_ref[...].astype(F32))
    pick = iota((total, LANES), 1) == iota((total, LANES), 0) % cap + first
    return jnp.sum(jnp.where(pick, each, 0.0), axis=1, keepdims=True)


def serve_kernel(cap, asked_ref, table_ref, served_ref):
    rows = asked_column(cap, asked_ref, 0)
    total = rows.shape[0]
    step = min(512, table_ref.shape[0])
    lane = iota((total, step), 1).astype(F32)
    acc = None
    for base in range(0, table_ref.shape[0], step):
        pick = jnp.where(rows - float(base) == lane, 1.0, 0.0).astype(BF16)
        part = dot_nn(pick, table_ref[base : base + step, :])
        acc = part if acc is None else acc + part
    served_ref[...] = acc.astype(BF16)


def counts_kernel(cap, items, asked_ref, counts_ref, new_ref, log_ref, row_ref):
    rows = asked_column(cap, asked_ref, 0)
    added = asked_column(cap, asked_ref, cap)
    total = rows.shape[0]
    lines = counts_ref.shape[0]
    line = jnp.floor(rows * (1.0 / LANES))
    lane = rows - line * LANES
    by_line = jnp.where(line == iota((total, lines), 1).astype(F32), added, 0.0).astype(BF16)
    by_lane = jnp.where(lane == iota((total, LANES), 1).astype(F32), 1.0, 0.0).astype(BF16)
    new = counts_ref[...].astype(F32) + dot_tn(by_line, by_lane)
    whole = jnp.sum(asked_ref[:, 2 * cap : 2 * cap + 1].astype(F32), axis=0, keepdims=True)
    new_ref[...] = new.astype(I32)
    log_ref[...] = jnp.log(new + 1.0) - jnp.log(whole + float(items))
    row_ref[...] = jnp.transpose(jnp.broadcast_to(rows, (total, LANES)))[0:8, :]


def take_kernel(slot_ref, fetched_ref, home_ref):
    total = fetched_ref.shape[0]
    pick = jnp.where(slot_ref[...] == iota((total, slot_ref.shape[1]), 0), 1.0, 0.0).astype(BF16)
    home_ref[...] = dot_tn(pick, fetched_ref[...]).astype(BF16)


def slot_sum_kernel(slot_ref, back_ref, sums_ref):
    total = sums_ref.shape[0]
    pick = jnp.where(slot_ref[...] == iota((total, slot_ref.shape[1]), 0), 1.0, 0.0).astype(BF16)
    sums_ref[...] = dot_nn(pick, back_ref[...]).astype(BF16)


def scatter_kernel(row_ref, got_ref, out_ref, held_ref, sems):
    parts, block, _ = held_ref.shape
    total = got_ref.shape[0]
    line = iota((block, total), 0).astype(F32)
    copies = []
    for n in range(parts):
        pick = jnp.where(row_ref[0:1, :] - float(n * block) == line, 1.0, 0.0).astype(BF16)
        held_ref[n] = dot_nn(pick, got_ref[...])
        copies += start_all(
            (held_ref.at[n],), (out_ref.at[pl.ds(n * block, block), :],), sems.at[pl.ds(n, 1)]
        )
    for copy in copies:
        copy.wait()


def segments(len_ref, dest_ref, rows):
    nhist = len_ref.shape[1]
    mine = jnp.where(dest_ref[...] == lax.axis_index("dp"), len_ref[...], 0).astype(F32)
    later = iota((nhist, nhist), 0)
    other = iota((nhist, nhist), 1)
    ends = jnp.sum(jnp.where(other <= later, mine, 0.0), axis=1, keepdims=True)
    starts = jnp.sum(jnp.where(other < later, mine, 0.0), axis=1, keepdims=True)
    place = iota((nhist, rows), 1).astype(F32)
    label = iota((nhist, rows), 0).astype(F32) + 1.0
    return jnp.sum(jnp.where((starts <= place) & (place < ends), label, 0.0), axis=0, keepdims=True)


def valid_rows(seg, rows):
    return jnp.transpose(jnp.broadcast_to(jnp.where(seg > 0.0, 1.0, 0.0), (LANES, rows)))


def masked_grad(og_ref, valid):
    wide = og_ref.shape[1] // LANES
    return (og_ref[...].astype(F32) * jnp.concatenate([valid] * wide, axis=1)).astype(BF16)


def go_kernel(len_ref, dest_ref, og_ref, go_ref):
    rows = og_ref.shape[0]
    go_ref[...] = masked_grad(og_ref, valid_rows(segments(len_ref, dest_ref, rows), rows))


def pos_bounds(rows, count):
    return [max(1, rows // 2 ** (count - m)) for m in range(count)]


def time_bounds(count):
    return [float(4**m) for m in range(count)]


def time_gaps(time_ref, rows):
    stamp = jnp.broadcast_to(time_ref[...].astype(F32), (rows, rows))
    return jnp.transpose(stamp) - stamp


def steps_passed(value, bounds):
    total = jnp.where(value >= bounds[0], 1, 0)
    for bound in bounds[1:]:
        total = total + jnp.where(value >= bound, 1, 0)
    return total


def bias_index(seg, time_ref, rows, count):
    across = jnp.broadcast_to(seg, (rows, rows))
    down = jnp.transpose(across)
    dist = iota((rows, rows), 0) - iota((rows, rows), 1)
    near = steps_passed(dist, pos_bounds(rows, count))
    late = steps_passed(time_gaps(time_ref, rows), time_bounds(count))
    mask = (across == down) & (down > 0.0) & (dist >= 0)
    return jnp.where(mask, near * (count + 1) + late, LANES - 1)


def bias_table(pos_ref, timew_ref):
    heads, count = pos_ref.shape
    entry = iota((heads, LANES), 1)
    near = entry // (count + 1)
    late = entry - near * (count + 1)
    table = jnp.zeros((heads, LANES), F32)
    for m in range(count):
        table = table + jnp.where(near > m, pos_ref[:, m : m + 1], 0.0)
        table = table + jnp.where(late > m, timew_ref[:, m : m + 1], 0.0)
    return jnp.where(entry == LANES - 1, MASKED, table)


def look_up(table_row, index):
    rows, cols = index.shape
    spread = jnp.broadcast_to(table_row, (rows, LANES))
    return jnp.concatenate(
        [jnp.take_along_axis(spread, index[:, at : at + LANES], axis=1) for at in range(0, cols, LANES)], axis=1
    )


def norm_of(value):
    centered = value - jnp.mean(value, axis=1, keepdims=True)
    scale = lax.rsqrt(jnp.mean(centered * centered, axis=1, keepdims=True) + EPSILON)
    return centered * scale, scale


def norm_back(grad_hat, normed, scale):
    first = jnp.mean(grad_hat, axis=1, keepdims=True)
    second = jnp.mean(grad_hat * normed, axis=1, keepdims=True)
    return scale * (grad_hat - first - normed * second)


def sigmoid(value):
    return 1.0 / (1.0 + jnp.exp(-value))


def layer_kernel(
    staged,
    x_ref,
    w_ref,
    b_ref,
    g1_ref,
    g2_ref,
    wo_ref,
    bo_ref,
    len_ref,
    dest_ref,
    time_ref,
    og_ref,
    pos_ref,
    timew_ref,
    lo_ref,
    n1_ref,
    y_ref,
    dh_ref,
    ds_ref,
    g2g_ref,
    msg_ref,
    h_ref,
    slope_ref,
    a_ref,
):
    rows, width = x_ref.shape
    heads, count = pos_ref.shape
    pairs = heads // 2
    seg = segments(len_ref, dest_ref, rows)
    valid = valid_rows(seg, rows)
    dmix = dot_nt(masked_grad(og_ref, valid), wo_ref[...])
    index = bias_index(seg, time_ref, rows, count)
    table = bias_table(pos_ref, timew_ref)
    x = x_ref[...].astype(F32)
    xhat, _ = norm_of(x)
    n1 = (xhat * g1_ref[...]).astype(BF16)
    n1_ref[...] = n1
    acts = []
    for part in range(4):
        cols = slice(part * width, (part + 1) * width)
        h = dot_nn(n1, w_ref[:, cols]) + b_ref[:, cols]
        sig = sigmoid(h)
        acts.append(h * sig)
        h_ref[:, cols] = sig * (1.0 + h * (1.0 - sig))
    u = acts[0]
    v, q, k = (a.astype(BF16) for a in acts[1:])
    lane = iota((rows, LANES), 1)
    low = lane < LANES // 2
    zero = jnp.zeros((rows, LANES), BF16)

    def half(value, parity):
        return jnp.where(low if parity == 0 else ~low, value, zero)

    outs = []
    for pair in range(pairs):
        cols = slice(pair * LANES, (pair + 1) * LANES)
        total = None
        for parity in range(2):
            g = pair * 2 + parity
            s = dot_nt(half(q[:, cols], parity), k[:, cols]) * 0.125 + look_up(table[g : g + 1, :], index)
            sig = sigmoid(s)
            a = (s * sig).astype(BF16)
            a_ref[g] = a
            slope_ref[g] = sig * (1.0 + s * (1.0 - sig))
            part = dot_nn(a, half(v[:, cols], parity))
            total = part if total is None else total + part
        outs.append(total)
    o = jnp.concatenate(outs, axis=1)
    ohat, scale2 = norm_of(o)
    g2 = g2_ref[...]
    n2 = ohat * g2
    y = (n2 * u).astype(BF16)
    y_ref[...] = y
    branch = dot_nn(y, wo_ref[...]) + bo_ref[...]
    lo_ref[...] = (jnp.concatenate([valid] * (width // LANES), axis=1) * (x + branch)).astype(BF16)
    du = dmix * n2
    e2 = dmix * u
    g2g_ref[...] = jnp.sum(e2 * ohat, axis=0, keepdims=True)
    do = norm_back(e2 * g2, ohat, scale2).astype(BF16)
    dh_ref[:, 0:width] = (du * h_ref[:, 0:width]).astype(BF16)
    for pair in range(pairs):
        cols = slice(pair * LANES, (pair + 1) * LANES)
        dv, dq, dk = None, None, None
        for parity in range(2):
            g = pair * 2 + parity
            dom = half(do[:, cols], parity)
            da = dot_nt(dom, v[:, cols])
            ds = (da * slope_ref[g]).astype(BF16)
            ds_ref[g] = ds
            parts = (
                dot_tn(a_ref[g], dom),
                dot_nn(ds, half(k[:, cols], parity)),
                dot_tn(ds, half(q[:, cols], parity)),
            )
            if parity == 0:
                dv, dq, dk = parts
            else:
                dv, dq, dk = dv + parts[0], dq + parts[1], dk + parts[2]
        for part, value in ((1, dv), (2, dq * 0.125), (3, dk * 0.125)):
            at = slice(part * width + pair * LANES, part * width + (pair + 1) * LANES)
            dh_ref[:, at] = (value * h_ref[:, at]).astype(BF16)
    if staged:
        other = 1 - lax.axis_index("table")
        half_cols = 2 * width
        msg_ref[:, 0:half_cols] = dh_ref[:, pl.ds(pl.multiple_of(other * half_cols, half_cols), half_cols)]
        msg_ref[:, half_cols : half_cols + width] = n1
        half_y = width // 2
        msg_ref[:, half_cols + width :] = y_ref[:, pl.ds(pl.multiple_of(other * half_y, half_y), half_y)]
    else:
        msg_ref[...] = jnp.zeros_like(msg_ref)


def dx_kernel(dh_ref, w_ref, x_ref, g1_ref, go_ref, dx_ref, g1g_ref):
    xhat, scale = norm_of(x_ref[...].astype(F32))
    dn1 = dot_nt(dh_ref[...], w_ref[...])
    g1g_ref[...] = jnp.sum(dn1 * xhat, axis=0, keepdims=True)
    dx = norm_back(dn1 * g1_ref[...], xhat, scale) + go_ref[...].astype(F32)
    dx_ref[...] = dx.astype(BF16)


SMALL_ROWS = 48


def prefix_ends(time_ref, rows, count):
    time_lane = 64
    row = iota((1, rows), 1).astype(F32)
    ends = [row - float(bound) for bound in pos_bounds(rows, count)]
    ends += [jnp.full((time_lane - count, rows), -1.0, F32)]
    stamp = jnp.broadcast_to(time_ref[...].astype(F32), (rows, rows))
    gaps = stamp - jnp.transpose(stamp)
    for bound in time_bounds(count):
        ends.append(jnp.sum(jnp.where(gaps >= bound, 1.0, 0.0), axis=0, keepdims=True) - 1.0)
    ends += [jnp.full((LANES - time_lane - count, rows), -1.0, F32)]
    return jnp.transpose(jnp.concatenate(ends, axis=0)).astype(I32)


def small_kernel(count, ds_ref, time_ref, dh_ref, go_ref, g1g_ref, g2g_ref, out_ref):
    heads, rows, _ = ds_ref.shape
    width = go_ref.shape[1]
    out_ref[...] = jnp.zeros_like(out_ref)
    b_grad = jnp.sum(dh_ref[...].astype(F32), axis=0, keepdims=True)
    go_sum = jnp.sum(go_ref[...].astype(F32), axis=0, keepdims=True)
    at = 0
    for value in (b_grad, g1g_ref[...], g2g_ref[...], go_sum):
        for col in range(0, value.shape[1], LANES):
            out_ref[at : at + 1, :] = value[:, col : col + LANES]
            at += 1
    at = (at + 7) // 8 * 8
    ends = prefix_ends(time_ref, rows, count)
    upto = jnp.where(iota((rows, rows), 0) <= iota((rows, rows), 1), 1.0, 0.0).astype(BF16)
    sums = []
    for g in range(heads):
        prefix = dot_nn(ds_ref[g], upto)
        found = jnp.zeros((rows, LANES), F32)
        for first in range(0, rows, LANES):
            here = (ends >= first) & (ends < first + LANES)
            value = jnp.take_along_axis(
                prefix[:, first : first + LANES], jnp.where(here, ends - first, 0), axis=1
            )
            found = found + jnp.where(here, value, 0.0)
        sums.append(jnp.sum(found, axis=0, keepdims=True))
    sums = jnp.concatenate(sums, axis=0)
    out_ref[at : at + heads, :] = sums
    out_ref[at + heads : at + 2 * heads, 0 : LANES // 2] = sums[:, LANES // 2 :]


def place_of(columns):
    my_dp = lax.axis_index("dp")
    return lax.rem(my_dp, columns), lax.div(my_dp, columns)


def pack_kernel(planes, columns, dh_ref, n1_ref, y_ref, go_ref, got_ref, got_go_ref, small_ref, *rest):
    nears, fars, (uv_ref, wo_ref) = rest[:columns], rest[columns : 2 * columns], rest[2 * columns :]
    width = n1_ref.shape[1]
    core = lax.axis_index("table")
    my_xy, my_z = place_of(columns)
    half_cols = 2 * width
    half_y = width // 2
    dh = jnp.concatenate(
        [dh_ref[:, pl.ds(pl.multiple_of(core * half_cols, half_cols), half_cols)], got_ref[:, 0:half_cols]],
        axis=0,
    )
    n1 = jnp.concatenate([n1_ref[...], got_ref[:, half_cols : half_cols + width]], axis=0)
    y = jnp.concatenate(
        [y_ref[:, pl.ds(pl.multiple_of(core * half_y, half_y), half_y)], got_ref[:, half_cols + width :]],
        axis=0,
    )
    go = jnp.concatenate([go_ref[...], got_go_ref[...]], axis=0)
    uv_ref[...] = dot_tn(n1, dh)
    wo_ref[...] = dot_tn(y, go)
    short = half_y // (planes * columns)
    for rel_xy in range(columns):
        for rel_z in range(planes):
            chunk = jnp.bitwise_xor(my_xy, rel_xy) * planes + jnp.bitwise_xor(my_z, rel_z)
            out = (nears, fars)[rel_z // 2][rel_xy].at[rel_z % 2]
            for part in range(2):
                at = pl.multiple_of((2 * chunk + part) * short, short)
                out[:, part * half_cols : (part + 1) * half_cols] = uv_ref[pl.ds(at, short), :].astype(BF16)
            at = pl.multiple_of(chunk * short, short)
            out[:, 2 * half_cols : 2 * half_cols + width] = wo_ref[pl.ds(at, short), :].astype(BF16)
            out[:, 2 * half_cols + width :] = small_ref[pl.ds(at, short), :].astype(BF16)


def unpack(planes, columns, chunks, mine, theirs, uvqk_ref, wout_ref, small_ref, held_uvqk, held_wout, sems):
    short = held_wout.shape[1]
    width = held_wout.shape[2]
    core = lax.axis_index("table")
    my_xy, my_z = place_of(columns)
    half_cols = 2 * width
    half_y = width // 2
    wout_lanes = slice(2 * half_cols, 2 * half_cols + width)
    small_lanes = slice(2 * half_cols + width, 2 * half_cols + width + LANES)
    copies = []
    for rel_xy, rel_z, ref, at in chunks:
        chunk = jnp.bitwise_xor(my_xy, rel_xy) * planes + jnp.bitwise_xor(my_z, rel_z)
        pieces = mine[ref].at[at], theirs[ref].at[at]
        for piece, side in zip(pieces, (core, 1 - core)):
            n = len(copies) // 2
            for part in range(2):
                held_uvqk[n, part * short : (part + 1) * short, :] = piece[
                    :, part * half_cols : (part + 1) * half_cols
                ].astype(F32)
            held_wout[n] = piece[:, wout_lanes].astype(F32)
            tall = pl.ds(pl.multiple_of(chunk * 2 * short, 2 * short), 2 * short)
            cols = pl.ds(pl.multiple_of(side * half_cols, half_cols), half_cols)
            rows = pl.ds(pl.multiple_of(side * half_y + chunk * short, short), short)
            copies += start_all(
                (held_uvqk.at[n], held_wout.at[n]),
                (uvqk_ref.at[tall, cols], wout_ref.at[rows, :]),
                sems.at[pl.ds(2 * n, 2)],
            )
        small_ref[pl.ds(pl.multiple_of(chunk * short, short), short), :] = pieces[0][:, small_lanes].astype(
            F32
        ) + pieces[1][:, small_lanes].astype(F32)
    return copies


def first_chunks(planes, columns):
    near = [(xy, z, xy, z) for xy in range(columns) for z in range(2)]
    return near + [(0, z, columns, z - 2) for z in range(2, planes)]


def last_chunks(planes, columns):
    return [(xy, z, xy - 1, z - 2) for xy in range(1, columns) for z in range(2, planes)]


def unpack_first_kernel(planes, columns, *refs):
    mine, theirs = refs[: columns + 1], refs[columns + 1 : 2 * columns + 2]
    uvqk_ref, wout_ref, small_ref, held_uvqk, held_wout, sems = refs[2 * columns + 2 :]
    small_ref[...] = jnp.zeros_like(small_ref)
    chunks = first_chunks(planes, columns)
    for copy in unpack(
        planes, columns, chunks, mine, theirs, uvqk_ref, wout_ref, small_ref, held_uvqk, held_wout, sems
    ):
        copy.wait()


def unpack_last_kernel(planes, columns, *refs):
    peers = columns - 1
    mine, theirs, first_ref = refs[:peers], refs[peers : 2 * peers], refs[2 * peers + 2]
    uvqk_ref, wout_ref, b_ref, g1_ref, g2_ref, bo_ref, pos_ref, time_ref = refs[2 * peers + 3 : 2 * peers + 11]
    small_ref, held_uvqk, held_wout, sems = refs[2 * peers + 11 :]
    small_ref[...] = first_ref[...]
    chunks = last_chunks(planes, columns)
    copies = unpack(
        planes, columns, chunks, mine, theirs, uvqk_ref, wout_ref, small_ref, held_uvqk, held_wout, sems
    )
    at = 0
    for out in (b_ref, g1_ref, g2_ref, bo_ref):
        for col in range(0, out.shape[1], LANES):
            out[:, col : col + LANES] = small_ref[at : at + 1, :]
            at += 1
    at = (at + 7) // 8 * 8
    heads, count = pos_ref.shape
    pos_ref[...] = small_ref[at : at + heads, 0:count]
    time_ref[...] = small_ref[at + heads : at + 2 * heads, 0:count]
    for copy in copies:
        copy.wait()


def add_up(first, *rest):
    total = first.astype(F32)
    for other in rest:
        total = total + other.astype(F32)
    return total.astype(BF16)


def xor_step(value, size, step):
    return lax.ppermute(value, "dp", [(i, i ^ step) for i in range(size)])


def reduce_step(pieces, size, stride):
    return add_up(pieces[0], *(xor_step(pieces[k], size, k * stride) for k in range(1, len(pieces))))


def gather_step(own, size, stride, peers):
    return [own] + [xor_step(own, size, k * stride) for k in range(1, peers)]


def swap_cores(value):
    return lax.ppermute(value, "table", [(0, 1), (1, 0)])


def on_device(
    item_table,
    token_request_slot,
    request_rows,
    lengths,
    assignment,
    timestamps,
    item_counts,
    first_norm_gain,
    w_uvqk,
    b_uvqk,
    norm2_gain,
    w_out,
    b_out,
    pos_weight,
    time_weight,
    out_grad,
):
    rows = token_request_slot.shape[0]
    rows_dev, width = item_table.shape
    replicas = lax.axis_size("dp")
    groups = lax.axis_size("table")
    devices = replicas * groups
    cap = request_rows.shape[2]
    piece = rows // replicas
    heads, count = pos_weight.shape
    slots = devices * cap
    columns = 4
    planes = replicas // columns
    staged = (
        groups == 2
        and replicas == 16
        and width % (32 * replicas) == 0
        and (2 * heads + SMALL_ROWS - 16) <= width // 2
    )
    mb = MIB

    slot_row = token_request_slot.reshape(1, rows)
    time_row = timestamps.reshape(1, rows)
    counts_2d = item_counts.reshape(rows_dev // LANES, LANES)
    msg = call(
        functools.partial(request_kernel, piece, cap),
        shape_of((devices, LANES), I32),
        [HBM] * 5,
        mb,
        mb // 8,
        scratch=(
            pltpu.VMEM((cap, devices), I32),
            pltpu.VMEM((1, rows), I32),
            pltpu.VMEM(lengths.shape, I32),
            pltpu.VMEM(lengths.shape, I32),
            pltpu.VMEM(counts_2d.shape, I32),
            pltpu.SemaphoreType.DMA((5,)),
        ),
        room=64,
    )(request_rows.transpose(0, 2, 1).reshape(cap, devices), slot_row, lengths, assignment, counts_2d)
    asked = lax.all_to_all(msg.reshape(devices, 1, LANES), BOTH, 0, 0, tiled=True).reshape(devices, LANES)
    served = call(
        functools.partial(serve_kernel, cap), shape_of((slots, width), BF16), [VMEM] * 2, 1 << 30, 5 * mb
    )(asked, item_table)
    go = call(go_kernel, shape_of((rows, width), BF16), [VMEM] * 3, 64 * mb, mb)(lengths, assignment, out_grad)
    fetched = lax.all_to_all(served.reshape(devices, cap, width), BOTH, 0, 0, tiled=True)
    new_counts, log_q, asked_row = call(
        functools.partial(counts_kernel, cap, rows_dev * devices),
        (
            shape_of((rows_dev // LANES, LANES), I32),
            shape_of((rows_dev // LANES, LANES), F32),
            shape_of((8, slots), F32),
        ),
        [VMEM] * 2,
        64 * mb,
        mb,
    )(asked, counts_2d)
    home = call(take_kernel, shape_of((rows, width), BF16), [VMEM] * 2, 64 * mb, mb)(
        slot_row, fetched.reshape(slots, width)
    )
    if staged:
        got_go = swap_cores(go)
    x = lax.all_to_all(home.reshape(replicas, piece, width), "dp", 0, 0, tiled=True).reshape(rows, width)
    if staged:
        x, got_go = lax.optimization_barrier((x, got_go))

    half_cols = 2 * width
    g1, g2 = first_norm_gain.reshape(1, width), norm2_gain.reshape(1, width)
    msg_cols = half_cols + width + width // 2 if staged else LANES
    layer_out, n1, y, dh, ds, g2_grad, to_core = call(
        functools.partial(layer_kernel, staged),
        (
            shape_of((rows, width), BF16),
            shape_of((rows, width), BF16),
            shape_of((rows, width), BF16),
            shape_of((rows, 4 * width), BF16),
            shape_of((heads, rows, rows), BF16),
            shape_of((1, width), F32),
            shape_of((rows, msg_cols), BF16),
        ),
        [VMEM] * 13,
        2 << 30,
        8 * mb,
        scratch=(
            pltpu.VMEM((rows, 4 * width), F32),
            pltpu.VMEM((heads, rows, rows), F32),
            pltpu.VMEM((heads, rows, rows), BF16),
        ),
        room=24,
    )(
        x,
        w_uvqk,
        b_uvqk.reshape(1, 4 * width),
        g1,
        g2,
        w_out,
        b_out.reshape(1, width),
        lengths,
        assignment,
        time_row,
        out_grad,
        pos_weight,
        time_weight,
    )
    def home_again(dx):
        return lax.all_to_all(dx.reshape(replicas, piece, width), "dp", 0, 0, tiled=True).reshape(rows, width)

    def to_owners(back):
        return send_sums(slot_sums(back))

    def slot_sums(back):
        return call(slot_sum_kernel, shape_of((slots, width), BF16), [VMEM] * 2, 64 * mb, mb)(slot_row, back)
    def send_sums(sums):
        sums = lax.all_to_all(sums.reshape(devices, cap, width), BOTH, 0, 0, tiled=True)
        return sums.reshape(slots, width)

    def into_table(got_sums):
        block = min(512, rows_dev)
        return call(
            scatter_kernel,
            shape_of((rows_dev, width), F32),
            [VMEM] * 2,
            1 << 30,
            8 * mb,
            scratch=(
                pltpu.VMEM((rows_dev // block, block, width), F32),
                pltpu.SemaphoreType.DMA((rows_dev // block,)),
            ),
            room=24,
            out_specs=HBM,
        )(asked_row, got_sums)

    if staged:
        got = swap_cores(to_core)
    dx, g1_grad = call(
        dx_kernel, (shape_of((rows, width), BF16), shape_of((1, width), F32)), [VMEM] * 5, 1 << 29, 4 * mb
    )(dh, w_uvqk, x, g1, go)
    small = call(
        functools.partial(small_kernel, count),
        shape_of((width // 2, LANES), F32),
        [VMEM] * 6,
        1 << 28,
        2 * mb,
    )(ds, time_row, dh, go, g1_grad, g2_grad)
    if staged:
        short = width // replicas // 2
        pieces = call(
            functools.partial(pack_kernel, planes, columns),
            tuple(shape_of((2, short, 5 * width + LANES), BF16) for _ in range(2 * columns)),
            [VMEM] * 7,
            1 << 30,
            6 * mb,
            scratch=(pltpu.VMEM((width, half_cols), F32), pltpu.VMEM((width // 2, width), F32)),
        )(dh, n1, y, go, got, got_go, small)
        dx, *pieces = lax.optimization_barrier((dx, *pieces))
        nears, fars = pieces[:columns], pieces[columns:]
        back = home_again(dx)
        got_far = [xor_step(fars[k], replicas, k) for k in range(1, columns)]
        nears, got_far[0] = lax.optimization_barrier((nears, got_far[0]))
        far_line = add_up(fars[0], *got_far)
        got_line = [xor_step(far_line[k - 2], replicas, k * columns) for k in range(2, planes)]
        near_line = reduce_step(nears, replicas, 1)
        near_line, back = lax.optimization_barrier((near_line, back))
        got_next = xor_step(near_line[1], replicas, columns)
        sums = slot_sums(back)
        own = add_up(near_line[0], got_next, *got_line)
        own, sums = lax.optimization_barrier((own, sums))
        next_own = xor_step(own, replicas, columns)
        far = [xor_step(own, replicas, k * columns) for k in range(2, planes)]
        near = jnp.stack([own, next_own])
        nears = gather_step(near, replicas, 1, columns)
        nears[1], sums = lax.optimization_barrier((nears[1], sums))
        got_sums = send_sums(sums)
        far = jnp.stack(far)
        far, nears = lax.optimization_barrier((far, nears))
        table_grad = into_table(got_sums)
        fars = gather_step(far, replicas, 1, columns)
        their_nears = [swap_cores(piece) for piece in nears]
        their_far = swap_cores(far)
        small_shape = shape_of((width // 2, LANES), F32)
        wide_shapes = (shape_of((width, 4 * width), F32), shape_of((width, width), F32))

        def unpack_scratch(chunks):
            n = 2 * len(chunks)
            return (
                pltpu.VMEM((n, 2 * short, half_cols), F32),
                pltpu.VMEM((n, short, width), F32),
                pltpu.SemaphoreType.DMA((2 * n,)),
            )

        w_uvqk_sum, w_out_sum, small_sum = call(
            functools.partial(unpack_first_kernel, planes, columns),
            wide_shapes + (small_shape,),
            [VMEM] * (2 * columns + 2),
            mb,
            5 * mb,
            scratch=unpack_scratch(first_chunks(planes, columns)),
            out_specs=(HBM, HBM, VMEM),
        )(*nears, far, *their_nears, their_far)
        fars, small_sum, table_grad = lax.optimization_barrier((fars, small_sum, table_grad))
        their_fars = [swap_cores(piece) for piece in fars[1:]]
        w_uvqk_sum, w_out_sum, b_sum, g1_sum, g2_sum, bo_sum, pos_sum, time_sum = call(
            functools.partial(unpack_last_kernel, planes, columns),
            wide_shapes
            + (
                shape_of((1, 4 * width), F32),
                shape_of((1, width), F32),
                shape_of((1, width), F32),
                shape_of((1, width), F32),
                shape_of((heads, count), F32),
                shape_of((heads, count), F32),
            ),
            [VMEM] * (2 * columns - 2) + [HBM, HBM, VMEM],
            mb,
            3 * mb,
            scratch=(pltpu.VMEM(small_shape.shape, F32),) + unpack_scratch(last_chunks(planes, columns)),
            out_specs=(HBM, HBM) + (VMEM,) * 6,
            aliases={2 * columns - 2: 0, 2 * columns - 1: 1},
        )(*fars[1:], *their_fars, w_uvqk_sum, w_out_sum, small_sum)
    else:
        table_grad = into_table(to_owners(home_again(dx)))
        w_uvqk_sum, w_out_sum, parts = lax.psum((dot_tn(n1, dh), dot_tn(y, go), small[0:SMALL_ROWS]), BOTH)
        at = 4 * width // LANES
        step = width // LANES
        b_sum = parts[0:at]
        g1_sum, g2_sum, bo_sum = (parts[at + n * step : at + (n + 1) * step] for n in range(3))
        at = (at + 3 * step + 7) // 8 * 8
        pos_sum = parts[at : at + heads, 0:count]
        time_sum = parts[at + heads : at + 2 * heads, 0:count]
    return (
        layer_out,
        table_grad,
        g1_sum.reshape(width),
        w_uvqk_sum,
        b_sum.reshape(4 * width),
        g2_sum.reshape(width),
        w_out_sum,
        bo_sum.reshape(width),
        pos_sum,
        time_sum,
        new_counts.reshape(rows_dev),
        log_q.reshape(rows_dev),
    )


def solution(mesh):
    split = P(("dp", "table"))
    rows_split = P(("dp", "table"), None)
    placed = (
        rows_split,
        split,
        P(("dp", "table"), None, None),
        P("table", None),
        P("table", None),
        split,
        split,
        P(),
        P(),
        P(),
        P(),
        P(),
        P(),
        P(),
        P(),
        rows_split,
    )
    return jax.shard_map(
        on_device,
        mesh=mesh,
        in_specs=placed,
        out_specs=(rows_split, rows_split, P(), P(), P(), P(), P(), P(), P(), P(), split, split),
        check_vma=False,
    )
```

```python
import functools

import jax
import jax.numpy as jnp
from jax import lax
from jax.experimental import pallas as pl
from jax.experimental.pallas import tpu as pltpu
from jax.sharding import PartitionSpec as P

EPSILON = 1e-05
MASKED = -1e30
F32 = jnp.float32
BF16 = jnp.bfloat16
I32 = jnp.int32
BOTH = ("dp", "table")
LANES = 128
VMEM = pl.BlockSpec(memory_space=pltpu.VMEM)
SMEM = pl.BlockSpec(memory_space=pltpu.SMEM)
HBM = pl.BlockSpec(memory_space=pltpu.HBM)
MIB = 1 << 20


def dot_nn(a, b):
    return lax.dot_general(a, b, (((1,), (0,)), ((), ())), preferred_element_type=F32)


def dot_nt(a, b):
    return lax.dot_general(a, b, (((1,), (1,)), ((), ())), preferred_element_type=F32)


def dot_tn(a, b):
    return lax.dot_general(a, b, (((0,), (0,)), ((), ())), preferred_element_type=F32)


def dot_exact(a, b):
    return lax.dot_general(
        a, b, (((1,), (0,)), ((), ())), precision=lax.Precision.HIGHEST, preferred_element_type=F32
    )


def iota(shape, dim):
    return lax.broadcasted_iota(I32, shape, dim)


def shape_of(shape, dtype):
    return jax.ShapeDtypeStruct(shape, dtype)


def cost(flops, moved):
    return pl.CostEstimate(flops=int(flops), bytes_accessed=int(moved), transcendentals=0)


def params(mib):
    return pltpu.CompilerParams(vmem_limit_bytes=mib * MIB)


def call(body, outs, specs, flops, moved, scratch=(), room=16, out_specs=None, aliases=None):
    if out_specs is None:
        out_specs = tuple(VMEM for _ in outs) if isinstance(outs, tuple) else VMEM
    return pl.pallas_call(
        body,
        out_shape=outs,
        in_specs=specs,
        out_specs=out_specs,
        scratch_shapes=list(scratch),
        input_output_aliases=aliases or {},
        compiler_params=params(room),
        cost_estimate=cost(flops, moved),
    )


def start_all(sources, targets, sems):
    copies = [pltpu.make_async_copy(a, b, sems.at[n]) for n, (a, b) in enumerate(zip(sources, targets))]
    for copy in copies:
        copy.start()
    return copies


def request_kernel(piece, cap, *refs):
    sources, msg_ref, held, sems = refs[:5], refs[5], refs[6:11], refs[11]
    for copy in start_all(sources, held, sems):
        copy.wait()
    rows_ref, slot_ref, len_ref, dest_ref, counts_ref = held
    owners = rows_ref.shape[1]
    tokens = slot_ref.shape[1]
    replicas = tokens // piece
    my_dp = lax.axis_index("dp")
    lens = len_ref[...].astype(F32)
    takes = dest_ref[...] == iota((replicas, dest_ref.shape[1]), 0)
    totals = jnp.sum(jnp.where(takes, lens, 0.0), axis=1, keepdims=True)
    token = iota((replicas, tokens), 1)
    target = iota((replicas, tokens), 0)
    place = (my_dp * piece + token - target * piece).astype(F32)
    here = (token >= target * piece) & (token < (target + 1) * piece) & (place < totals)
    valid = jnp.sum(jnp.where(here, 1.0, 0.0), axis=0, keepdims=True)
    slot = slot_ref[...]
    by_owner = jnp.where(slot // cap == iota((owners, tokens), 0), valid, 0.0).astype(BF16)
    by_slot = jnp.where(slot % cap + cap == iota((LANES, tokens), 0), 1.0, 0.0).astype(BF16)
    counts = dot_nt(by_owner, by_slot)
    old = jnp.sum(counts_ref[...].astype(F32), axis=0, keepdims=True)
    total = jnp.sum(old, axis=1, keepdims=True) + jnp.sum(valid, axis=1, keepdims=True)
    lane = iota((owners, LANES), 1)
    place = jnp.where(iota((cap, LANES), 0) == iota((cap, LANES), 1), 1.0, 0.0)
    wanted = dot_exact(jnp.transpose(rows_ref[...].astype(F32)), place)
    msg_ref[...] = (jnp.where(lane == 2 * cap, total, counts) + wanted).astype(I32)


def asked_column(cap, asked_ref, first):
    askers = asked_ref.shape[0]
    total = askers * cap
    spread = jnp.where(iota((total, askers), 0) // cap == iota((total, askers), 1), 1.0, 0.0)
    each = dot_exact(spread, asked_ref[...].astype(F32))
    pick = iota((total, LANES), 1) == iota((total, LANES), 0) % cap + first
    return jnp.sum(jnp.where(pick, each, 0.0), axis=1, keepdims=True)


def serve_kernel(cap, asked_ref, table_ref, served_ref):
    rows = asked_column(cap, asked_ref, 0)
    total = rows.shape[0]
    step = min(512, table_ref.shape[0])
    lane = iota((total, step), 1).astype(F32)
    acc = None
    for base in range(0, table_ref.shape[0], step):
        pick = jnp.where(rows - float(base) == lane, 1.0, 0.0).astype(BF16)
        part = dot_nn(pick, table_ref[base : base + step, :])
        acc = part if acc is None else acc + part
    served_ref[...] = acc.astype(BF16)


def counts_kernel(cap, items, asked_ref, counts_ref, new_ref, log_ref, row_ref):
    rows = asked_column(cap, asked_ref, 0)
    added = asked_column(cap, asked_ref, cap)
    total = rows.shape[0]
    lines = counts_ref.shape[0]
    line = jnp.floor(rows * (1.0 / LANES))
    lane = rows - line * LANES
    by_line = jnp.where(line == iota((total, lines), 1).astype(F32), added, 0.0).astype(BF16)
    by_lane = jnp.where(lane == iota((total, LANES), 1).astype(F32), 1.0, 0.0).astype(BF16)
    new = counts_ref[...].astype(F32) + dot_tn(by_line, by_lane)
    whole = jnp.sum(asked_ref[:, 2 * cap : 2 * cap + 1].astype(F32), axis=0, keepdims=True)
    new_ref[...] = new.astype(I32)
    log_ref[...] = jnp.log(new + 1.0) - jnp.log(whole + float(items))
    row_ref[...] = jnp.transpose(jnp.broadcast_to(rows, (total, LANES)))[0:8, :]


def take_kernel(slot_ref, fetched_ref, home_ref):
    total = fetched_ref.shape[0]
    pick = jnp.where(slot_ref[...] == iota((total, slot_ref.shape[1]), 0), 1.0, 0.0).astype(BF16)
    home_ref[...] = dot_tn(pick, fetched_ref[...]).astype(BF16)


def slot_sum_kernel(slot_ref, back_ref, sums_ref):
    total = sums_ref.shape[0]
    pick = jnp.where(slot_ref[...] == iota((total, slot_ref.shape[1]), 0), 1.0, 0.0).astype(BF16)
    sums_ref[...] = dot_nn(pick, back_ref[...]).astype(BF16)


def scatter_kernel(row_ref, got_ref, out_ref, held_ref, sems):
    parts, block, _ = held_ref.shape
    total = got_ref.shape[0]
    line = iota((block, total), 0).astype(F32)
    copies = []
    for n in range(parts):
        pick = jnp.where(row_ref[0:1, :] - float(n * block) == line, 1.0, 0.0).astype(BF16)
        held_ref[n] = dot_nn(pick, got_ref[...])
        copies += start_all(
            (held_ref.at[n],), (out_ref.at[pl.ds(n * block, block), :],), sems.at[pl.ds(n, 1)]
        )
    for copy in copies:
        copy.wait()


def segments(len_ref, dest_ref, rows):
    nhist = len_ref.shape[1]
    mine = jnp.where(dest_ref[...] == lax.axis_index("dp"), len_ref[...], 0).astype(F32)
    later = iota((nhist, nhist), 0)
    other = iota((nhist, nhist), 1)
    ends = jnp.sum(jnp.where(other <= later, mine, 0.0), axis=1, keepdims=True)
    starts = jnp.sum(jnp.where(other < later, mine, 0.0), axis=1, keepdims=True)
    place = iota((nhist, rows), 1).astype(F32)
    label = iota((nhist, rows), 0).astype(F32) + 1.0
    return jnp.sum(jnp.where((starts <= place) & (place < ends), label, 0.0), axis=0, keepdims=True)


def valid_rows(seg, rows):
    return jnp.transpose(jnp.broadcast_to(jnp.where(seg > 0.0, 1.0, 0.0), (LANES, rows)))


def masked_grad(og_ref, valid):
    wide = og_ref.shape[1] // LANES
    return (og_ref[...].astype(F32) * jnp.concatenate([valid] * wide, axis=1)).astype(BF16)


def go_kernel(len_ref, dest_ref, og_ref, go_ref):
    rows = og_ref.shape[0]
    go_ref[...] = masked_grad(og_ref, valid_rows(segments(len_ref, dest_ref, rows), rows))


def pos_bounds(rows, count):
    return [max(1, rows // 2 ** (count - m)) for m in range(count)]


def time_bounds(count):
    return [float(4**m) for m in range(count)]


def time_gaps(time_ref, rows):
    stamp = jnp.broadcast_to(time_ref[...].astype(F32), (rows, rows))
    return jnp.transpose(stamp) - stamp


def steps_passed(value, bounds):
    total = jnp.where(value >= bounds[0], 1, 0)
    for bound in bounds[1:]:
        total = total + jnp.where(value >= bound, 1, 0)
    return total


def bias_index(seg, time_ref, rows, count):
    across = jnp.broadcast_to(seg, (rows, rows))
    down = jnp.transpose(across)
    dist = iota((rows, rows), 0) - iota((rows, rows), 1)
    near = steps_passed(dist, pos_bounds(rows, count))
    late = steps_passed(time_gaps(time_ref, rows), time_bounds(count))
    mask = (across == down) & (down > 0.0) & (dist >= 0)
    return jnp.where(mask, near * (count + 1) + late, LANES - 1)


def bias_table(pos_ref, timew_ref):
    heads, count = pos_ref.shape
    entry = iota((heads, LANES), 1)
    near = entry // (count + 1)
    late = entry - near * (count + 1)
    table = jnp.zeros((heads, LANES), F32)
    for m in range(count):
        table = table + jnp.where(near > m, pos_ref[:, m : m + 1], 0.0)
        table = table + jnp.where(late > m, timew_ref[:, m : m + 1], 0.0)
    return jnp.where(entry == LANES - 1, MASKED, table)


def look_up(table_row, index):
    rows, cols = index.shape
    spread = jnp.broadcast_to(table_row, (rows, LANES))
    return jnp.concatenate(
        [jnp.take_along_axis(spread, index[:, at : at + LANES], axis=1) for at in range(0, cols, LANES)], axis=1
    )


def norm_of(value):
    centered = value - jnp.mean(value, axis=1, keepdims=True)
    scale = lax.rsqrt(jnp.mean(centered * centered, axis=1, keepdims=True) + EPSILON)
    return centered * scale, scale


def norm_back(grad_hat, normed, scale):
    first = jnp.mean(grad_hat, axis=1, keepdims=True)
    second = jnp.mean(grad_hat * normed, axis=1, keepdims=True)
    return scale * (grad_hat - first - normed * second)


def sigmoid(value):
    return 0.5 * jnp.tanh(0.5 * value) + 0.5


def layer_kernel(
    staged,
    x_ref,
    w_ref,
    b_ref,
    g1_ref,
    g2_ref,
    wo_ref,
    bo_ref,
    len_ref,
    dest_ref,
    time_ref,
    og_ref,
    pos_ref,
    timew_ref,
    lo_ref,
    n1_ref,
    y_ref,
    dh_ref,
    ds_ref,
    g2g_ref,
    msg_ref,
    h_ref,
    slope_ref,
    a_ref,
):
    rows, width = x_ref.shape
    heads, count = pos_ref.shape
    pairs = heads // 2
    seg = segments(len_ref, dest_ref, rows)
    valid = valid_rows(seg, rows)
    dmix = dot_nt(masked_grad(og_ref, valid), wo_ref[...])
    index = bias_index(seg, time_ref, rows, count)
    table = bias_table(pos_ref, timew_ref)
    x = x_ref[...].astype(F32)
    xhat, _ = norm_of(x)
    n1 = (xhat * g1_ref[...]).astype(BF16)
    n1_ref[...] = n1
    acts = []
    for part in range(4):
        cols = slice(part * width, (part + 1) * width)
        h = dot_nn(n1, w_ref[:, cols]) + b_ref[:, cols]
        sig = sigmoid(h)
        acts.append(h * sig)
        h_ref[:, cols] = sig * (1.0 + h * (1.0 - sig))
    u = acts[0]
    v, q, k = (a.astype(BF16) for a in acts[1:])
    lane = iota((rows, LANES), 1)
    low = lane < LANES // 2
    zero = jnp.zeros((rows, LANES), BF16)

    def half(value, parity):
        return jnp.where(low if parity == 0 else ~low, value, zero)

    outs = []
    for pair in range(pairs):
        cols = slice(pair * LANES, (pair + 1) * LANES)
        total = None
        for parity in range(2):
            g = pair * 2 + parity
            s = dot_nt(half(q[:, cols], parity), k[:, cols]) * 0.125 + look_up(table[g : g + 1, :], index)
            sig = sigmoid(s)
            a = (s * sig).astype(BF16)
            a_ref[g] = a
            slope_ref[g] = sig * (1.0 + s * (1.0 - sig))
            part = dot_nn(a, half(v[:, cols], parity))
            total = part if total is None else total + part
        outs.append(total)
    o = jnp.concatenate(outs, axis=1)
    ohat, scale2 = norm_of(o)
    g2 = g2_ref[...]
    n2 = ohat * g2
    y = (n2 * u).astype(BF16)
    y_ref[...] = y
    branch = dot_nn(y, wo_ref[...]) + bo_ref[...]
    lo_ref[...] = (jnp.concatenate([valid] * (width // LANES), axis=1) * (x + branch)).astype(BF16)
    du = dmix * n2
    e2 = dmix * u
    g2g_ref[...] = jnp.sum(e2 * ohat, axis=0, keepdims=True)
    do = norm_back(e2 * g2, ohat, scale2).astype(BF16)
    dh_ref[:, 0:width] = (du * h_ref[:, 0:width]).astype(BF16)
    for pair in range(pairs):
        cols = slice(pair * LANES, (pair + 1) * LANES)
        dv, dq, dk = None, None, None
        for parity in range(2):
            g = pair * 2 + parity
            dom = half(do[:, cols], parity)
            da = dot_nt(dom, v[:, cols])
            ds = (da * slope_ref[g]).astype(BF16)
            ds_ref[g] = ds
            parts = (
                dot_tn(a_ref[g], dom),
                dot_nn(ds, half(k[:, cols], parity)),
                dot_tn(ds, half(q[:, cols], parity)),
            )
            if parity == 0:
                dv, dq, dk = parts
            else:
                dv, dq, dk = dv + parts[0], dq + parts[1], dk + parts[2]
        for part, value in ((1, dv), (2, dq * 0.125), (3, dk * 0.125)):
            at = slice(part * width + pair * LANES, part * width + (pair + 1) * LANES)
            dh_ref[:, at] = (value * h_ref[:, at]).astype(BF16)
    if staged:
        other = 1 - lax.axis_index("table")
        half_cols = 2 * width
        msg_ref[:, 0:half_cols] = dh_ref[:, pl.ds(pl.multiple_of(other * half_cols, half_cols), half_cols)]
        msg_ref[:, half_cols : half_cols + width] = n1
        half_y = width // 2
        msg_ref[:, half_cols + width :] = y_ref[:, pl.ds(pl.multiple_of(other * half_y, half_y), half_y)]
    else:
        msg_ref[...] = jnp.zeros_like(msg_ref)


def dx_kernel(dh_ref, w_ref, x_ref, g1_ref, go_ref, dx_ref, g1g_ref):
    xhat, scale = norm_of(x_ref[...].astype(F32))
    dn1 = dot_nt(dh_ref[...], w_ref[...])
    g1g_ref[...] = jnp.sum(dn1 * xhat, axis=0, keepdims=True)
    dx = norm_back(dn1 * g1_ref[...], xhat, scale) + go_ref[...].astype(F32)
    dx_ref[...] = dx.astype(BF16)


SMALL_ROWS = 48


def prefix_ends(time_ref, rows, count):
    time_lane = 64
    row = iota((1, rows), 1).astype(F32)
    ends = [row - float(bound) for bound in pos_bounds(rows, count)]
    ends += [jnp.full((time_lane - count, rows), -1.0, F32)]
    stamp = jnp.broadcast_to(time_ref[...].astype(F32), (rows, rows))
    gaps = stamp - jnp.transpose(stamp)
    for bound in time_bounds(count):
        ends.append(jnp.sum(jnp.where(gaps >= bound, 1.0, 0.0), axis=0, keepdims=True) - 1.0)
    ends += [jnp.full((LANES - time_lane - count, rows), -1.0, F32)]
    return jnp.transpose(jnp.concatenate(ends, axis=0)).astype(I32)


def small_kernel(count, ds_ref, time_ref, dh_ref, go_ref, g1g_ref, g2g_ref, out_ref):
    heads, rows, _ = ds_ref.shape
    width = go_ref.shape[1]
    out_ref[...] = jnp.zeros_like(out_ref)
    b_grad = jnp.sum(dh_ref[...].astype(F32), axis=0, keepdims=True)
    go_sum = jnp.sum(go_ref[...].astype(F32), axis=0, keepdims=True)
    at = 0
    for value in (b_grad, g1g_ref[...], g2g_ref[...], go_sum):
        for col in range(0, value.shape[1], LANES):
            out_ref[at : at + 1, :] = value[:, col : col + LANES]
            at += 1
    at = (at + 7) // 8 * 8
    ends = prefix_ends(time_ref, rows, count)
    upto = jnp.where(iota((rows, rows), 0) <= iota((rows, rows), 1), 1.0, 0.0).astype(BF16)
    sums = []
    for g in range(heads):
        prefix = dot_nn(ds_ref[g], upto)
        found = jnp.zeros((rows, LANES), F32)
        for first in range(0, rows, LANES):
            here = (ends >= first) & (ends < first + LANES)
            value = jnp.take_along_axis(
                prefix[:, first : first + LANES], jnp.where(here, ends - first, 0), axis=1
            )
            found = found + jnp.where(here, value, 0.0)
        sums.append(jnp.sum(found, axis=0, keepdims=True))
    sums = jnp.concatenate(sums, axis=0)
    out_ref[at : at + heads, :] = sums
    out_ref[at + heads : at + 2 * heads, 0 : LANES // 2] = sums[:, LANES // 2 :]


def place_of(columns):
    my_dp = lax.axis_index("dp")
    return lax.rem(my_dp, columns), lax.div(my_dp, columns)


def pack_kernel(planes, columns, dh_ref, n1_ref, y_ref, go_ref, got_ref, got_go_ref, small_ref, *rest):
    nears, fars, (uv_ref, wo_ref) = rest[:columns], rest[columns : 2 * columns], rest[2 * columns :]
    width = n1_ref.shape[1]
    core = lax.axis_index("table")
    my_xy, my_z = place_of(columns)
    half_cols = 2 * width
    half_y = width // 2
    dh = jnp.concatenate(
        [dh_ref[:, pl.ds(pl.multiple_of(core * half_cols, half_cols), half_cols)], got_ref[:, 0:half_cols]],
        axis=0,
    )
    n1 = jnp.concatenate([n1_ref[...], got_ref[:, half_cols : half_cols + width]], axis=0)
    y = jnp.concatenate(
        [y_ref[:, pl.ds(pl.multiple_of(core * half_y, half_y), half_y)], got_ref[:, half_cols + width :]],
        axis=0,
    )
    go = jnp.concatenate([go_ref[...], got_go_ref[...]], axis=0)
    uv_ref[...] = dot_tn(n1, dh)
    wo_ref[...] = dot_tn(y, go)
    short = half_y // (planes * columns)
    for rel_xy in range(columns):
        for rel_z in range(planes):
            chunk = jnp.bitwise_xor(my_xy, rel_xy) * planes + jnp.bitwise_xor(my_z, rel_z)
            out = (nears, fars)[rel_z // 2][rel_xy].at[rel_z % 2]
            for part in range(2):
                at = pl.multiple_of((2 * chunk + part) * short, short)
                out[:, part * half_cols : (part + 1) * half_cols] = uv_ref[pl.ds(at, short), :].astype(BF16)
            at = pl.multiple_of(chunk * short, short)
            out[:, 2 * half_cols : 2 * half_cols + width] = wo_ref[pl.ds(at, short), :].astype(BF16)
            out[:, 2 * half_cols + width :] = small_ref[pl.ds(at, short), :].astype(BF16)


def unpack(planes, columns, chunks, uvqk_ref, wout_ref, small_ref, held_uvqk, held_wout, sems):
    short = held_wout.shape[1]
    width = held_wout.shape[2]
    core = lax.axis_index("table")
    my_xy, my_z = place_of(columns)
    half_cols = 2 * width
    half_y = width // 2
    wout_lanes = slice(2 * half_cols, 2 * half_cols + width)
    small_lanes = slice(2 * half_cols + width, 2 * half_cols + width + LANES)
    copies = []
    for n, (rel_xy, rel_z, whose, piece) in enumerate(chunks):
        chunk = jnp.bitwise_xor(my_xy, rel_xy) * planes + jnp.bitwise_xor(my_z, rel_z)
        side = jnp.bitwise_xor(core, whose)
        for part in range(2):
            held_uvqk[n, part * short : (part + 1) * short, :] = piece[
                :, part * half_cols : (part + 1) * half_cols
            ].astype(F32)
        held_wout[n] = piece[:, wout_lanes].astype(F32)
        tall = pl.ds(pl.multiple_of(chunk * 2 * short, 2 * short), 2 * short)
        cols = pl.ds(pl.multiple_of(side * half_cols, half_cols), half_cols)
        rows = pl.ds(pl.multiple_of(side * half_y + chunk * short, short), short)
        copies += start_all(
            (held_uvqk.at[n], held_wout.at[n]),
            (uvqk_ref.at[tall, cols], wout_ref.at[rows, :]),
            sems.at[pl.ds(2 * n, 2)],
        )
        small_ref[pl.ds(pl.multiple_of(chunk * short, short), short), :] += piece[:, small_lanes].astype(F32)
    return copies


def chunks_of(planes, first_z, pieces, whose, first_xy=0):
    return [
        (first_xy + xy, first_z + z, whose, piece.at[z])
        for xy, piece in enumerate(pieces)
        for z in range(min(2, planes - first_z))
    ]


def unpack_first_kernel(planes, columns, *refs):
    mine, theirs = refs[: columns + 1], refs[columns + 1 : 2 * columns + 2]
    uvqk_ref, wout_ref, small_ref, *scratch = refs[2 * columns + 2 :]
    small_ref[...] = jnp.zeros_like(small_ref)
    chunks = []
    for whose, pieces in enumerate((mine, theirs)):
        chunks += chunks_of(planes, 0, pieces[:columns], whose) + chunks_of(planes, 2, pieces[columns:], whose)
    for copy in unpack(planes, columns, chunks, uvqk_ref, wout_ref, small_ref, *scratch):
        copy.wait()


def unpack_next_kernel(planes, columns, *refs):
    peers = columns - 1
    mine, before_ref = refs[:peers], refs[peers + 2]
    uvqk_ref, wout_ref, small_ref, *scratch = refs[peers + 3 :]
    small_ref[...] = before_ref[...]
    chunks = chunks_of(planes, 2, mine, 0, 1)
    for copy in unpack(planes, columns, chunks, uvqk_ref, wout_ref, small_ref, *scratch):
        copy.wait()


def unpack_last_kernel(planes, columns, *refs):
    peers = columns - 1
    theirs, before_ref = refs[:peers], refs[peers + 2]
    uvqk_ref, wout_ref, b_ref, g1_ref, g2_ref, bo_ref, pos_ref, time_ref, small_ref, *scratch = refs[peers + 3 :]
    small_ref[...] = before_ref[...]
    chunks = chunks_of(planes, 2, theirs, 1, 1)
    copies = unpack(planes, columns, chunks, uvqk_ref, wout_ref, small_ref, *scratch)
    at = 0
    for out in (b_ref, g1_ref, g2_ref, bo_ref):
        for col in range(0, out.shape[1], LANES):
            out[:, col : col + LANES] = small_ref[at : at + 1, :]
            at += 1
    at = (at + 7) // 8 * 8
    heads, count = pos_ref.shape
    pos_ref[...] = small_ref[at : at + heads, 0:count]
    time_ref[...] = small_ref[at + heads : at + 2 * heads, 0:count]
    for copy in copies:
        copy.wait()


def add_up(first, *rest):
    total = first.astype(F32)
    for other in rest:
        total = total + other.astype(F32)
    return total.astype(BF16)


def xor_step(value, size, step):
    return lax.ppermute(value, "dp", [(i, i ^ step) for i in range(size)])


def reduce_step(pieces, size, stride):
    return add_up(pieces[0], *(xor_step(pieces[k], size, k * stride) for k in range(1, len(pieces))))


def gather_step(own, size, stride, peers):
    return [own] + [xor_step(own, size, k * stride) for k in range(1, peers)]


def swap_cores(value):
    return lax.ppermute(value, "table", [(0, 1), (1, 0)])


def on_device(
    item_table,
    token_request_slot,
    request_rows,
    lengths,
    assignment,
    timestamps,
    item_counts,
    first_norm_gain,
    w_uvqk,
    b_uvqk,
    norm2_gain,
    w_out,
    b_out,
    pos_weight,
    time_weight,
    out_grad,
):
    rows = token_request_slot.shape[0]
    rows_dev, width = item_table.shape
    replicas = lax.axis_size("dp")
    groups = lax.axis_size("table")
    devices = replicas * groups
    cap = request_rows.shape[2]
    piece = rows // replicas
    heads, count = pos_weight.shape
    slots = devices * cap
    columns = 4
    planes = replicas // columns
    staged = (
        groups == 2
        and replicas == 16
        and width % (32 * replicas) == 0
        and (2 * heads + SMALL_ROWS - 16) <= width // 2
    )
    mb = MIB

    slot_row = token_request_slot.reshape(1, rows)
    time_row = timestamps.reshape(1, rows)
    counts_2d = item_counts.reshape(rows_dev // LANES, LANES)
    msg = call(
        functools.partial(request_kernel, piece, cap),
        shape_of((devices, LANES), I32),
        [HBM] * 5,
        mb,
        mb // 8,
        scratch=(
            pltpu.VMEM((cap, devices), I32),
            pltpu.VMEM((1, rows), I32),
            pltpu.VMEM(lengths.shape, I32),
            pltpu.VMEM(lengths.shape, I32),
            pltpu.VMEM(counts_2d.shape, I32),
            pltpu.SemaphoreType.DMA((5,)),
        ),
        room=64,
    )(request_rows.transpose(0, 2, 1).reshape(cap, devices), slot_row, lengths, assignment, counts_2d)
    asked = lax.all_to_all(msg.reshape(devices, 1, LANES), BOTH, 0, 0, tiled=True).reshape(devices, LANES)
    served = call(
        functools.partial(serve_kernel, cap), shape_of((slots, width), BF16), [VMEM] * 2, 1 << 30, 5 * mb
    )(asked, item_table)
    go = call(go_kernel, shape_of((rows, width), BF16), [VMEM] * 3, 64 * mb, mb)(lengths, assignment, out_grad)
    fetched = lax.all_to_all(served.reshape(devices, cap, width), BOTH, 0, 0, tiled=True)
    new_counts, log_q, asked_row = call(
        functools.partial(counts_kernel, cap, rows_dev * devices),
        (
            shape_of((rows_dev // LANES, LANES), I32),
            shape_of((rows_dev // LANES, LANES), F32),
            shape_of((8, slots), F32),
        ),
        [VMEM] * 2,
        64 * mb,
        mb,
    )(asked, counts_2d)
    home = call(take_kernel, shape_of((rows, width), BF16), [VMEM] * 2, 64 * mb, mb)(
        slot_row, fetched.reshape(slots, width)
    )
    if staged:
        got_go = swap_cores(go)
    x = lax.all_to_all(home.reshape(replicas, piece, width), "dp", 0, 0, tiled=True).reshape(rows, width)
    if staged:
        x, got_go = lax.optimization_barrier((x, got_go))

    half_cols = 2 * width
    g1, g2 = first_norm_gain.reshape(1, width), norm2_gain.reshape(1, width)
    msg_cols = half_cols + width + width // 2 if staged else LANES
    layer_out, n1, y, dh, ds, g2_grad, to_core = call(
        functools.partial(layer_kernel, staged),
        (
            shape_of((rows, width), BF16),
            shape_of((rows, width), BF16),
            shape_of((rows, width), BF16),
            shape_of((rows, 4 * width), BF16),
            shape_of((heads, rows, rows), BF16),
            shape_of((1, width), F32),
            shape_of((rows, msg_cols), BF16),
        ),
        [VMEM] * 13,
        2 << 30,
        8 * mb,
        scratch=(
            pltpu.VMEM((rows, 4 * width), F32),
            pltpu.VMEM((heads, rows, rows), F32),
            pltpu.VMEM((heads, rows, rows), BF16),
        ),
        room=24,
    )(
        x,
        w_uvqk,
        b_uvqk.reshape(1, 4 * width),
        g1,
        g2,
        w_out,
        b_out.reshape(1, width),
        lengths,
        assignment,
        time_row,
        out_grad,
        pos_weight,
        time_weight,
    )
    def home_again(dx):
        return lax.all_to_all(dx.reshape(replicas, piece, width), "dp", 0, 0, tiled=True).reshape(rows, width)

    def to_owners(back):
        return send_sums(slot_sums(back))

    def slot_sums(back):
        return call(slot_sum_kernel, shape_of((slots, width), BF16), [VMEM] * 2, 64 * mb, mb)(slot_row, back)
    def send_sums(sums):
        sums = lax.all_to_all(sums.reshape(devices, cap, width), BOTH, 0, 0, tiled=True)
        return sums.reshape(slots, width)

    def into_table(got_sums):
        block = min(512, rows_dev)
        return call(
            scatter_kernel,
            shape_of((rows_dev, width), F32),
            [VMEM] * 2,
            1 << 30,
            8 * mb,
            scratch=(
                pltpu.VMEM((rows_dev // block, block, width), F32),
                pltpu.SemaphoreType.DMA((rows_dev // block,)),
            ),
            room=24,
            out_specs=HBM,
        )(asked_row, got_sums)

    if staged:
        got = swap_cores(to_core)
    dx, g1_grad = call(
        dx_kernel, (shape_of((rows, width), BF16), shape_of((1, width), F32)), [VMEM] * 5, 1 << 29, 4 * mb
    )(dh, w_uvqk, x, g1, go)
    small = call(
        functools.partial(small_kernel, count),
        shape_of((width // 2, LANES), F32),
        [VMEM] * 6,
        1 << 28,
        2 * mb,
    )(ds, time_row, dh, go, g1_grad, g2_grad)
    if staged:
        short = width // replicas // 2
        pieces = call(
            functools.partial(pack_kernel, planes, columns),
            tuple(shape_of((2, short, 5 * width + LANES), BF16) for _ in range(2 * columns)),
            [VMEM] * 7,
            1 << 30,
            6 * mb,
            scratch=(pltpu.VMEM((width, half_cols), F32), pltpu.VMEM((width // 2, width), F32)),
        )(dh, n1, y, go, got, got_go, small)
        dx, *pieces = lax.optimization_barrier((dx, *pieces))
        nears, fars = pieces[:columns], pieces[columns:]
        back = home_again(dx)
        got_far = [xor_step(fars[k], replicas, k) for k in range(1, columns)]
        nears, got_far[0] = lax.optimization_barrier((nears, got_far[0]))
        far_line = add_up(fars[0], *got_far)
        got_line = [xor_step(far_line[k - 2], replicas, k * columns) for k in range(2, planes)]
        near_line = reduce_step(nears, replicas, 1)
        near_line, back = lax.optimization_barrier((near_line, back))
        got_next = xor_step(near_line[1], replicas, columns)
        sums = slot_sums(back)
        own = add_up(near_line[0], got_next, *got_line)
        own, sums = lax.optimization_barrier((own, sums))
        next_own = xor_step(own, replicas, columns)
        far = [xor_step(own, replicas, k * columns) for k in range(2, planes)]
        near = jnp.stack([own, next_own])
        nears = gather_step(near, replicas, 1, columns)
        far[1], sums = lax.optimization_barrier((far[1], sums))
        got_sums = send_sums(sums)
        far = jnp.stack(far)
        table_grad = into_table(got_sums)
        fars = gather_step(far, replicas, 1, columns)
        their_nears = [swap_cores(piece) for piece in nears]
        their_far = swap_cores(far)
        small_shape = shape_of((width // 2, LANES), F32)
        wide_shapes = (shape_of((width, 4 * width), F32), shape_of((width, width), F32))

        def unpack_call(body, specs, outs, chunks, scratch=(), aliases=None):
            return call(
                functools.partial(body, planes, columns),
                wide_shapes + outs,
                specs,
                mb,
                3 * mb,
                scratch=scratch
                + (
                    pltpu.VMEM((chunks, 2 * short, half_cols), F32),
                    pltpu.VMEM((chunks, short, width), F32),
                    pltpu.SemaphoreType.DMA((2 * chunks,)),
                ),
                out_specs=(HBM, HBM) + (VMEM,) * len(outs),
                aliases=aliases,
            )

        peers = columns - 1
        wides = {peers: 0, peers + 1: 1}
        wide_specs = [VMEM] * peers + [HBM, HBM, VMEM]
        *sums_so_far, small_sum = unpack_call(
            unpack_first_kernel, [VMEM] * (2 * columns + 2), (small_shape,), 2 * (2 * columns + 2)
        )(*nears, far, *their_nears, their_far)
        fars, small_sum, table_grad = lax.optimization_barrier((fars, small_sum, table_grad))
        their_fars = [swap_cores(piece) for piece in fars[1:]]
        *sums_so_far, small_sum = unpack_call(
            unpack_next_kernel, wide_specs, (small_shape,), 2 * peers, aliases=wides
        )(*fars[1:], *sums_so_far, small_sum)
        w_uvqk_sum, w_out_sum, b_sum, g1_sum, g2_sum, bo_sum, pos_sum, time_sum = unpack_call(
            unpack_last_kernel,
            wide_specs,
            (
                shape_of((1, 4 * width), F32),
                shape_of((1, width), F32),
                shape_of((1, width), F32),
                shape_of((1, width), F32),
                shape_of((heads, count), F32),
                shape_of((heads, count), F32),
            ),
            2 * peers,
            scratch=(pltpu.VMEM(small_shape.shape, F32),),
            aliases=wides,
        )(*their_fars, *sums_so_far, small_sum)
    else:
        table_grad = into_table(to_owners(home_again(dx)))
        w_uvqk_sum, w_out_sum, parts = lax.psum((dot_tn(n1, dh), dot_tn(y, go), small[0:SMALL_ROWS]), BOTH)
        at = 4 * width // LANES
        step = width // LANES
        b_sum = parts[0:at]
        g1_sum, g2_sum, bo_sum = (parts[at + n * step : at + (n + 1) * step] for n in range(3))
        at = (at + 3 * step + 7) // 8 * 8
        pos_sum = parts[at : at + heads, 0:count]
        time_sum = parts[at + heads : at + 2 * heads, 0:count]
    return (
        layer_out,
        table_grad,
        g1_sum.reshape(width),
        w_uvqk_sum,
        b_sum.reshape(4 * width),
        g2_sum.reshape(width),
        w_out_sum,
        bo_sum.reshape(width),
        pos_sum,
        time_sum,
        new_counts.reshape(rows_dev),
        log_q.reshape(rows_dev),
    )


def solution(mesh):
    split = P(("dp", "table"))
    rows_split = P(("dp", "table"), None)
    placed = (
        rows_split,
        split,
        P(("dp", "table"), None, None),
        P("table", None),
        P("table", None),
        split,
        split,
        P(),
        P(),
        P(),
        P(),
        P(),
        P(),
        P(),
        P(),
        rows_split,
    )
    return jax.shard_map(
        on_device,
        mesh=mesh,
        in_specs=placed,
        out_specs=(rows_split, rows_split, P(), P(), P(), P(), P(), P(), P(), P(), split, split),
        check_vma=False,
    )
```

```python
import functools

import jax
import jax.numpy as jnp
from jax import lax
from jax.experimental import pallas as pl
from jax.experimental.pallas import tpu as pltpu
from jax.sharding import PartitionSpec as P

EPSILON = 1e-05
MASKED = -1e30
F32 = jnp.float32
BF16 = jnp.bfloat16
I32 = jnp.int32
BOTH = ("dp", "table")
LANES = 128
VMEM = pl.BlockSpec(memory_space=pltpu.VMEM)
SMEM = pl.BlockSpec(memory_space=pltpu.SMEM)
HBM = pl.BlockSpec(memory_space=pltpu.HBM)
MIB = 1 << 20


def dot_nn(a, b):
    return lax.dot_general(a, b, (((1,), (0,)), ((), ())), preferred_element_type=F32)


def dot_nt(a, b):
    return lax.dot_general(a, b, (((1,), (1,)), ((), ())), preferred_element_type=F32)


def dot_tn(a, b):
    return lax.dot_general(a, b, (((0,), (0,)), ((), ())), preferred_element_type=F32)


def dot_exact(a, b):
    return lax.dot_general(
        a, b, (((1,), (0,)), ((), ())), precision=lax.Precision.HIGHEST, preferred_element_type=F32
    )


def iota(shape, dim):
    return lax.broadcasted_iota(I32, shape, dim)


def shape_of(shape, dtype):
    return jax.ShapeDtypeStruct(shape, dtype)


def cost(flops, moved):
    return pl.CostEstimate(flops=int(flops), bytes_accessed=int(moved), transcendentals=0)


def params(mib):
    return pltpu.CompilerParams(vmem_limit_bytes=mib * MIB)


def call(body, outs, specs, flops, moved, scratch=(), room=16, out_specs=None, aliases=None):
    if out_specs is None:
        out_specs = tuple(VMEM for _ in outs) if isinstance(outs, tuple) else VMEM
    return pl.pallas_call(
        body,
        out_shape=outs,
        in_specs=specs,
        out_specs=out_specs,
        scratch_shapes=list(scratch),
        input_output_aliases=aliases or {},
        compiler_params=params(room),
        cost_estimate=cost(flops, moved),
    )


def start_all(sources, targets, sems):
    copies = [pltpu.make_async_copy(a, b, sems.at[n]) for n, (a, b) in enumerate(zip(sources, targets))]
    for copy in copies:
        copy.start()
    return copies


def request_kernel(piece, cap, *refs):
    sources, msg_ref, held, sems = refs[:5], refs[5], refs[6:11], refs[11]
    for copy in start_all(sources, held, sems):
        copy.wait()
    rows_ref, slot_ref, len_ref, dest_ref, counts_ref = held
    owners = rows_ref.shape[1]
    tokens = slot_ref.shape[1]
    replicas = tokens // piece
    my_dp = lax.axis_index("dp")
    lens = len_ref[...].astype(F32)
    takes = dest_ref[...] == iota((replicas, dest_ref.shape[1]), 0)
    totals = jnp.sum(jnp.where(takes, lens, 0.0), axis=1, keepdims=True)
    token = iota((replicas, tokens), 1)
    target = iota((replicas, tokens), 0)
    place = (my_dp * piece + token - target * piece).astype(F32)
    here = (token >= target * piece) & (token < (target + 1) * piece) & (place < totals)
    valid = jnp.sum(jnp.where(here, 1.0, 0.0), axis=0, keepdims=True)
    slot = slot_ref[...]
    by_owner = jnp.where(slot // cap == iota((owners, tokens), 0), valid, 0.0).astype(BF16)
    by_slot = jnp.where(slot % cap + cap == iota((LANES, tokens), 0), 1.0, 0.0).astype(BF16)
    counts = dot_nt(by_owner, by_slot)
    old = jnp.sum(counts_ref[...].astype(F32), axis=0, keepdims=True)
    total = jnp.sum(old, axis=1, keepdims=True) + jnp.sum(valid, axis=1, keepdims=True)
    lane = iota((owners, LANES), 1)
    place = jnp.where(iota((cap, LANES), 0) == iota((cap, LANES), 1), 1.0, 0.0)
    wanted = dot_exact(jnp.transpose(rows_ref[...].astype(F32)), place)
    msg_ref[...] = (jnp.where(lane == 2 * cap, total, counts) + wanted).astype(I32)


def asked_column(cap, asked_ref, first):
    askers = asked_ref.shape[0]
    total = askers * cap
    spread = jnp.where(iota((total, askers), 0) // cap == iota((total, askers), 1), 1.0, 0.0)
    each = dot_exact(spread, asked_ref[...].astype(F32))
    pick = iota((total, LANES), 1) == iota((total, LANES), 0) % cap + first
    return jnp.sum(jnp.where(pick, each, 0.0), axis=1, keepdims=True)


def serve_kernel(cap, asked_ref, table_ref, served_ref):
    rows = asked_column(cap, asked_ref, 0)
    total = rows.shape[0]
    step = min(512, table_ref.shape[0])
    lane = iota((total, step), 1).astype(F32)
    acc = None
    for base in range(0, table_ref.shape[0], step):
        pick = jnp.where(rows - float(base) == lane, 1.0, 0.0).astype(BF16)
        part = dot_nn(pick, table_ref[base : base + step, :])
        acc = part if acc is None else acc + part
    served_ref[...] = acc.astype(BF16)


def counts_kernel(cap, items, asked_ref, counts_ref, new_ref, log_ref, row_ref):
    rows = asked_column(cap, asked_ref, 0)
    added = asked_column(cap, asked_ref, cap)
    total = rows.shape[0]
    lines = counts_ref.shape[0]
    line = jnp.floor(rows * (1.0 / LANES))
    lane = rows - line * LANES
    by_line = jnp.where(line == iota((total, lines), 1).astype(F32), added, 0.0).astype(BF16)
    by_lane = jnp.where(lane == iota((total, LANES), 1).astype(F32), 1.0, 0.0).astype(BF16)
    new = counts_ref[...].astype(F32) + dot_tn(by_line, by_lane)
    whole = jnp.sum(asked_ref[:, 2 * cap : 2 * cap + 1].astype(F32), axis=0, keepdims=True)
    new_ref[...] = new.astype(I32)
    log_ref[...] = jnp.log(new + 1.0) - jnp.log(whole + float(items))
    row_ref[...] = jnp.transpose(jnp.broadcast_to(rows, (total, LANES)))[0:8, :]


def take_kernel(slot_ref, fetched_ref, home_ref):
    total = fetched_ref.shape[0]
    pick = jnp.where(slot_ref[...] == iota((total, slot_ref.shape[1]), 0), 1.0, 0.0).astype(BF16)
    home_ref[...] = dot_tn(pick, fetched_ref[...]).astype(BF16)


def slot_sum_kernel(slot_ref, back_ref, sums_ref):
    total = sums_ref.shape[0]
    pick = jnp.where(slot_ref[...] == iota((total, slot_ref.shape[1]), 0), 1.0, 0.0).astype(BF16)
    sums_ref[...] = dot_nn(pick, back_ref[...]).astype(BF16)


def scatter_kernel(row_ref, got_ref, out_ref, held_ref, sems):
    parts, block, _ = held_ref.shape
    total = got_ref.shape[0]
    line = iota((block, total), 0).astype(F32)
    copies = []
    for n in range(parts):
        pick = jnp.where(row_ref[0:1, :] - float(n * block) == line, 1.0, 0.0).astype(BF16)
        held_ref[n] = dot_nn(pick, got_ref[...])
        copies += start_all(
            (held_ref.at[n],), (out_ref.at[pl.ds(n * block, block), :],), sems.at[pl.ds(n, 1)]
        )
    for copy in copies:
        copy.wait()


def segments(len_ref, dest_ref, rows):
    nhist = len_ref.shape[1]
    mine = jnp.where(dest_ref[...] == lax.axis_index("dp"), len_ref[...], 0).astype(F32)
    later = iota((nhist, nhist), 0)
    other = iota((nhist, nhist), 1)
    ends = jnp.sum(jnp.where(other <= later, mine, 0.0), axis=1, keepdims=True)
    starts = jnp.sum(jnp.where(other < later, mine, 0.0), axis=1, keepdims=True)
    place = iota((nhist, rows), 1).astype(F32)
    label = iota((nhist, rows), 0).astype(F32) + 1.0
    return jnp.sum(jnp.where((starts <= place) & (place < ends), label, 0.0), axis=0, keepdims=True)


def valid_rows(seg, rows):
    return jnp.transpose(jnp.broadcast_to(jnp.where(seg > 0.0, 1.0, 0.0), (LANES, rows)))


def masked_grad(og_ref, valid):
    wide = og_ref.shape[1] // LANES
    return (og_ref[...].astype(F32) * jnp.concatenate([valid] * wide, axis=1)).astype(BF16)


def pos_bounds(rows, count):
    return [max(1, rows // 2 ** (count - m)) for m in range(count)]


def time_bounds(count):
    return [float(4**m) for m in range(count)]


def time_gaps(time_ref, rows):
    stamp = jnp.broadcast_to(time_ref[...].astype(F32), (rows, rows))
    return jnp.transpose(stamp) - stamp


def steps_passed(value, bounds):
    total = jnp.where(value >= bounds[0], 1, 0)
    for bound in bounds[1:]:
        total = total + jnp.where(value >= bound, 1, 0)
    return total


def bias_index(seg, time_ref, rows, count):
    across = jnp.broadcast_to(seg, (rows, rows))
    down = jnp.transpose(across)
    dist = iota((rows, rows), 0) - iota((rows, rows), 1)
    near = steps_passed(dist, pos_bounds(rows, count))
    late = steps_passed(time_gaps(time_ref, rows), time_bounds(count))
    mask = (across == down) & (down > 0.0) & (dist >= 0)
    return jnp.where(mask, near * (count + 1) + late, LANES - 1)


def bias_table(pos_ref, timew_ref):
    heads, count = pos_ref.shape
    entry = iota((heads, LANES), 1)
    near = entry // (count + 1)
    late = entry - near * (count + 1)
    table = jnp.zeros((heads, LANES), F32)
    for m in range(count):
        table = table + jnp.where(near > m, pos_ref[:, m : m + 1], 0.0)
        table = table + jnp.where(late > m, timew_ref[:, m : m + 1], 0.0)
    return jnp.where(entry == LANES - 1, MASKED, table)


def look_up(table_row, index):
    rows, cols = index.shape
    spread = jnp.broadcast_to(table_row, (rows, LANES))
    return jnp.concatenate(
        [jnp.take_along_axis(spread, index[:, at : at + LANES], axis=1) for at in range(0, cols, LANES)], axis=1
    )


def norm_of(value):
    centered = value - jnp.mean(value, axis=1, keepdims=True)
    scale = lax.rsqrt(jnp.mean(centered * centered, axis=1, keepdims=True) + EPSILON)
    return centered * scale, scale


def norm_back(grad_hat, normed, scale):
    first = jnp.mean(grad_hat, axis=1, keepdims=True)
    second = jnp.mean(grad_hat * normed, axis=1, keepdims=True)
    return scale * (grad_hat - first - normed * second)


def sigmoid(value):
    return 0.5 * jnp.tanh(0.5 * value) + 0.5


def layer_kernel(
    staged,
    x_ref,
    w_ref,
    b_ref,
    g1_ref,
    g2_ref,
    wo_ref,
    bo_ref,
    len_ref,
    dest_ref,
    time_ref,
    og_ref,
    pos_ref,
    timew_ref,
    lo_ref,
    n1_ref,
    y_ref,
    go_ref,
    dh_ref,
    ds_ref,
    g2g_ref,
    msg_ref,
    h_ref,
    slope_ref,
    a_ref,
):
    rows, width = x_ref.shape
    heads, count = pos_ref.shape
    pairs = heads // 2
    seg = segments(len_ref, dest_ref, rows)
    valid = valid_rows(seg, rows)
    go_ref[...] = masked_grad(og_ref, valid)
    dmix = dot_nt(go_ref[...], wo_ref[...])
    index = bias_index(seg, time_ref, rows, count)
    table = bias_table(pos_ref, timew_ref)
    x = x_ref[...].astype(F32)
    xhat, _ = norm_of(x)
    n1 = (xhat * g1_ref[...]).astype(BF16)
    n1_ref[...] = n1
    acts = []
    for part in range(4):
        cols = slice(part * width, (part + 1) * width)
        h = dot_nn(n1, w_ref[:, cols]) + b_ref[:, cols]
        sig = sigmoid(h)
        acts.append(h * sig)
        h_ref[:, cols] = sig * (1.0 + h * (1.0 - sig))
    u = acts[0]
    v, q, k = (a.astype(BF16) for a in acts[1:])
    lane = iota((rows, LANES), 1)
    low = lane < LANES // 2
    zero = jnp.zeros((rows, LANES), BF16)

    def half(value, parity):
        return jnp.where(low if parity == 0 else ~low, value, zero)

    def stacked(value):
        return jnp.concatenate([half(value, 0), half(value, 1)], axis=0)

    def abreast(value):
        return jnp.concatenate([value[:rows], value[rows:]], axis=1)

    outs = []
    for pair in range(pairs):
        cols = slice(pair * LANES, (pair + 1) * LANES)
        bias = jnp.concatenate([look_up(table[g : g + 1, :], index) for g in (2 * pair, 2 * pair + 1)], axis=0)
        s = dot_nt(stacked(q[:, cols]), k[:, cols]) * 0.125 + bias
        sig = sigmoid(s)
        a = (s * sig).astype(BF16)
        a_ref[pair] = a
        slope_ref[pair] = sig * (1.0 + s * (1.0 - sig))
        outs.append(dot_nn(abreast(a), stacked(v[:, cols])))
    o = jnp.concatenate(outs, axis=1)
    ohat, scale2 = norm_of(o)
    g2 = g2_ref[...]
    n2 = ohat * g2
    y = (n2 * u).astype(BF16)
    y_ref[...] = y
    branch = dot_nn(y, wo_ref[...]) + bo_ref[...]
    lo_ref[...] = (jnp.concatenate([valid] * (width // LANES), axis=1) * (x + branch)).astype(BF16)
    du = dmix * n2
    e2 = dmix * u
    g2g_ref[...] = jnp.sum(e2 * ohat, axis=0, keepdims=True)
    do = norm_back(e2 * g2, ohat, scale2).astype(BF16)
    dh_ref[:, 0:width] = (du * h_ref[:, 0:width]).astype(BF16)
    for pair in range(pairs):
        cols = slice(pair * LANES, (pair + 1) * LANES)
        dom = stacked(do[:, cols])
        ds = (dot_nt(dom, v[:, cols]) * slope_ref[pair]).astype(BF16)
        ds_ref[2 * pair] = ds[:rows]
        ds_ref[2 * pair + 1] = ds[rows:]
        dv = dot_tn(a_ref[pair], dom)
        dq = dot_nn(abreast(ds), stacked(k[:, cols]))
        dk = dot_tn(ds, stacked(q[:, cols]))
        for part, value in ((1, dv), (2, dq * 0.125), (3, dk * 0.125)):
            at = slice(part * width + pair * LANES, part * width + (pair + 1) * LANES)
            dh_ref[:, at] = (value * h_ref[:, at]).astype(BF16)
    if staged:
        other = 1 - lax.axis_index("table")
        half_cols = 2 * width
        msg_ref[:, 0:half_cols] = dh_ref[:, pl.ds(pl.multiple_of(other * half_cols, half_cols), half_cols)]
        msg_ref[:, half_cols : half_cols + width] = n1
        half_y = width // 2
        y_half = y_ref[:, pl.ds(pl.multiple_of(other * half_y, half_y), half_y)].astype(F32)
        y_half = y_half * jnp.concatenate([valid] * (half_y // LANES), axis=1)
        msg_ref[:, half_cols + width :] = y_half.astype(BF16)
    else:
        msg_ref[...] = jnp.zeros_like(msg_ref)


SMALL_ROWS = 48


def prefix_ends(time_ref, rows, count):
    time_lane = 64
    row = iota((1, rows), 1).astype(F32)
    ends = [row - float(bound) for bound in pos_bounds(rows, count)]
    ends += [jnp.full((time_lane - count, rows), -1.0, F32)]
    stamp = jnp.broadcast_to(time_ref[...].astype(F32), (rows, rows))
    gaps = stamp - jnp.transpose(stamp)
    for bound in time_bounds(count):
        ends.append(jnp.sum(jnp.where(gaps >= bound, 1.0, 0.0), axis=0, keepdims=True) - 1.0)
    ends += [jnp.full((LANES - time_lane - count, rows), -1.0, F32)]
    return jnp.transpose(jnp.concatenate(ends, axis=0)).astype(I32)


def after_kernel(count, dh_ref, w_ref, x_ref, g1_ref, go_ref, ds_ref, time_ref, g2g_ref, *rest):
    dx_out, out_ref, dx_ref, sem = rest
    heads, rows, _ = ds_ref.shape
    xhat, scale = norm_of(x_ref[...].astype(F32))
    dn1 = dot_nt(dh_ref[...], w_ref[...])
    go = go_ref[...].astype(F32)
    dx_ref[...] = (norm_back(dn1 * g1_ref[...], xhat, scale) + go).astype(BF16)
    copy = pltpu.make_async_copy(dx_ref, dx_out, sem)
    copy.start()
    out_ref[...] = jnp.zeros_like(out_ref)
    g1_grad = jnp.sum(dn1 * xhat, axis=0, keepdims=True)
    b_grad = jnp.sum(dh_ref[...].astype(F32), axis=0, keepdims=True)
    go_sum = jnp.sum(go, axis=0, keepdims=True)
    at = 0
    for value in (b_grad, g1_grad, g2g_ref[...], go_sum):
        for col in range(0, value.shape[1], LANES):
            out_ref[at : at + 1, :] = value[:, col : col + LANES]
            at += 1
    at = (at + 7) // 8 * 8
    ends = prefix_ends(time_ref, rows, count)
    upto = jnp.where(iota((rows, rows), 0) <= iota((rows, rows), 1), 1.0, 0.0).astype(BF16)
    prefix = dot_nn(ds_ref[...].reshape(heads * rows, rows), upto)
    tables = [
        ((ends >= first) & (ends < first + LANES), jnp.clip(ends - first, 0, LANES - 1))
        for first in range(0, rows, LANES)
    ]
    sums = []
    for g in range(heads):
        found = jnp.zeros((rows, LANES), F32)
        for n, (here, index) in enumerate(tables):
            value = prefix[g * rows : (g + 1) * rows, n * LANES : (n + 1) * LANES]
            found = found + jnp.where(here, jnp.take_along_axis(value, index, axis=1), 0.0)
        sums.append(jnp.sum(found, axis=0, keepdims=True))
    sums = jnp.concatenate(sums, axis=0)
    out_ref[at : at + heads, :] = sums
    out_ref[at + heads : at + 2 * heads, 0 : LANES // 2] = sums[:, LANES // 2 :]
    copy.wait()


def place_of(columns):
    my_dp = lax.axis_index("dp")
    return lax.rem(my_dp, columns), lax.div(my_dp, columns)


def pack_kernel(planes, columns, dh_ref, n1_ref, y_ref, go_ref, got_ref, got_grad_ref, small_ref, *rest):
    nears, fars, (uv_ref, wo_ref) = rest[:columns], rest[columns : 2 * columns], rest[2 * columns :]
    width = n1_ref.shape[1]
    core = lax.axis_index("table")
    my_xy, my_z = place_of(columns)
    half_cols = 2 * width
    half_y = width // 2
    dh = jnp.concatenate(
        [dh_ref[:, pl.ds(pl.multiple_of(core * half_cols, half_cols), half_cols)], got_ref[:, 0:half_cols]],
        axis=0,
    )
    n1 = jnp.concatenate([n1_ref[...], got_ref[:, half_cols : half_cols + width]], axis=0)
    y = jnp.concatenate(
        [y_ref[:, pl.ds(pl.multiple_of(core * half_y, half_y), half_y)], got_ref[:, half_cols + width :]],
        axis=0,
    )
    go = jnp.concatenate([go_ref[...], got_grad_ref[...]], axis=0)
    uv_ref[...] = dot_tn(n1, dh)
    wo_ref[...] = dot_tn(y, go)
    short = half_y // (planes * columns)
    for rel_xy in range(columns):
        for rel_z in range(planes):
            chunk = jnp.bitwise_xor(my_xy, rel_xy) * planes + jnp.bitwise_xor(my_z, rel_z)
            out = (nears, fars)[rel_z // 2][rel_xy].at[rel_z % 2]
            for part in range(2):
                at = pl.multiple_of((2 * chunk + part) * short, short)
                out[:, part * half_cols : (part + 1) * half_cols] = uv_ref[pl.ds(at, short), :].astype(BF16)
            at = pl.multiple_of(chunk * short, short)
            out[:, 2 * half_cols : 2 * half_cols + width] = wo_ref[pl.ds(at, short), :].astype(BF16)
            out[:, 2 * half_cols + width :] = small_ref[pl.ds(at, short), :].astype(BF16)


def unpack(planes, columns, chunks, uvqk_ref, wout_ref, small_ref, held_uvqk, held_wout, sems):
    short = held_wout.shape[1]
    width = held_wout.shape[2]
    core = lax.axis_index("table")
    my_xy, my_z = place_of(columns)
    half_cols = 2 * width
    half_y = width // 2
    wout_lanes = slice(2 * half_cols, 2 * half_cols + width)
    small_lanes = slice(2 * half_cols + width, 2 * half_cols + width + LANES)
    copies = []
    for n, (rel_xy, rel_z, whose, piece) in enumerate(chunks):
        chunk = jnp.bitwise_xor(my_xy, rel_xy) * planes + jnp.bitwise_xor(my_z, rel_z)
        side = jnp.bitwise_xor(core, whose)
        for part in range(2):
            held_uvqk[n, part * short : (part + 1) * short, :] = piece[
                :, part * half_cols : (part + 1) * half_cols
            ].astype(F32)
        held_wout[n] = piece[:, wout_lanes].astype(F32)
        tall = pl.ds(pl.multiple_of(chunk * 2 * short, 2 * short), 2 * short)
        cols = pl.ds(pl.multiple_of(side * half_cols, half_cols), half_cols)
        rows = pl.ds(pl.multiple_of(side * half_y + chunk * short, short), short)
        copies += start_all(
            (held_uvqk.at[n], held_wout.at[n]),
            (uvqk_ref.at[tall, cols], wout_ref.at[rows, :]),
            sems.at[pl.ds(2 * n, 2)],
        )
        small_ref[pl.ds(pl.multiple_of(chunk * short, short), short), :] += piece[:, small_lanes].astype(F32)
    return copies


def chunks_of(planes, first_z, pieces, whose, first_xy=0):
    return [
        (first_xy + xy, first_z + z, whose, piece.at[z])
        for xy, piece in enumerate(pieces)
        for z in range(min(2, planes - first_z))
    ]


def unpack_first_kernel(planes, columns, *refs):
    mine, theirs = refs[: columns + 1], refs[columns + 1 : 2 * columns + 2]
    uvqk_ref, wout_ref, small_ref, *scratch = refs[2 * columns + 2 :]
    small_ref[...] = jnp.zeros_like(small_ref)
    chunks = []
    for whose, pieces in enumerate((mine, theirs)):
        chunks += chunks_of(planes, 0, pieces[:columns], whose) + chunks_of(planes, 2, pieces[columns:], whose)
    for copy in unpack(planes, columns, chunks, uvqk_ref, wout_ref, small_ref, *scratch):
        copy.wait()


def unpack_next_kernel(planes, columns, *refs):
    peers = columns - 1
    mine, before_ref = refs[:peers], refs[peers + 2]
    uvqk_ref, wout_ref, small_ref, *scratch = refs[peers + 3 :]
    small_ref[...] = before_ref[...]
    chunks = chunks_of(planes, 2, mine, 0, 1)
    for copy in unpack(planes, columns, chunks, uvqk_ref, wout_ref, small_ref, *scratch):
        copy.wait()


def unpack_last_kernel(planes, columns, *refs):
    peers = columns - 1
    theirs, before_ref = refs[:peers], refs[peers + 2]
    uvqk_ref, wout_ref, b_ref, g1_ref, g2_ref, bo_ref, pos_ref, time_ref, small_ref, *scratch = refs[peers + 3 :]
    small_ref[...] = before_ref[...]
    chunks = chunks_of(planes, 2, theirs, 1, 1)
    copies = unpack(planes, columns, chunks, uvqk_ref, wout_ref, small_ref, *scratch)
    at = 0
    for out in (b_ref, g1_ref, g2_ref, bo_ref):
        for col in range(0, out.shape[1], LANES):
            out[:, col : col + LANES] = small_ref[at : at + 1, :]
            at += 1
    at = (at + 7) // 8 * 8
    heads, count = pos_ref.shape
    pos_ref[...] = small_ref[at : at + heads, 0:count]
    time_ref[...] = small_ref[at + heads : at + 2 * heads, 0:count]
    for copy in copies:
        copy.wait()


def add_up(first, *rest):
    total = first.astype(F32)
    for other in rest:
        total = total + other.astype(F32)
    return total.astype(BF16)


def xor_step(value, size, step):
    return lax.ppermute(value, "dp", [(i, i ^ step) for i in range(size)])


def reduce_step(pieces, size, stride):
    return add_up(pieces[0], *(xor_step(pieces[k], size, k * stride) for k in range(1, len(pieces))))


def gather_step(own, size, stride, peers):
    return [own] + [xor_step(own, size, k * stride) for k in range(1, peers)]


def swap_cores(value):
    return lax.ppermute(value, "table", [(0, 1), (1, 0)])


def on_device(
    item_table,
    token_request_slot,
    request_rows,
    lengths,
    assignment,
    timestamps,
    item_counts,
    first_norm_gain,
    w_uvqk,
    b_uvqk,
    norm2_gain,
    w_out,
    b_out,
    pos_weight,
    time_weight,
    out_grad,
):
    rows = token_request_slot.shape[0]
    rows_dev, width = item_table.shape
    replicas = lax.axis_size("dp")
    groups = lax.axis_size("table")
    devices = replicas * groups
    cap = request_rows.shape[2]
    piece = rows // replicas
    heads, count = pos_weight.shape
    slots = devices * cap
    columns = 4
    planes = replicas // columns
    staged = (
        groups == 2
        and replicas == 16
        and width % (32 * replicas) == 0
        and (2 * heads + SMALL_ROWS - 16) <= width // 2
    )
    mb = MIB

    slot_row = token_request_slot.reshape(1, rows)
    time_row = timestamps.reshape(1, rows)
    counts_2d = item_counts.reshape(rows_dev // LANES, LANES)
    msg = call(
        functools.partial(request_kernel, piece, cap),
        shape_of((devices, LANES), I32),
        [HBM] * 5,
        mb,
        mb // 8,
        scratch=(
            pltpu.VMEM((cap, devices), I32),
            pltpu.VMEM((1, rows), I32),
            pltpu.VMEM(lengths.shape, I32),
            pltpu.VMEM(lengths.shape, I32),
            pltpu.VMEM(counts_2d.shape, I32),
            pltpu.SemaphoreType.DMA((5,)),
        ),
        room=64,
    )(request_rows.transpose(0, 2, 1).reshape(cap, devices), slot_row, lengths, assignment, counts_2d)
    if staged:
        msg, other_grad = lax.optimization_barrier((msg, out_grad))
        got_grad = swap_cores(other_grad)
    asked = lax.all_to_all(msg.reshape(devices, 1, LANES), BOTH, 0, 0, tiled=True).reshape(devices, LANES)
    if staged:
        asked, got_grad = lax.optimization_barrier((asked, got_grad))
    served = call(
        functools.partial(serve_kernel, cap), shape_of((slots, width), BF16), [VMEM] * 2, 1 << 30, 5 * mb
    )(asked, item_table)
    fetched = lax.all_to_all(served.reshape(devices, cap, width), BOTH, 0, 0, tiled=True)
    new_counts, log_q, asked_row = call(
        functools.partial(counts_kernel, cap, rows_dev * devices),
        (
            shape_of((rows_dev // LANES, LANES), I32),
            shape_of((rows_dev // LANES, LANES), F32),
            shape_of((8, slots), F32),
        ),
        [VMEM] * 2,
        64 * mb,
        mb,
    )(asked, counts_2d)
    home = call(take_kernel, shape_of((rows, width), BF16), [VMEM] * 2, 64 * mb, mb)(
        slot_row, fetched.reshape(slots, width)
    )
    x = lax.all_to_all(home.reshape(replicas, piece, width), "dp", 0, 0, tiled=True).reshape(rows, width)

    half_cols = 2 * width
    g1, g2 = first_norm_gain.reshape(1, width), norm2_gain.reshape(1, width)
    msg_cols = half_cols + width + width // 2 if staged else LANES
    layer_out, n1, y, go, dh, ds, g2_grad, to_core = call(
        functools.partial(layer_kernel, staged),
        (
            shape_of((rows, width), BF16),
            shape_of((rows, width), BF16),
            shape_of((rows, width), BF16),
            shape_of((rows, width), BF16),
            shape_of((rows, 4 * width), BF16),
            shape_of((heads, rows, rows), BF16),
            shape_of((1, width), F32),
            shape_of((rows, msg_cols), BF16),
        ),
        [VMEM] * 13,
        2 << 30,
        8 * mb,
        scratch=(
            pltpu.VMEM((rows, 4 * width), F32),
            pltpu.VMEM((heads // 2, 2 * rows, rows), F32),
            pltpu.VMEM((heads // 2, 2 * rows, rows), BF16),
        ),
        room=24,
    )(
        x,
        w_uvqk,
        b_uvqk.reshape(1, 4 * width),
        g1,
        g2,
        w_out,
        b_out.reshape(1, width),
        lengths,
        assignment,
        time_row,
        out_grad,
        pos_weight,
        time_weight,
    )
    def home_again(dx):
        return lax.all_to_all(dx.reshape(replicas, piece, width), "dp", 0, 0, tiled=True).reshape(rows, width)

    def to_owners(back):
        return send_sums(slot_sums(back))

    def slot_sums(back):
        return call(slot_sum_kernel, shape_of((slots, width), BF16), [VMEM] * 2, 64 * mb, mb)(slot_row, back)
    def send_sums(sums):
        sums = lax.all_to_all(sums.reshape(devices, cap, width), BOTH, 0, 0, tiled=True)
        return sums.reshape(slots, width)

    def into_table(got_sums):
        block = min(512, rows_dev)
        return call(
            scatter_kernel,
            shape_of((rows_dev, width), F32),
            [VMEM] * 2,
            1 << 30,
            8 * mb,
            scratch=(
                pltpu.VMEM((rows_dev // block, block, width), F32),
                pltpu.SemaphoreType.DMA((rows_dev // block,)),
            ),
            room=24,
            out_specs=HBM,
        )(asked_row, got_sums)

    if staged:
        got = swap_cores(to_core)
    dx, small = call(
        functools.partial(after_kernel, count),
        (shape_of((rows, width), BF16), shape_of((width // 2, LANES), F32)),
        [VMEM] * 8,
        1 << 29,
        4 * mb,
        scratch=(pltpu.VMEM((rows, width), BF16), pltpu.SemaphoreType.DMA),
        out_specs=(HBM, VMEM),
    )(dh, w_uvqk, x, g1, go, ds, time_row, g2_grad)
    if staged:
        short = width // replicas // 2
        pieces = call(
            functools.partial(pack_kernel, planes, columns),
            tuple(shape_of((2, short, 5 * width + LANES), BF16) for _ in range(2 * columns)),
            [VMEM] * 7,
            1 << 30,
            6 * mb,
            scratch=(pltpu.VMEM((width, half_cols), F32), pltpu.VMEM((width // 2, width), F32)),
        )(dh, n1, y, go, got, got_grad, small)
        dx, *pieces = lax.optimization_barrier((dx, *pieces))
        nears, fars = pieces[:columns], pieces[columns:]
        back = home_again(dx)
        got_far = [xor_step(fars[k], replicas, k) for k in range(1, columns)]
        nears, got_far[0] = lax.optimization_barrier((nears, got_far[0]))
        far_line = add_up(fars[0], *got_far)
        got_line = [xor_step(far_line[k - 2], replicas, k * columns) for k in range(2, planes)]
        near_line = reduce_step(nears, replicas, 1)
        near_line, back = lax.optimization_barrier((near_line, back))
        got_next = xor_step(near_line[1], replicas, columns)
        sums = slot_sums(back)
        own = add_up(near_line[0], got_next, *got_line)
        own, sums = lax.optimization_barrier((own, sums))
        next_own = xor_step(own, replicas, columns)
        far = [xor_step(own, replicas, k * columns) for k in range(2, planes)]
        near = jnp.stack([own, next_own])
        nears = gather_step(near, replicas, 1, columns)
        far[1], sums = lax.optimization_barrier((far[1], sums))
        got_sums = send_sums(sums)
        far = jnp.stack(far)
        table_grad = into_table(got_sums)
        fars = gather_step(far, replicas, 1, columns)
        their_nears = [swap_cores(piece) for piece in nears]
        their_far = swap_cores(far)
        small_shape = shape_of((width // 2, LANES), F32)
        wide_shapes = (shape_of((width, 4 * width), F32), shape_of((width, width), F32))

        def unpack_call(body, specs, outs, chunks, scratch=(), aliases=None):
            return call(
                functools.partial(body, planes, columns),
                wide_shapes + outs,
                specs,
                mb,
                3 * mb,
                scratch=scratch
                + (
                    pltpu.VMEM((chunks, 2 * short, half_cols), F32),
                    pltpu.VMEM((chunks, short, width), F32),
                    pltpu.SemaphoreType.DMA((2 * chunks,)),
                ),
                out_specs=(HBM, HBM) + (VMEM,) * len(outs),
                aliases=aliases,
            )

        peers = columns - 1
        wides = {peers: 0, peers + 1: 1}
        wide_specs = [VMEM] * peers + [HBM, HBM, VMEM]
        *sums_so_far, small_sum = unpack_call(
            unpack_first_kernel, [VMEM] * (2 * columns + 2), (small_shape,), 2 * (2 * columns + 2)
        )(*nears, far, *their_nears, their_far)
        fars, small_sum, table_grad = lax.optimization_barrier((fars, small_sum, table_grad))
        their_fars = [swap_cores(piece) for piece in fars[1:]]
        *sums_so_far, small_sum = unpack_call(
            unpack_next_kernel, wide_specs, (small_shape,), 2 * peers, aliases=wides
        )(*fars[1:], *sums_so_far, small_sum)
        w_uvqk_sum, w_out_sum, b_sum, g1_sum, g2_sum, bo_sum, pos_sum, time_sum = unpack_call(
            unpack_last_kernel,
            wide_specs,
            (
                shape_of((1, 4 * width), F32),
                shape_of((1, width), F32),
                shape_of((1, width), F32),
                shape_of((1, width), F32),
                shape_of((heads, count), F32),
                shape_of((heads, count), F32),
            ),
            2 * peers,
            scratch=(pltpu.VMEM(small_shape.shape, F32),),
            aliases=wides,
        )(*their_fars, *sums_so_far, small_sum)
    else:
        table_grad = into_table(to_owners(home_again(dx)))
        w_uvqk_sum, w_out_sum, parts = lax.psum((dot_tn(n1, dh), dot_tn(y, go), small[0:SMALL_ROWS]), BOTH)
        at = 4 * width // LANES
        step = width // LANES
        b_sum = parts[0:at]
        g1_sum, g2_sum, bo_sum = (parts[at + n * step : at + (n + 1) * step] for n in range(3))
        at = (at + 3 * step + 7) // 8 * 8
        pos_sum = parts[at : at + heads, 0:count]
        time_sum = parts[at + heads : at + 2 * heads, 0:count]
    return (
        layer_out,
        table_grad,
        g1_sum.reshape(width),
        w_uvqk_sum,
        b_sum.reshape(4 * width),
        g2_sum.reshape(width),
        w_out_sum,
        bo_sum.reshape(width),
        pos_sum,
        time_sum,
        new_counts.reshape(rows_dev),
        log_q.reshape(rows_dev),
    )


def solution(mesh):
    split = P(("dp", "table"))
    rows_split = P(("dp", "table"), None)
    placed = (
        rows_split,
        split,
        P(("dp", "table"), None, None),
        P("table", None),
        P("table", None),
        split,
        split,
        P(),
        P(),
        P(),
        P(),
        P(),
        P(),
        P(),
        P(),
        rows_split,
    )
    return jax.shard_map(
        on_device,
        mesh=mesh,
        in_specs=placed,
        out_specs=(rows_split, rows_split, P(), P(), P(), P(), P(), P(), P(), P(), split, split),
        check_vma=False,
    )
```

```python
import functools

import jax
import jax.numpy as jnp
from jax import lax
from jax.experimental import pallas as pl
from jax.experimental.pallas import tpu as pltpu
from jax.sharding import PartitionSpec as P

EPSILON = 1e-05
MASKED = -1e30
F32 = jnp.float32
BF16 = jnp.bfloat16
I32 = jnp.int32
BOTH = ("dp", "table")
LANES = 128
VMEM = pl.BlockSpec(memory_space=pltpu.VMEM)
SMEM = pl.BlockSpec(memory_space=pltpu.SMEM)
HBM = pl.BlockSpec(memory_space=pltpu.HBM)
MIB = 1 << 20


def dot_nn(a, b):
    return lax.dot_general(a, b, (((1,), (0,)), ((), ())), preferred_element_type=F32)


def dot_nt(a, b):
    return lax.dot_general(a, b, (((1,), (1,)), ((), ())), preferred_element_type=F32)


def dot_tn(a, b):
    return lax.dot_general(a, b, (((0,), (0,)), ((), ())), preferred_element_type=F32)


def dot_exact(a, b):
    return lax.dot_general(
        a, b, (((1,), (0,)), ((), ())), precision=lax.Precision.HIGHEST, preferred_element_type=F32
    )


def iota(shape, dim):
    return lax.broadcasted_iota(I32, shape, dim)


def shape_of(shape, dtype):
    return jax.ShapeDtypeStruct(shape, dtype)


def cost(flops, moved):
    return pl.CostEstimate(flops=int(flops), bytes_accessed=int(moved), transcendentals=0)


def params(mib):
    return pltpu.CompilerParams(vmem_limit_bytes=mib * MIB)


def call(body, outs, specs, flops, moved, scratch=(), room=16, out_specs=None, aliases=None):
    if out_specs is None:
        out_specs = tuple(VMEM for _ in outs) if isinstance(outs, tuple) else VMEM
    return pl.pallas_call(
        body,
        out_shape=outs,
        in_specs=specs,
        out_specs=out_specs,
        scratch_shapes=list(scratch),
        input_output_aliases=aliases or {},
        compiler_params=params(room),
        cost_estimate=cost(flops, moved),
    )


def start_all(sources, targets, sems):
    copies = [pltpu.make_async_copy(a, b, sems.at[n]) for n, (a, b) in enumerate(zip(sources, targets))]
    for copy in copies:
        copy.start()
    return copies


def request_kernel(piece, cap, *refs):
    sources, msg_ref, held, sems = refs[:5], refs[5], refs[6:11], refs[11]
    for copy in start_all(sources, held, sems):
        copy.wait()
    rows_ref, slot_ref, len_ref, dest_ref, counts_ref = held
    owners = rows_ref.shape[1]
    tokens = slot_ref.shape[1]
    replicas = tokens // piece
    my_dp = lax.axis_index("dp")
    lens = len_ref[...].astype(F32)
    takes = dest_ref[...] == iota((replicas, dest_ref.shape[1]), 0)
    totals = jnp.sum(jnp.where(takes, lens, 0.0), axis=1, keepdims=True)
    token = iota((replicas, tokens), 1)
    target = iota((replicas, tokens), 0)
    place = (my_dp * piece + token - target * piece).astype(F32)
    here = (token >= target * piece) & (token < (target + 1) * piece) & (place < totals)
    valid = jnp.sum(jnp.where(here, 1.0, 0.0), axis=0, keepdims=True)
    slot = slot_ref[...]
    by_owner = jnp.where(slot // cap == iota((owners, tokens), 0), valid, 0.0).astype(BF16)
    by_slot = jnp.where(slot % cap + cap == iota((LANES, tokens), 0), 1.0, 0.0).astype(BF16)
    counts = dot_nt(by_owner, by_slot)
    old = jnp.sum(counts_ref[...].astype(F32), axis=0, keepdims=True)
    total = jnp.sum(old, axis=1, keepdims=True) + jnp.sum(valid, axis=1, keepdims=True)
    lane = iota((owners, LANES), 1)
    place = jnp.where(iota((cap, LANES), 0) == iota((cap, LANES), 1), 1.0, 0.0)
    wanted = dot_exact(jnp.transpose(rows_ref[...].astype(F32)), place)
    msg_ref[...] = (jnp.where(lane == 2 * cap, total, counts) + wanted).astype(I32)


def asked_column(cap, asked_ref, first):
    askers = asked_ref.shape[0]
    total = askers * cap
    spread = jnp.where(iota((total, askers), 0) // cap == iota((total, askers), 1), 1.0, 0.0)
    each = dot_exact(spread, asked_ref[...].astype(F32))
    pick = iota((total, LANES), 1) == iota((total, LANES), 0) % cap + first
    return jnp.sum(jnp.where(pick, each, 0.0), axis=1, keepdims=True)


def serve_kernel(cap, asked_ref, table_ref, served_ref):
    rows = asked_column(cap, asked_ref, 0)
    total = rows.shape[0]
    step = min(512, table_ref.shape[0])
    lane = iota((total, step), 1).astype(F32)
    acc = None
    for base in range(0, table_ref.shape[0], step):
        pick = jnp.where(rows - float(base) == lane, 1.0, 0.0).astype(BF16)
        part = dot_nn(pick, table_ref[base : base + step, :])
        acc = part if acc is None else acc + part
    served_ref[...] = acc.astype(BF16)


def counts_kernel(cap, items, asked_ref, counts_ref, new_ref, log_ref, row_ref):
    rows = asked_column(cap, asked_ref, 0)
    added = asked_column(cap, asked_ref, cap)
    total = rows.shape[0]
    lines = counts_ref.shape[0]
    line = jnp.floor(rows * (1.0 / LANES))
    lane = rows - line * LANES
    by_line = jnp.where(line == iota((total, lines), 1).astype(F32), added, 0.0).astype(BF16)
    by_lane = jnp.where(lane == iota((total, LANES), 1).astype(F32), 1.0, 0.0).astype(BF16)
    new = counts_ref[...].astype(F32) + dot_tn(by_line, by_lane)
    whole = jnp.sum(asked_ref[:, 2 * cap : 2 * cap + 1].astype(F32), axis=0, keepdims=True)
    new_ref[...] = new.astype(I32)
    log_ref[...] = jnp.log(new + 1.0) - jnp.log(whole + float(items))
    row_ref[...] = jnp.transpose(jnp.broadcast_to(rows, (total, LANES)))[0:8, :]


def take_kernel(slot_ref, fetched_ref, home_ref):
    total = fetched_ref.shape[0]
    pick = jnp.where(slot_ref[...] == iota((total, slot_ref.shape[1]), 0), 1.0, 0.0).astype(BF16)
    home_ref[...] = dot_tn(pick, fetched_ref[...]).astype(BF16)


def slot_sum_kernel(slot_ref, back_ref, sums_ref):
    total = sums_ref.shape[0]
    pick = jnp.where(slot_ref[...] == iota((total, slot_ref.shape[1]), 0), 1.0, 0.0).astype(BF16)
    sums_ref[...] = dot_nn(pick, back_ref[...]).astype(BF16)


def scatter_kernel(row_ref, got_ref, out_ref, held_ref, sems):
    parts, block, _ = held_ref.shape
    total = got_ref.shape[0]
    line = iota((block, total), 0).astype(F32)
    copies = []
    for n in range(parts):
        pick = jnp.where(row_ref[0:1, :] - float(n * block) == line, 1.0, 0.0).astype(BF16)
        held_ref[n] = dot_nn(pick, got_ref[...])
        copies += start_all(
            (held_ref.at[n],), (out_ref.at[pl.ds(n * block, block), :],), sems.at[pl.ds(n, 1)]
        )
    for copy in copies:
        copy.wait()


def segments(len_ref, dest_ref, rows):
    nhist = len_ref.shape[1]
    mine = jnp.where(dest_ref[...] == lax.axis_index("dp"), len_ref[...], 0).astype(F32)
    later = iota((nhist, nhist), 0)
    other = iota((nhist, nhist), 1)
    ends = jnp.sum(jnp.where(other <= later, mine, 0.0), axis=1, keepdims=True)
    starts = jnp.sum(jnp.where(other < later, mine, 0.0), axis=1, keepdims=True)
    place = iota((nhist, rows), 1).astype(F32)
    label = iota((nhist, rows), 0).astype(F32) + 1.0
    return jnp.sum(jnp.where((starts <= place) & (place < ends), label, 0.0), axis=0, keepdims=True)


def valid_rows(seg, rows):
    return jnp.transpose(jnp.broadcast_to(jnp.where(seg > 0.0, 1.0, 0.0), (LANES, rows)))


def masked_grad(og_ref, valid):
    wide = og_ref.shape[1] // LANES
    return (og_ref[...].astype(F32) * jnp.concatenate([valid] * wide, axis=1)).astype(BF16)


def pos_bounds(rows, count):
    return [max(1, rows // 2 ** (count - m)) for m in range(count)]


def time_bounds(count):
    return [float(4**m) for m in range(count)]


def time_gaps(time_ref, rows):
    stamp = jnp.broadcast_to(time_ref[...].astype(F32), (rows, rows))
    return jnp.transpose(stamp) - stamp


def steps_passed(value, bounds):
    total = jnp.where(value >= bounds[0], 1, 0)
    for bound in bounds[1:]:
        total = total + jnp.where(value >= bound, 1, 0)
    return total


def bias_index(seg, time_ref, rows, count):
    across = jnp.broadcast_to(seg, (rows, rows))
    down = jnp.transpose(across)
    dist = iota((rows, rows), 0) - iota((rows, rows), 1)
    near = steps_passed(dist, pos_bounds(rows, count))
    late = steps_passed(time_gaps(time_ref, rows), time_bounds(count))
    mask = (across == down) & (down > 0.0) & (dist >= 0)
    return jnp.where(mask, near * (count + 1) + late, LANES - 1)


def bias_table(pos_ref, timew_ref):
    heads, count = pos_ref.shape
    entry = iota((heads, LANES), 1)
    near = entry // (count + 1)
    late = entry - near * (count + 1)
    table = jnp.zeros((heads, LANES), F32)
    for m in range(count):
        table = table + jnp.where(near > m, pos_ref[:, m : m + 1], 0.0)
        table = table + jnp.where(late > m, timew_ref[:, m : m + 1], 0.0)
    return jnp.where(entry == LANES - 1, MASKED, table)


def look_up(table_row, index):
    rows, cols = index.shape
    spread = jnp.broadcast_to(table_row, (rows, LANES))
    return jnp.concatenate(
        [jnp.take_along_axis(spread, index[:, at : at + LANES], axis=1) for at in range(0, cols, LANES)], axis=1
    )


def norm_of(value):
    centered = value - jnp.mean(value, axis=1, keepdims=True)
    scale = lax.rsqrt(jnp.mean(centered * centered, axis=1, keepdims=True) + EPSILON)
    return centered * scale, scale


def norm_back(grad_hat, normed, scale):
    first = jnp.mean(grad_hat, axis=1, keepdims=True)
    second = jnp.mean(grad_hat * normed, axis=1, keepdims=True)
    return scale * (grad_hat - first - normed * second)


def sigmoid(value):
    return 0.5 * jnp.tanh(0.5 * value) + 0.5


def layer_kernel(
    staged,
    x_ref,
    w_ref,
    b_ref,
    g1_ref,
    g2_ref,
    wo_ref,
    bo_ref,
    len_ref,
    dest_ref,
    time_ref,
    og_ref,
    pos_ref,
    timew_ref,
    lo_out,
    n1_ref,
    y_ref,
    go_ref,
    dh_ref,
    ds_ref,
    g2g_ref,
    msg_ref,
    h_ref,
    slope_ref,
    a_ref,
    lo_ref,
    sem,
):
    rows, width = x_ref.shape
    heads, count = pos_ref.shape
    pairs = heads // 2
    seg = segments(len_ref, dest_ref, rows)
    valid = valid_rows(seg, rows)
    go_ref[...] = masked_grad(og_ref, valid)
    dmix = dot_nt(go_ref[...], wo_ref[...])
    index = bias_index(seg, time_ref, rows, count)
    table = bias_table(pos_ref, timew_ref)
    x = x_ref[...].astype(F32)
    xhat, _ = norm_of(x)
    n1 = (xhat * g1_ref[...]).astype(BF16)
    n1_ref[...] = n1
    acts = []
    for part in range(4):
        cols = slice(part * width, (part + 1) * width)
        h = dot_nn(n1, w_ref[:, cols]) + b_ref[:, cols]
        sig = sigmoid(h)
        acts.append(h * sig)
        h_ref[:, cols] = sig * (1.0 + h * (1.0 - sig))
    u = acts[0]
    v, q, k = (a.astype(BF16) for a in acts[1:])
    lane = iota((rows, LANES), 1)
    low = lane < LANES // 2
    zero = jnp.zeros((rows, LANES), BF16)

    def half(value, parity):
        return jnp.where(low if parity == 0 else ~low, value, zero)

    def stacked(value):
        return jnp.concatenate([half(value, 0), half(value, 1)], axis=0)

    def abreast(value):
        return jnp.concatenate([value[:rows], value[rows:]], axis=1)

    outs = []
    for pair in range(pairs):
        cols = slice(pair * LANES, (pair + 1) * LANES)
        bias = jnp.concatenate([look_up(table[g : g + 1, :], index) for g in (2 * pair, 2 * pair + 1)], axis=0)
        s = dot_nt(stacked(q[:, cols]), k[:, cols]) * 0.125 + bias
        sig = sigmoid(s)
        a = (s * sig).astype(BF16)
        a_ref[pair] = a
        slope_ref[pair] = sig * (1.0 + s * (1.0 - sig))
        outs.append(dot_nn(abreast(a), stacked(v[:, cols])))
    o = jnp.concatenate(outs, axis=1)
    ohat, scale2 = norm_of(o)
    g2 = g2_ref[...]
    n2 = ohat * g2
    y = (n2 * u).astype(BF16)
    y_ref[...] = y
    branch = dot_nn(y, wo_ref[...]) + bo_ref[...]
    lo_ref[...] = (jnp.concatenate([valid] * (width // LANES), axis=1) * (x + branch)).astype(BF16)
    out_copy = pltpu.make_async_copy(lo_ref, lo_out, sem)
    out_copy.start()
    du = dmix * n2
    e2 = dmix * u
    g2g_ref[...] = jnp.sum(e2 * ohat, axis=0, keepdims=True)
    do = norm_back(e2 * g2, ohat, scale2).astype(BF16)
    dh_ref[:, 0:width] = (du * h_ref[:, 0:width]).astype(BF16)
    for pair in range(pairs):
        cols = slice(pair * LANES, (pair + 1) * LANES)
        dom = stacked(do[:, cols])
        ds = (dot_nt(dom, v[:, cols]) * slope_ref[pair]).astype(BF16)
        ds_ref[2 * pair] = ds[:rows]
        ds_ref[2 * pair + 1] = ds[rows:]
        dv = dot_tn(a_ref[pair], dom)
        dq = dot_nn(abreast(ds), stacked(k[:, cols]))
        dk = dot_tn(ds, stacked(q[:, cols]))
        for part, value in ((1, dv), (2, dq * 0.125), (3, dk * 0.125)):
            at = slice(part * width + pair * LANES, part * width + (pair + 1) * LANES)
            dh_ref[:, at] = (value * h_ref[:, at]).astype(BF16)
    if staged:
        other = 1 - lax.axis_index("table")
        half_cols = 2 * width
        msg_ref[:, 0:half_cols] = dh_ref[:, pl.ds(pl.multiple_of(other * half_cols, half_cols), half_cols)]
        msg_ref[:, half_cols : half_cols + width] = n1
        half_y = width // 2
        y_half = y_ref[:, pl.ds(pl.multiple_of(other * half_y, half_y), half_y)].astype(F32)
        y_half = y_half * jnp.concatenate([valid] * (half_y // LANES), axis=1)
        msg_ref[:, half_cols + width :] = y_half.astype(BF16)
    else:
        msg_ref[...] = jnp.zeros_like(msg_ref)
    out_copy.wait()


SMALL_ROWS = 48


def prefix_ends(time_ref, rows, count):
    time_lane = 64
    row = iota((1, rows), 1).astype(F32)
    ends = [row - float(bound) for bound in pos_bounds(rows, count)]
    ends += [jnp.full((time_lane - count, rows), -1.0, F32)]
    stamp = jnp.broadcast_to(time_ref[...].astype(F32), (rows, rows))
    gaps = stamp - jnp.transpose(stamp)
    for bound in time_bounds(count):
        ends.append(jnp.sum(jnp.where(gaps >= bound, 1.0, 0.0), axis=0, keepdims=True) - 1.0)
    ends += [jnp.full((LANES - time_lane - count, rows), -1.0, F32)]
    return jnp.transpose(jnp.concatenate(ends, axis=0)).astype(I32)


def after_kernel(count, dh_ref, w_ref, x_ref, g1_ref, go_ref, ds_ref, time_ref, g2g_ref, *rest):
    dx_out, out_ref, dx_ref, sem = rest
    heads, rows, _ = ds_ref.shape
    xhat, scale = norm_of(x_ref[...].astype(F32))
    dn1 = dot_nt(dh_ref[...], w_ref[...])
    go = go_ref[...].astype(F32)
    dx_ref[...] = (norm_back(dn1 * g1_ref[...], xhat, scale) + go).astype(BF16)
    copy = pltpu.make_async_copy(dx_ref, dx_out, sem)
    copy.start()
    out_ref[...] = jnp.zeros_like(out_ref)
    g1_grad = jnp.sum(dn1 * xhat, axis=0, keepdims=True)
    b_grad = jnp.sum(dh_ref[...].astype(F32), axis=0, keepdims=True)
    go_sum = jnp.sum(go, axis=0, keepdims=True)
    at = 0
    for value in (b_grad, g1_grad, g2g_ref[...], go_sum):
        for col in range(0, value.shape[1], LANES):
            out_ref[at : at + 1, :] = value[:, col : col + LANES]
            at += 1
    at = (at + 7) // 8 * 8
    ends = prefix_ends(time_ref, rows, count)
    upto = jnp.where(iota((rows, rows), 0) <= iota((rows, rows), 1), 1.0, 0.0).astype(BF16)
    prefix = dot_nn(ds_ref[...].reshape(heads * rows, rows), upto)
    tables = [
        ((ends >= first) & (ends < first + LANES), jnp.clip(ends - first, 0, LANES - 1))
        for first in range(0, rows, LANES)
    ]
    sums = []
    for g in range(heads):
        found = jnp.zeros((rows, LANES), F32)
        for n, (here, index) in enumerate(tables):
            value = prefix[g * rows : (g + 1) * rows, n * LANES : (n + 1) * LANES]
            found = found + jnp.where(here, jnp.take_along_axis(value, index, axis=1), 0.0)
        sums.append(jnp.sum(found, axis=0, keepdims=True))
    sums = jnp.concatenate(sums, axis=0)
    out_ref[at : at + heads, :] = sums
    out_ref[at + heads : at + 2 * heads, 0 : LANES // 2] = sums[:, LANES // 2 :]
    copy.wait()


def place_of(columns):
    my_dp = lax.axis_index("dp")
    return lax.rem(my_dp, columns), lax.div(my_dp, columns)


def pack_kernel(planes, columns, dh_ref, n1_ref, y_ref, go_ref, got_ref, got_grad_ref, small_ref, *rest):
    nears, fars, (uv_ref, wo_ref) = rest[:columns], rest[columns : 2 * columns], rest[2 * columns :]
    width = n1_ref.shape[1]
    core = lax.axis_index("table")
    my_xy, my_z = place_of(columns)
    half_cols = 2 * width
    half_y = width // 2
    dh = jnp.concatenate(
        [dh_ref[:, pl.ds(pl.multiple_of(core * half_cols, half_cols), half_cols)], got_ref[:, 0:half_cols]],
        axis=0,
    )
    n1 = jnp.concatenate([n1_ref[...], got_ref[:, half_cols : half_cols + width]], axis=0)
    y = jnp.concatenate(
        [y_ref[:, pl.ds(pl.multiple_of(core * half_y, half_y), half_y)], got_ref[:, half_cols + width :]],
        axis=0,
    )
    go = jnp.concatenate([go_ref[...], got_grad_ref[...]], axis=0)
    uv_ref[...] = dot_tn(n1, dh)
    wo_ref[...] = dot_tn(y, go)
    short = half_y // (planes * columns)
    for rel_xy in range(columns):
        for rel_z in range(planes):
            chunk = jnp.bitwise_xor(my_xy, rel_xy) * planes + jnp.bitwise_xor(my_z, rel_z)
            out = (nears, fars)[rel_z // 2][rel_xy].at[rel_z % 2]
            for part in range(2):
                at = pl.multiple_of((2 * chunk + part) * short, short)
                out[:, part * half_cols : (part + 1) * half_cols] = uv_ref[pl.ds(at, short), :].astype(BF16)
            at = pl.multiple_of(chunk * short, short)
            out[:, 2 * half_cols : 2 * half_cols + width] = wo_ref[pl.ds(at, short), :].astype(BF16)
            out[:, 2 * half_cols + width :] = small_ref[pl.ds(at, short), :].astype(BF16)


def unpack(planes, columns, chunks, uvqk_ref, wout_ref, small_ref, held_uvqk, held_wout, sems):
    short = held_wout.shape[1]
    width = held_wout.shape[2]
    core = lax.axis_index("table")
    my_xy, my_z = place_of(columns)
    half_cols = 2 * width
    half_y = width // 2
    wout_lanes = slice(2 * half_cols, 2 * half_cols + width)
    small_lanes = slice(2 * half_cols + width, 2 * half_cols + width + LANES)
    copies = []
    for n, (rel_xy, rel_z, whose, piece) in enumerate(chunks):
        chunk = jnp.bitwise_xor(my_xy, rel_xy) * planes + jnp.bitwise_xor(my_z, rel_z)
        side = jnp.bitwise_xor(core, whose)
        for part in range(2):
            held_uvqk[n, part * short : (part + 1) * short, :] = piece[
                :, part * half_cols : (part + 1) * half_cols
            ].astype(F32)
        held_wout[n] = piece[:, wout_lanes].astype(F32)
        tall = pl.ds(pl.multiple_of(chunk * 2 * short, 2 * short), 2 * short)
        cols = pl.ds(pl.multiple_of(side * half_cols, half_cols), half_cols)
        rows = pl.ds(pl.multiple_of(side * half_y + chunk * short, short), short)
        copies += start_all(
            (held_uvqk.at[n], held_wout.at[n]),
            (uvqk_ref.at[tall, cols], wout_ref.at[rows, :]),
            sems.at[pl.ds(2 * n, 2)],
        )
        small_ref[pl.ds(pl.multiple_of(chunk * short, short), short), :] += piece[:, small_lanes].astype(F32)
    return copies


def chunks_of(planes, first_z, pieces, whose, first_xy=0):
    return [
        (first_xy + xy, first_z + z, whose, piece.at[z])
        for xy, piece in enumerate(pieces)
        for z in range(min(2, planes - first_z))
    ]


def unpack_first_kernel(planes, columns, *refs):
    mine, theirs = refs[: columns + 1], refs[columns + 1 : 2 * columns + 2]
    uvqk_ref, wout_ref, small_ref, *scratch = refs[2 * columns + 2 :]
    small_ref[...] = jnp.zeros_like(small_ref)
    chunks = []
    for whose, pieces in enumerate((mine, theirs)):
        chunks += chunks_of(planes, 0, pieces[:columns], whose) + chunks_of(planes, 2, pieces[columns:], whose)
    for copy in unpack(planes, columns, chunks, uvqk_ref, wout_ref, small_ref, *scratch):
        copy.wait()


def unpack_next_kernel(planes, columns, *refs):
    peers = columns - 1
    mine, before_ref = refs[:peers], refs[peers + 2]
    uvqk_ref, wout_ref, small_ref, *scratch = refs[peers + 3 :]
    small_ref[...] = before_ref[...]
    chunks = chunks_of(planes, 2, mine, 0, 1)
    for copy in unpack(planes, columns, chunks, uvqk_ref, wout_ref, small_ref, *scratch):
        copy.wait()


def unpack_last_kernel(planes, columns, *refs):
    peers = columns - 1
    theirs, before_ref = refs[:peers], refs[peers + 2]
    uvqk_ref, wout_ref, *small_outs = refs[peers + 3 : peers + 11]
    small_ref, *held, small_sems = refs[peers + 11 : peers + 19]
    b_ref, g1_ref, g2_ref, bo_ref, pos_ref, time_ref = held
    scratch = refs[peers + 19 :]
    small_ref[...] = before_ref[...]
    chunks = chunks_of(planes, 2, theirs, 1, 1)
    copies = unpack(planes, columns, chunks, uvqk_ref, wout_ref, small_ref, *scratch)
    at = 0
    for out in (b_ref, g1_ref, g2_ref, bo_ref):
        for col in range(0, out.shape[1], LANES):
            out[:, col : col + LANES] = small_ref[at : at + 1, :]
            at += 1
    at = (at + 7) // 8 * 8
    heads, count = pos_ref.shape
    pos_ref[...] = small_ref[at : at + heads, 0:count]
    time_ref[...] = small_ref[at + heads : at + 2 * heads, 0:count]
    for copy in copies + start_all(held, small_outs, small_sems):
        copy.wait()


def add_up(first, *rest):
    total = first.astype(F32)
    for other in rest:
        total = total + other.astype(F32)
    return total.astype(BF16)


def xor_step(value, size, step):
    return lax.ppermute(value, "dp", [(i, i ^ step) for i in range(size)])


def reduce_step(pieces, size, stride):
    return add_up(pieces[0], *(xor_step(pieces[k], size, k * stride) for k in range(1, len(pieces))))


def gather_step(own, size, stride, peers):
    return [own] + [xor_step(own, size, k * stride) for k in range(1, peers)]


def swap_cores(value):
    return lax.ppermute(value, "table", [(0, 1), (1, 0)])


def on_device(
    item_table,
    token_request_slot,
    request_rows,
    lengths,
    assignment,
    timestamps,
    item_counts,
    first_norm_gain,
    w_uvqk,
    b_uvqk,
    norm2_gain,
    w_out,
    b_out,
    pos_weight,
    time_weight,
    out_grad,
):
    rows = token_request_slot.shape[0]
    rows_dev, width = item_table.shape
    replicas = lax.axis_size("dp")
    groups = lax.axis_size("table")
    devices = replicas * groups
    cap = request_rows.shape[2]
    piece = rows // replicas
    heads, count = pos_weight.shape
    slots = devices * cap
    columns = 4
    planes = replicas // columns
    staged = (
        groups == 2
        and replicas == 16
        and width % (32 * replicas) == 0
        and (2 * heads + SMALL_ROWS - 16) <= width // 2
    )
    mb = MIB

    slot_row = token_request_slot.reshape(1, rows)
    time_row = timestamps.reshape(1, rows)
    counts_2d = item_counts.reshape(rows_dev // LANES, LANES)
    msg = call(
        functools.partial(request_kernel, piece, cap),
        shape_of((devices, LANES), I32),
        [HBM] * 5,
        mb,
        mb // 8,
        scratch=(
            pltpu.VMEM((cap, devices), I32),
            pltpu.VMEM((1, rows), I32),
            pltpu.VMEM(lengths.shape, I32),
            pltpu.VMEM(lengths.shape, I32),
            pltpu.VMEM(counts_2d.shape, I32),
            pltpu.SemaphoreType.DMA((5,)),
        ),
        room=64,
    )(request_rows.transpose(0, 2, 1).reshape(cap, devices), slot_row, lengths, assignment, counts_2d)
    if staged:
        msg, other_grad = lax.optimization_barrier((msg, out_grad))
        got_grad = swap_cores(other_grad)
    asked = lax.all_to_all(msg.reshape(devices, 1, LANES), BOTH, 0, 0, tiled=True).reshape(devices, LANES)
    if staged:
        asked, got_grad = lax.optimization_barrier((asked, got_grad))
    served = call(
        functools.partial(serve_kernel, cap), shape_of((slots, width), BF16), [VMEM] * 2, 1 << 30, 5 * mb
    )(asked, item_table)
    fetched = lax.all_to_all(served.reshape(devices, cap, width), BOTH, 0, 0, tiled=True)
    new_counts, log_q, asked_row = call(
        functools.partial(counts_kernel, cap, rows_dev * devices),
        (
            shape_of((rows_dev // LANES, LANES), I32),
            shape_of((rows_dev // LANES, LANES), F32),
            shape_of((8, slots), F32),
        ),
        [VMEM] * 2,
        64 * mb,
        mb,
    )(asked, counts_2d)
    home = call(take_kernel, shape_of((rows, width), BF16), [VMEM] * 2, 64 * mb, mb)(
        slot_row, fetched.reshape(slots, width)
    )
    x = lax.all_to_all(home.reshape(replicas, piece, width), "dp", 0, 0, tiled=True).reshape(rows, width)

    half_cols = 2 * width
    g1, g2 = first_norm_gain.reshape(1, width), norm2_gain.reshape(1, width)
    msg_cols = half_cols + width + width // 2 if staged else LANES
    layer_out, n1, y, go, dh, ds, g2_grad, to_core = call(
        functools.partial(layer_kernel, staged),
        (
            shape_of((rows, width), BF16),
            shape_of((rows, width), BF16),
            shape_of((rows, width), BF16),
            shape_of((rows, width), BF16),
            shape_of((rows, 4 * width), BF16),
            shape_of((heads, rows, rows), BF16),
            shape_of((1, width), F32),
            shape_of((rows, msg_cols), BF16),
        ),
        [VMEM] * 13,
        2 << 30,
        8 * mb,
        scratch=(
            pltpu.VMEM((rows, 4 * width), F32),
            pltpu.VMEM((heads // 2, 2 * rows, rows), F32),
            pltpu.VMEM((heads // 2, 2 * rows, rows), BF16),
            pltpu.VMEM((rows, width), BF16),
            pltpu.SemaphoreType.DMA,
        ),
        room=24,
        out_specs=(HBM,) + (VMEM,) * 7,
    )(
        x,
        w_uvqk,
        b_uvqk.reshape(1, 4 * width),
        g1,
        g2,
        w_out,
        b_out.reshape(1, width),
        lengths,
        assignment,
        time_row,
        out_grad,
        pos_weight,
        time_weight,
    )
    def home_again(dx):
        return lax.all_to_all(dx.reshape(replicas, piece, width), "dp", 0, 0, tiled=True).reshape(rows, width)

    def to_owners(back):
        return send_sums(slot_sums(back))

    def slot_sums(back):
        return call(slot_sum_kernel, shape_of((slots, width), BF16), [VMEM] * 2, 64 * mb, mb)(slot_row, back)
    def send_sums(sums):
        sums = lax.all_to_all(sums.reshape(devices, cap, width), BOTH, 0, 0, tiled=True)
        return sums.reshape(slots, width)

    def into_table(got_sums):
        block = min(512, rows_dev)
        return call(
            scatter_kernel,
            shape_of((rows_dev, width), F32),
            [VMEM] * 2,
            1 << 30,
            8 * mb,
            scratch=(
                pltpu.VMEM((rows_dev // block, block, width), F32),
                pltpu.SemaphoreType.DMA((rows_dev // block,)),
            ),
            room=24,
            out_specs=HBM,
        )(asked_row, got_sums)

    if staged:
        got = swap_cores(to_core)
    dx, small = call(
        functools.partial(after_kernel, count),
        (shape_of((rows, width), BF16), shape_of((width // 2, LANES), F32)),
        [VMEM] * 8,
        1 << 29,
        4 * mb,
        scratch=(pltpu.VMEM((rows, width), BF16), pltpu.SemaphoreType.DMA),
        out_specs=(HBM, VMEM),
    )(dh, w_uvqk, x, g1, go, ds, time_row, g2_grad)
    if staged:
        short = width // replicas // 2
        pieces = call(
            functools.partial(pack_kernel, planes, columns),
            tuple(shape_of((2, short, 5 * width + LANES), BF16) for _ in range(2 * columns)),
            [VMEM] * 7,
            1 << 30,
            6 * mb,
            scratch=(pltpu.VMEM((width, half_cols), F32), pltpu.VMEM((width // 2, width), F32)),
        )(dh, n1, y, go, got, got_grad, small)
        dx, *pieces = lax.optimization_barrier((dx, *pieces))
        nears, fars = pieces[:columns], pieces[columns:]
        back = home_again(dx)
        got_far = [xor_step(fars[k], replicas, k) for k in range(1, columns)]
        nears, got_far[0] = lax.optimization_barrier((nears, got_far[0]))
        far_line = add_up(fars[0], *got_far)
        got_line = [xor_step(far_line[k - 2], replicas, k * columns) for k in range(2, planes)]
        near_line = reduce_step(nears, replicas, 1)
        near_line, back = lax.optimization_barrier((near_line, back))
        got_next = xor_step(near_line[1], replicas, columns)
        sums = slot_sums(back)
        own = add_up(near_line[0], got_next, *got_line)
        own, sums = lax.optimization_barrier((own, sums))
        next_own = xor_step(own, replicas, columns)
        far = [xor_step(own, replicas, k * columns) for k in range(2, planes)]
        near = jnp.stack([own, next_own])
        nears = gather_step(near, replicas, 1, columns)
        far[1], sums = lax.optimization_barrier((far[1], sums))
        got_sums = send_sums(sums)
        far = jnp.stack(far)
        table_grad = into_table(got_sums)
        fars = gather_step(far, replicas, 1, columns)
        their_nears = [swap_cores(piece) for piece in nears]
        their_far = swap_cores(far)
        small_shape = shape_of((width // 2, LANES), F32)
        wide_shapes = (shape_of((width, 4 * width), F32), shape_of((width, width), F32))

        def unpack_call(body, specs, outs, chunks, scratch=(), aliases=None, place=VMEM):
            return call(
                functools.partial(body, planes, columns),
                wide_shapes + outs,
                specs,
                mb,
                3 * mb,
                scratch=scratch
                + (
                    pltpu.VMEM((chunks, 2 * short, half_cols), F32),
                    pltpu.VMEM((chunks, short, width), F32),
                    pltpu.SemaphoreType.DMA((2 * chunks,)),
                ),
                out_specs=(HBM, HBM) + (place,) * len(outs),
                aliases=aliases,
            )

        peers = columns - 1
        wides = {peers: 0, peers + 1: 1}
        wide_specs = [VMEM] * peers + [HBM, HBM, VMEM]
        *sums_so_far, small_sum = unpack_call(
            unpack_first_kernel, [VMEM] * (2 * columns + 2), (small_shape,), 2 * (2 * columns + 2)
        )(*nears, far, *their_nears, their_far)
        fars, small_sum, table_grad = lax.optimization_barrier((fars, small_sum, table_grad))
        their_fars = [swap_cores(piece) for piece in fars[1:]]
        *sums_so_far, small_sum = unpack_call(
            unpack_next_kernel, wide_specs, (small_shape,), 2 * peers, aliases=wides
        )(*fars[1:], *sums_so_far, small_sum)
        small_outs = ((1, 4 * width),) + ((1, width),) * 3 + ((heads, count),) * 2
        w_uvqk_sum, w_out_sum, b_sum, g1_sum, g2_sum, bo_sum, pos_sum, time_sum = unpack_call(
            unpack_last_kernel,
            wide_specs,
            tuple(shape_of(shape, F32) for shape in small_outs),
            2 * peers,
            scratch=(
                pltpu.VMEM(small_shape.shape, F32),
                *(pltpu.VMEM(shape, F32) for shape in small_outs),
                pltpu.SemaphoreType.DMA((len(small_outs),)),
            ),
            aliases=wides,
            place=HBM,
        )(*their_fars, *sums_so_far, small_sum)
    else:
        table_grad = into_table(to_owners(home_again(dx)))
        w_uvqk_sum, w_out_sum, parts = lax.psum((dot_tn(n1, dh), dot_tn(y, go), small[0:SMALL_ROWS]), BOTH)
        at = 4 * width // LANES
        step = width // LANES
        b_sum = parts[0:at]
        g1_sum, g2_sum, bo_sum = (parts[at + n * step : at + (n + 1) * step] for n in range(3))
        at = (at + 3 * step + 7) // 8 * 8
        pos_sum = parts[at : at + heads, 0:count]
        time_sum = parts[at + heads : at + 2 * heads, 0:count]
    return (
        layer_out,
        table_grad,
        g1_sum.reshape(width),
        w_uvqk_sum,
        b_sum.reshape(4 * width),
        g2_sum.reshape(width),
        w_out_sum,
        bo_sum.reshape(width),
        pos_sum,
        time_sum,
        new_counts.reshape(rows_dev),
        log_q.reshape(rows_dev),
    )


def solution(mesh):
    split = P(("dp", "table"))
    rows_split = P(("dp", "table"), None)
    placed = (
        rows_split,
        split,
        P(("dp", "table"), None, None),
        P("table", None),
        P("table", None),
        split,
        split,
        P(),
        P(),
        P(),
        P(),
        P(),
        P(),
        P(),
        P(),
        rows_split,
    )
    return jax.shard_map(
        on_device,
        mesh=mesh,
        in_specs=placed,
        out_specs=(rows_split, rows_split, P(), P(), P(), P(), P(), P(), P(), P(), split, split),
        check_vma=False,
    )
```

```python
import functools

import jax
import jax.numpy as jnp
from jax import lax
from jax.experimental import pallas as pl
from jax.experimental.pallas import tpu as pltpu
from jax.sharding import PartitionSpec as P

EPSILON = 1e-05
MASKED = -1e30
F32 = jnp.float32
BF16 = jnp.bfloat16
I32 = jnp.int32
BOTH = ("dp", "table")
LANES = 128
VMEM = pl.BlockSpec(memory_space=pltpu.VMEM)
SMEM = pl.BlockSpec(memory_space=pltpu.SMEM)
HBM = pl.BlockSpec(memory_space=pltpu.HBM)
MIB = 1 << 20


def dot_nn(a, b):
    return lax.dot_general(a, b, (((1,), (0,)), ((), ())), preferred_element_type=F32)


def dot_nt(a, b):
    return lax.dot_general(a, b, (((1,), (1,)), ((), ())), preferred_element_type=F32)


def dot_tn(a, b):
    return lax.dot_general(a, b, (((0,), (0,)), ((), ())), preferred_element_type=F32)


def dot_exact(a, b):
    return lax.dot_general(
        a, b, (((1,), (0,)), ((), ())), precision=lax.Precision.HIGHEST, preferred_element_type=F32
    )


def iota(shape, dim):
    return lax.broadcasted_iota(I32, shape, dim)


def shape_of(shape, dtype):
    return jax.ShapeDtypeStruct(shape, dtype)


def cost(flops, moved):
    return pl.CostEstimate(flops=int(flops), bytes_accessed=int(moved), transcendentals=0)


def params(mib):
    return pltpu.CompilerParams(vmem_limit_bytes=mib * MIB)


def call(body, outs, specs, flops, moved, scratch=(), room=16, out_specs=None, aliases=None):
    if out_specs is None:
        out_specs = tuple(VMEM for _ in outs) if isinstance(outs, tuple) else VMEM
    return pl.pallas_call(
        body,
        out_shape=outs,
        in_specs=specs,
        out_specs=out_specs,
        scratch_shapes=list(scratch),
        input_output_aliases=aliases or {},
        compiler_params=params(room),
        cost_estimate=cost(flops, moved),
    )


def start_all(sources, targets, sems):
    copies = [pltpu.make_async_copy(a, b, sems.at[n]) for n, (a, b) in enumerate(zip(sources, targets))]
    for copy in copies:
        copy.start()
    return copies


def request_kernel(piece, cap, *refs):
    sources, msg_ref, held, sems = refs[:5], refs[5], refs[6:11], refs[11]
    for copy in start_all(sources, held, sems):
        copy.wait()
    rows_ref, slot_ref, len_ref, dest_ref, counts_ref = held
    owners = rows_ref.shape[1]
    tokens = slot_ref.shape[1]
    replicas = tokens // piece
    my_dp = lax.axis_index("dp")
    lens = len_ref[...].astype(F32)
    takes = dest_ref[...] == iota((replicas, dest_ref.shape[1]), 0)
    totals = jnp.sum(jnp.where(takes, lens, 0.0), axis=1, keepdims=True)
    token = iota((replicas, tokens), 1)
    target = iota((replicas, tokens), 0)
    place = (my_dp * piece + token - target * piece).astype(F32)
    here = (token >= target * piece) & (token < (target + 1) * piece) & (place < totals)
    valid = jnp.sum(jnp.where(here, 1.0, 0.0), axis=0, keepdims=True)
    slot = slot_ref[...]
    by_owner = jnp.where(slot // cap == iota((owners, tokens), 0), valid, 0.0).astype(BF16)
    by_slot = jnp.where(slot % cap + cap == iota((LANES, tokens), 0), 1.0, 0.0).astype(BF16)
    counts = dot_nt(by_owner, by_slot)
    old = jnp.sum(counts_ref[...].astype(F32), axis=0, keepdims=True)
    total = jnp.sum(old, axis=1, keepdims=True) + jnp.sum(valid, axis=1, keepdims=True)
    lane = iota((owners, LANES), 1)
    place = jnp.where(iota((cap, LANES), 0) == iota((cap, LANES), 1), 1.0, 0.0)
    wanted = dot_exact(jnp.transpose(rows_ref[...].astype(F32)), place)
    msg_ref[...] = (jnp.where(lane == 2 * cap, total, counts) + wanted).astype(I32)


def asked_column(cap, asked_ref, first):
    askers = asked_ref.shape[0]
    total = askers * cap
    ahead = iota((total, askers), 0) - iota((total, askers), 1) * cap
    spread = jnp.where((ahead >= 0) & (ahead < cap), 1.0, 0.0).astype(BF16)
    asked = asked_ref[...].astype(F32)
    high = jnp.floor(asked * (1.0 / LANES))
    low = asked - high * LANES
    each = dot_nn(spread, high.astype(BF16)) * LANES + dot_nn(spread, low.astype(BF16))
    pick = iota((total, LANES), 1) == iota((total, LANES), 0) % cap + first
    return jnp.sum(jnp.where(pick, each, 0.0), axis=1, keepdims=True)


def serve_kernel(cap, asked_ref, table_ref, served_ref):
    rows = asked_column(cap, asked_ref, 0)
    total = rows.shape[0]
    step = min(256, table_ref.shape[0])
    lane = iota((total, step), 1).astype(F32)
    acc = None
    for base in range(0, table_ref.shape[0], step):
        pick = jnp.where(rows - float(base) == lane, 1.0, 0.0).astype(BF16)
        part = dot_nn(pick, table_ref[base : base + step, :])
        acc = part if acc is None else acc + part
    served_ref[...] = acc.astype(BF16)


def counts_kernel(cap, items, asked_ref, counts_ref, new_ref, log_ref, row_ref):
    rows = asked_column(cap, asked_ref, 0)
    added = asked_column(cap, asked_ref, cap)
    total = rows.shape[0]
    lines = counts_ref.shape[0]
    line = jnp.floor(rows * (1.0 / LANES))
    lane = rows - line * LANES
    by_line = jnp.where(line == iota((total, lines), 1).astype(F32), added, 0.0).astype(BF16)
    by_lane = jnp.where(lane == iota((total, LANES), 1).astype(F32), 1.0, 0.0).astype(BF16)
    new = counts_ref[...].astype(F32) + dot_tn(by_line, by_lane)
    whole = jnp.sum(asked_ref[:, 2 * cap : 2 * cap + 1].astype(F32), axis=0, keepdims=True)
    new_ref[...] = new.astype(I32)
    log_ref[...] = jnp.log(new + 1.0) - jnp.log(whole + float(items))
    row_ref[...] = jnp.transpose(jnp.broadcast_to(rows, (total, LANES)))[0:8, :]


def take_kernel(slot_ref, fetched_ref, home_ref):
    total = fetched_ref.shape[0]
    pick = jnp.where(slot_ref[...] == iota((total, slot_ref.shape[1]), 0), 1.0, 0.0).astype(BF16)
    home_ref[...] = dot_tn(pick, fetched_ref[...]).astype(BF16)


def slot_sum_kernel(slot_ref, back_ref, sums_ref):
    total = sums_ref.shape[0]
    pick = jnp.where(slot_ref[...] == iota((total, slot_ref.shape[1]), 0), 1.0, 0.0).astype(BF16)
    sums_ref[...] = dot_nn(pick, back_ref[...]).astype(BF16)


def scatter_kernel(row_ref, got_ref, out_ref, held_ref, sems):
    parts, block, _ = held_ref.shape
    total = got_ref.shape[0]
    line = iota((block, total), 0).astype(F32)
    copies = []
    for n in range(parts):
        pick = jnp.where(row_ref[0:1, :] - float(n * block) == line, 1.0, 0.0).astype(BF16)
        held_ref[n] = dot_nn(pick, got_ref[...])
        copies += start_all(
            (held_ref.at[n],), (out_ref.at[pl.ds(n * block, block), :],), sems.at[pl.ds(n, 1)]
        )
    for copy in copies:
        copy.wait()


def segments(len_ref, dest_ref, rows):
    nhist = len_ref.shape[1]
    mine = jnp.where(dest_ref[...] == lax.axis_index("dp"), len_ref[...], 0).astype(F32)
    later = iota((nhist, nhist), 0)
    other = iota((nhist, nhist), 1)
    ends = jnp.sum(jnp.where(other <= later, mine, 0.0), axis=1, keepdims=True)
    starts = jnp.sum(jnp.where(other < later, mine, 0.0), axis=1, keepdims=True)
    place = iota((nhist, rows), 1).astype(F32)
    label = iota((nhist, rows), 0).astype(F32) + 1.0
    return jnp.sum(jnp.where((starts <= place) & (place < ends), label, 0.0), axis=0, keepdims=True)


def valid_rows(seg, rows):
    return jnp.transpose(jnp.broadcast_to(jnp.where(seg > 0.0, 1.0, 0.0), (LANES, rows)))


def masked_grad(og_ref, valid):
    wide = og_ref.shape[1] // LANES
    return (og_ref[...].astype(F32) * jnp.concatenate([valid] * wide, axis=1)).astype(BF16)


def pos_bounds(rows, count):
    return [max(1, rows // 2 ** (count - m)) for m in range(count)]


def time_bounds(count):
    return [float(4**m) for m in range(count)]


def time_gaps(time_ref, rows):
    stamp = jnp.broadcast_to(time_ref[...].astype(F32), (rows, rows))
    return jnp.transpose(stamp) - stamp


def steps_passed(value, bounds):
    total = jnp.where(value >= bounds[0], 1, 0)
    for bound in bounds[1:]:
        total = total + jnp.where(value >= bound, 1, 0)
    return total


def bias_index(seg, time_ref, rows, count):
    across = jnp.broadcast_to(seg, (rows, rows))
    down = jnp.transpose(across)
    dist = iota((rows, rows), 0) - iota((rows, rows), 1)
    near = steps_passed(dist, pos_bounds(rows, count))
    late = steps_passed(time_gaps(time_ref, rows), time_bounds(count))
    mask = (across == down) & (down > 0.0) & (dist >= 0)
    return jnp.where(mask, near * (count + 1) + late, LANES - 1)


def bias_table(pos_ref, timew_ref):
    heads, count = pos_ref.shape
    entry = iota((heads, LANES), 1)
    near = entry // (count + 1)
    late = entry - near * (count + 1)
    table = jnp.zeros((heads, LANES), F32)
    for m in range(count):
        table = table + jnp.where(near > m, pos_ref[:, m : m + 1], 0.0)
        table = table + jnp.where(late > m, timew_ref[:, m : m + 1], 0.0)
    return jnp.where(entry == LANES - 1, MASKED, table)


def look_up(table_row, index):
    rows, cols = index.shape
    spread = jnp.broadcast_to(table_row, (rows, LANES))
    return jnp.concatenate(
        [jnp.take_along_axis(spread, index[:, at : at + LANES], axis=1) for at in range(0, cols, LANES)], axis=1
    )


def norm_of(value):
    centered = value - jnp.mean(value, axis=1, keepdims=True)
    scale = lax.rsqrt(jnp.mean(centered * centered, axis=1, keepdims=True) + EPSILON)
    return centered * scale, scale


def norm_back(grad_hat, normed, scale):
    first = jnp.mean(grad_hat, axis=1, keepdims=True)
    second = jnp.mean(grad_hat * normed, axis=1, keepdims=True)
    return scale * (grad_hat - first - normed * second)


def sigmoid(value):
    return 0.5 * jnp.tanh(0.5 * value) + 0.5


def layer_kernel(
    staged,
    x_ref,
    w_ref,
    b_ref,
    g1_ref,
    g2_ref,
    wo_ref,
    bo_ref,
    len_ref,
    dest_ref,
    time_ref,
    og_ref,
    pos_ref,
    timew_ref,
    lo_out,
    n1_ref,
    y_ref,
    go_ref,
    dh_ref,
    ds_ref,
    g2g_ref,
    msg_ref,
    h_ref,
    slope_ref,
    a_ref,
    lo_ref,
    sem,
):
    rows, width = x_ref.shape
    heads, count = pos_ref.shape
    pairs = heads // 2
    seg = segments(len_ref, dest_ref, rows)
    valid = valid_rows(seg, rows)
    go_ref[...] = masked_grad(og_ref, valid)
    dmix = dot_nt(go_ref[...], wo_ref[...])
    index = bias_index(seg, time_ref, rows, count)
    table = bias_table(pos_ref, timew_ref)
    x = x_ref[...].astype(F32)
    xhat, _ = norm_of(x)
    n1 = (xhat * g1_ref[...]).astype(BF16)
    n1_ref[...] = n1
    acts = []
    for part in range(4):
        cols = slice(part * width, (part + 1) * width)
        h = dot_nn(n1, w_ref[:, cols]) + b_ref[:, cols]
        sig = sigmoid(h)
        acts.append(h * sig)
        h_ref[:, cols] = sig * (1.0 + h * (1.0 - sig))
    u = acts[0]
    v, q, k = (a.astype(BF16) for a in acts[1:])
    lane = iota((rows, LANES), 1)
    low = lane < LANES // 2
    zero = jnp.zeros((rows, LANES), BF16)

    def half(value, parity):
        return jnp.where(low if parity == 0 else ~low, value, zero)

    def stacked(value):
        return jnp.concatenate([half(value, 0), half(value, 1)], axis=0)

    def abreast(value):
        return jnp.concatenate([value[:rows], value[rows:]], axis=1)

    outs = []
    for pair in range(pairs):
        cols = slice(pair * LANES, (pair + 1) * LANES)
        bias = jnp.concatenate([look_up(table[g : g + 1, :], index) for g in (2 * pair, 2 * pair + 1)], axis=0)
        s = dot_nt(stacked(q[:, cols]), k[:, cols]) * 0.125 + bias
        sig = sigmoid(s)
        a = (s * sig).astype(BF16)
        a_ref[pair] = a
        slope_ref[pair] = sig * (1.0 + s * (1.0 - sig))
        outs.append(dot_nn(abreast(a), stacked(v[:, cols])))
    o = jnp.concatenate(outs, axis=1)
    ohat, scale2 = norm_of(o)
    g2 = g2_ref[...]
    n2 = ohat * g2
    y = (n2 * u).astype(BF16)
    y_ref[...] = y
    branch = dot_nn(y, wo_ref[...]) + bo_ref[...]
    lo_ref[...] = (jnp.concatenate([valid] * (width // LANES), axis=1) * (x + branch)).astype(BF16)
    out_copy = pltpu.make_async_copy(lo_ref, lo_out, sem)
    out_copy.start()
    du = dmix * n2
    e2 = dmix * u
    g2g_ref[...] = jnp.sum(e2 * ohat, axis=0, keepdims=True)
    do = norm_back(e2 * g2, ohat, scale2).astype(BF16)
    dh_ref[:, 0:width] = (du * h_ref[:, 0:width]).astype(BF16)
    for pair in range(pairs):
        cols = slice(pair * LANES, (pair + 1) * LANES)
        dom = stacked(do[:, cols])
        ds = (dot_nt(dom, v[:, cols]) * slope_ref[pair]).astype(BF16)
        ds_ref[2 * pair] = ds[:rows]
        ds_ref[2 * pair + 1] = ds[rows:]
        dv = dot_tn(a_ref[pair], dom)
        dq = dot_nn(abreast(ds), stacked(k[:, cols]))
        dk = dot_tn(ds, stacked(q[:, cols]))
        for part, value in ((1, dv), (2, dq * 0.125), (3, dk * 0.125)):
            at = slice(part * width + pair * LANES, part * width + (pair + 1) * LANES)
            dh_ref[:, at] = (value * h_ref[:, at]).astype(BF16)
    if staged:
        other = 1 - lax.axis_index("table")
        half_cols = 2 * width
        msg_ref[:, 0:half_cols] = dh_ref[:, pl.ds(pl.multiple_of(other * half_cols, half_cols), half_cols)]
        msg_ref[:, half_cols : half_cols + width] = n1
        half_y = width // 2
        y_half = y_ref[:, pl.ds(pl.multiple_of(other * half_y, half_y), half_y)].astype(F32)
        y_half = y_half * jnp.concatenate([valid] * (half_y // LANES), axis=1)
        msg_ref[:, half_cols + width :] = y_half.astype(BF16)
    else:
        msg_ref[...] = jnp.zeros_like(msg_ref)
    out_copy.wait()


SMALL_ROWS = 48


def prefix_ends(time_ref, rows, count):
    time_lane = 64
    row = iota((1, rows), 1).astype(F32)
    ends = [row - float(bound) for bound in pos_bounds(rows, count)]
    ends += [jnp.full((time_lane - count, rows), -1.0, F32)]
    stamp = jnp.broadcast_to(time_ref[...].astype(F32), (rows, rows))
    gaps = stamp - jnp.transpose(stamp)
    for bound in time_bounds(count):
        ends.append(jnp.sum(jnp.where(gaps >= bound, 1.0, 0.0), axis=0, keepdims=True) - 1.0)
    ends += [jnp.full((LANES - time_lane - count, rows), -1.0, F32)]
    return jnp.transpose(jnp.concatenate(ends, axis=0)).astype(I32)


def after_kernel(count, dh_ref, w_ref, x_ref, g1_ref, go_ref, ds_ref, time_ref, g2g_ref, *rest):
    dx_out, out_ref, dx_ref, sem = rest
    heads, rows, _ = ds_ref.shape
    xhat, scale = norm_of(x_ref[...].astype(F32))
    dn1 = dot_nt(dh_ref[...], w_ref[...])
    go = go_ref[...].astype(F32)
    dx_ref[...] = (norm_back(dn1 * g1_ref[...], xhat, scale) + go).astype(BF16)
    copy = pltpu.make_async_copy(dx_ref, dx_out, sem)
    copy.start()
    out_ref[...] = jnp.zeros_like(out_ref)
    g1_grad = jnp.sum(dn1 * xhat, axis=0, keepdims=True)
    b_grad = jnp.sum(dh_ref[...].astype(F32), axis=0, keepdims=True)
    go_sum = jnp.sum(go, axis=0, keepdims=True)
    at = 0
    for value in (b_grad, g1_grad, g2g_ref[...], go_sum):
        for col in range(0, value.shape[1], LANES):
            out_ref[at : at + 1, :] = value[:, col : col + LANES]
            at += 1
    at = (at + 7) // 8 * 8
    ends = prefix_ends(time_ref, rows, count)
    upto = jnp.where(iota((rows, rows), 0) <= iota((rows, rows), 1), 1.0, 0.0).astype(BF16)
    prefix = dot_nn(ds_ref[...].reshape(heads * rows, rows), upto)
    tables = [
        ((ends >= first) & (ends < first + LANES), jnp.clip(ends - first, 0, LANES - 1))
        for first in range(0, rows, LANES)
    ]
    sums = []
    for g in range(heads):
        found = jnp.zeros((rows, LANES), F32)
        for n, (here, index) in enumerate(tables):
            value = prefix[g * rows : (g + 1) * rows, n * LANES : (n + 1) * LANES]
            found = found + jnp.where(here, jnp.take_along_axis(value, index, axis=1), 0.0)
        sums.append(jnp.sum(found, axis=0, keepdims=True))
    sums = jnp.concatenate(sums, axis=0)
    out_ref[at : at + heads, :] = sums
    out_ref[at + heads : at + 2 * heads, 0 : LANES // 2] = sums[:, LANES // 2 :]
    copy.wait()


def place_of(columns):
    my_dp = lax.axis_index("dp")
    return lax.rem(my_dp, columns), lax.div(my_dp, columns)


def pack_kernel(planes, columns, dh_ref, n1_ref, y_ref, go_ref, got_ref, got_grad_ref, small_ref, *rest):
    nears, fars, (uv_ref, wo_ref) = rest[:columns], rest[columns : 2 * columns], rest[2 * columns :]
    width = n1_ref.shape[1]
    core = lax.axis_index("table")
    my_xy, my_z = place_of(columns)
    half_cols = 2 * width
    half_y = width // 2
    dh = jnp.concatenate(
        [dh_ref[:, pl.ds(pl.multiple_of(core * half_cols, half_cols), half_cols)], got_ref[:, 0:half_cols]],
        axis=0,
    )
    n1 = jnp.concatenate([n1_ref[...], got_ref[:, half_cols : half_cols + width]], axis=0)
    y = jnp.concatenate(
        [y_ref[:, pl.ds(pl.multiple_of(core * half_y, half_y), half_y)], got_ref[:, half_cols + width :]],
        axis=0,
    )
    go = jnp.concatenate([go_ref[...], got_grad_ref[...]], axis=0)
    uv_ref[...] = dot_tn(n1, dh)
    wo_ref[...] = dot_tn(y, go)
    short = half_y // (planes * columns)
    for rel_xy in range(columns):
        for rel_z in range(planes):
            chunk = jnp.bitwise_xor(my_xy, rel_xy) * planes + jnp.bitwise_xor(my_z, rel_z)
            out = (nears, fars)[rel_z // 2][rel_xy].at[rel_z % 2]
            for part in range(2):
                at = pl.multiple_of((2 * chunk + part) * short, short)
                out[:, part * half_cols : (part + 1) * half_cols] = uv_ref[pl.ds(at, short), :].astype(BF16)
            at = pl.multiple_of(chunk * short, short)
            out[:, 2 * half_cols : 2 * half_cols + width] = wo_ref[pl.ds(at, short), :].astype(BF16)
            out[:, 2 * half_cols + width :] = small_ref[pl.ds(at, short), :].astype(BF16)


def unpack(planes, columns, chunks, uvqk_ref, wout_ref, small_ref, held_uvqk, held_wout, sems):
    short = held_wout.shape[1]
    width = held_wout.shape[2]
    core = lax.axis_index("table")
    my_xy, my_z = place_of(columns)
    half_cols = 2 * width
    half_y = width // 2
    wout_lanes = slice(2 * half_cols, 2 * half_cols + width)
    small_lanes = slice(2 * half_cols + width, 2 * half_cols + width + LANES)
    copies = []
    for n, (rel_xy, rel_z, whose, piece) in enumerate(chunks):
        chunk = jnp.bitwise_xor(my_xy, rel_xy) * planes + jnp.bitwise_xor(my_z, rel_z)
        side = jnp.bitwise_xor(core, whose)
        for part in range(2):
            held_uvqk[n, part * short : (part + 1) * short, :] = piece[
                :, part * half_cols : (part + 1) * half_cols
            ].astype(F32)
        held_wout[n] = piece[:, wout_lanes].astype(F32)
        tall = pl.ds(pl.multiple_of(chunk * 2 * short, 2 * short), 2 * short)
        cols = pl.ds(pl.multiple_of(side * half_cols, half_cols), half_cols)
        rows = pl.ds(pl.multiple_of(side * half_y + chunk * short, short), short)
        copies += start_all(
            (held_uvqk.at[n], held_wout.at[n]),
            (uvqk_ref.at[tall, cols], wout_ref.at[rows, :]),
            sems.at[pl.ds(2 * n, 2)],
        )
        small_ref[pl.ds(pl.multiple_of(chunk * short, short), short), :] += piece[:, small_lanes].astype(F32)
    return copies


def chunks_of(planes, first_z, pieces, whose, first_xy=0):
    return [
        (first_xy + xy, first_z + z, whose, piece.at[z])
        for xy, piece in enumerate(pieces)
        for z in range(min(2, planes - first_z))
    ]


def unpack_first_kernel(planes, columns, *refs):
    mine, theirs = refs[: columns + 1], refs[columns + 1 : 2 * columns + 2]
    uvqk_ref, wout_ref, small_ref, *scratch = refs[2 * columns + 2 :]
    small_ref[...] = jnp.zeros_like(small_ref)
    chunks = []
    for whose, pieces in enumerate((mine, theirs)):
        chunks += chunks_of(planes, 0, pieces[:columns], whose) + chunks_of(planes, 2, pieces[columns:], whose)
    for copy in unpack(planes, columns, chunks, uvqk_ref, wout_ref, small_ref, *scratch):
        copy.wait()


def unpack_next_kernel(planes, columns, *refs):
    peers = columns - 1
    mine, before_ref = refs[:peers], refs[peers + 2]
    uvqk_ref, wout_ref, small_ref, *scratch = refs[peers + 3 :]
    small_ref[...] = before_ref[...]
    chunks = chunks_of(planes, 2, mine, 0, 1)
    for copy in unpack(planes, columns, chunks, uvqk_ref, wout_ref, small_ref, *scratch):
        copy.wait()


def unpack_last_kernel(planes, columns, *refs):
    peers = columns - 1
    theirs, before_ref = refs[:peers], refs[peers + 2]
    uvqk_ref, wout_ref, *small_outs = refs[peers + 3 : peers + 11]
    small_ref, *held, small_sems = refs[peers + 11 : peers + 19]
    b_ref, g1_ref, g2_ref, bo_ref, pos_ref, time_ref = held
    scratch = refs[peers + 19 :]
    small_ref[...] = before_ref[...]
    chunks = chunks_of(planes, 2, theirs, 1, 1)
    copies = unpack(planes, columns, chunks, uvqk_ref, wout_ref, small_ref, *scratch)
    at = 0
    for out in (b_ref, g1_ref, g2_ref, bo_ref):
        for col in range(0, out.shape[1], LANES):
            out[:, col : col + LANES] = small_ref[at : at + 1, :]
            at += 1
    at = (at + 7) // 8 * 8
    heads, count = pos_ref.shape
    pos_ref[...] = small_ref[at : at + heads, 0:count]
    time_ref[...] = small_ref[at + heads : at + 2 * heads, 0:count]
    for copy in copies + start_all(held, small_outs, small_sems):
        copy.wait()


def add_up(first, *rest):
    total = first.astype(F32)
    for other in rest:
        total = total + other.astype(F32)
    return total.astype(BF16)


def xor_step(value, size, step):
    return lax.ppermute(value, "dp", [(i, i ^ step) for i in range(size)])


def reduce_step(pieces, size, stride):
    return add_up(pieces[0], *(xor_step(pieces[k], size, k * stride) for k in range(1, len(pieces))))


def gather_step(own, size, stride, peers):
    return [own] + [xor_step(own, size, k * stride) for k in range(1, peers)]


def swap_cores(value):
    return lax.ppermute(value, "table", [(0, 1), (1, 0)])


def on_device(
    item_table,
    token_request_slot,
    request_rows,
    lengths,
    assignment,
    timestamps,
    item_counts,
    first_norm_gain,
    w_uvqk,
    b_uvqk,
    norm2_gain,
    w_out,
    b_out,
    pos_weight,
    time_weight,
    out_grad,
):
    rows = token_request_slot.shape[0]
    rows_dev, width = item_table.shape
    replicas = lax.axis_size("dp")
    groups = lax.axis_size("table")
    devices = replicas * groups
    cap = request_rows.shape[2]
    piece = rows // replicas
    heads, count = pos_weight.shape
    slots = devices * cap
    columns = 4
    planes = replicas // columns
    staged = (
        groups == 2
        and replicas == 16
        and width % (32 * replicas) == 0
        and (2 * heads + SMALL_ROWS - 16) <= width // 2
    )
    mb = MIB

    slot_row = token_request_slot.reshape(1, rows)
    time_row = timestamps.reshape(1, rows)
    counts_2d = item_counts.reshape(rows_dev // LANES, LANES)
    msg = call(
        functools.partial(request_kernel, piece, cap),
        shape_of((devices, LANES), I32),
        [HBM] * 5,
        mb,
        mb // 8,
        scratch=(
            pltpu.VMEM((cap, devices), I32),
            pltpu.VMEM((1, rows), I32),
            pltpu.VMEM(lengths.shape, I32),
            pltpu.VMEM(lengths.shape, I32),
            pltpu.VMEM(counts_2d.shape, I32),
            pltpu.SemaphoreType.DMA((5,)),
        ),
        room=64,
    )(request_rows.transpose(0, 2, 1).reshape(cap, devices), slot_row, lengths, assignment, counts_2d)
    if staged:
        msg, other_grad = lax.optimization_barrier((msg, out_grad))
        got_grad = swap_cores(other_grad)
    asked = lax.all_to_all(msg.reshape(devices, 1, LANES), BOTH, 0, 0, tiled=True).reshape(devices, LANES)
    if staged:
        asked, got_grad = lax.optimization_barrier((asked, got_grad))
    served = call(
        functools.partial(serve_kernel, cap), shape_of((slots, width), BF16), [VMEM] * 2, 1 << 30, 5 * mb
    )(asked, item_table)
    fetched = lax.all_to_all(served.reshape(devices, cap, width), BOTH, 0, 0, tiled=True)
    new_counts, log_q, asked_row = call(
        functools.partial(counts_kernel, cap, rows_dev * devices),
        (
            shape_of((rows_dev // LANES, LANES), I32),
            shape_of((rows_dev // LANES, LANES), F32),
            shape_of((8, slots), F32),
        ),
        [VMEM] * 2,
        64 * mb,
        mb,
    )(asked, counts_2d)
    home = call(take_kernel, shape_of((rows, width), BF16), [VMEM] * 2, 64 * mb, mb)(
        slot_row, fetched.reshape(slots, width)
    )
    x = lax.all_to_all(home.reshape(replicas, piece, width), "dp", 0, 0, tiled=True).reshape(rows, width)

    half_cols = 2 * width
    g1, g2 = first_norm_gain.reshape(1, width), norm2_gain.reshape(1, width)
    msg_cols = half_cols + width + width // 2 if staged else LANES
    layer_out, n1, y, go, dh, ds, g2_grad, to_core = call(
        functools.partial(layer_kernel, staged),
        (
            shape_of((rows, width), BF16),
            shape_of((rows, width), BF16),
            shape_of((rows, width), BF16),
            shape_of((rows, width), BF16),
            shape_of((rows, 4 * width), BF16),
            shape_of((heads, rows, rows), BF16),
            shape_of((1, width), F32),
            shape_of((rows, msg_cols), BF16),
        ),
        [VMEM] * 13,
        2 << 30,
        8 * mb,
        scratch=(
            pltpu.VMEM((rows, 4 * width), F32),
            pltpu.VMEM((heads // 2, 2 * rows, rows), F32),
            pltpu.VMEM((heads // 2, 2 * rows, rows), BF16),
            pltpu.VMEM((rows, width), BF16),
            pltpu.SemaphoreType.DMA,
        ),
        room=24,
        out_specs=(HBM,) + (VMEM,) * 7,
    )(
        x,
        w_uvqk,
        b_uvqk.reshape(1, 4 * width),
        g1,
        g2,
        w_out,
        b_out.reshape(1, width),
        lengths,
        assignment,
        time_row,
        out_grad,
        pos_weight,
        time_weight,
    )
    def home_again(dx):
        return lax.all_to_all(dx.reshape(replicas, piece, width), "dp", 0, 0, tiled=True).reshape(rows, width)

    def to_owners(back):
        return send_sums(slot_sums(back))

    def slot_sums(back):
        return call(slot_sum_kernel, shape_of((slots, width), BF16), [VMEM] * 2, 64 * mb, mb)(slot_row, back)
    def send_sums(sums):
        sums = lax.all_to_all(sums.reshape(devices, cap, width), BOTH, 0, 0, tiled=True)
        return sums.reshape(slots, width)

    def into_table(got_sums):
        block = min(512, rows_dev)
        return call(
            scatter_kernel,
            shape_of((rows_dev, width), F32),
            [VMEM] * 2,
            1 << 30,
            8 * mb,
            scratch=(
                pltpu.VMEM((rows_dev // block, block, width), F32),
                pltpu.SemaphoreType.DMA((rows_dev // block,)),
            ),
            room=24,
            out_specs=HBM,
        )(asked_row, got_sums)

    if staged:
        got = swap_cores(to_core)
    dx, small = call(
        functools.partial(after_kernel, count),
        (shape_of((rows, width), BF16), shape_of((width // 2, LANES), F32)),
        [VMEM] * 8,
        1 << 29,
        4 * mb,
        scratch=(pltpu.VMEM((rows, width), BF16), pltpu.SemaphoreType.DMA),
        out_specs=(HBM, VMEM),
    )(dh, w_uvqk, x, g1, go, ds, time_row, g2_grad)
    if staged:
        short = width // replicas // 2
        pieces = call(
            functools.partial(pack_kernel, planes, columns),
            tuple(shape_of((2, short, 5 * width + LANES), BF16) for _ in range(2 * columns)),
            [VMEM] * 7,
            1 << 30,
            6 * mb,
            scratch=(pltpu.VMEM((width, half_cols), F32), pltpu.VMEM((width // 2, width), F32)),
        )(dh, n1, y, go, got, got_grad, small)
        dx, *pieces = lax.optimization_barrier((dx, *pieces))
        nears, fars = pieces[:columns], pieces[columns:]
        back = home_again(dx)
        got_far = [xor_step(fars[k], replicas, k) for k in range(1, columns)]
        nears, got_far[0] = lax.optimization_barrier((nears, got_far[0]))
        far_line = add_up(fars[0], *got_far)
        got_line = [xor_step(far_line[k - 2], replicas, k * columns) for k in range(2, planes)]
        near_line = reduce_step(nears, replicas, 1)
        near_line, back = lax.optimization_barrier((near_line, back))
        got_next = xor_step(near_line[1], replicas, columns)
        sums = slot_sums(back)
        own = add_up(near_line[0], got_next, *got_line)
        own, sums = lax.optimization_barrier((own, sums))
        next_own = xor_step(own, replicas, columns)
        far = [xor_step(own, replicas, k * columns) for k in range(2, planes)]
        near = jnp.stack([own, next_own])
        nears = gather_step(near, replicas, 1, columns)
        far[1], sums = lax.optimization_barrier((far[1], sums))
        got_sums = send_sums(sums)
        far = jnp.stack(far)
        table_grad = into_table(got_sums)
        fars = gather_step(far, replicas, 1, columns)
        their_nears = [swap_cores(piece) for piece in nears]
        their_far = swap_cores(far)
        small_shape = shape_of((width // 2, LANES), F32)
        wide_shapes = (shape_of((width, 4 * width), F32), shape_of((width, width), F32))

        def unpack_call(body, specs, outs, chunks, scratch=(), aliases=None, place=VMEM):
            return call(
                functools.partial(body, planes, columns),
                wide_shapes + outs,
                specs,
                mb,
                3 * mb,
                scratch=scratch
                + (
                    pltpu.VMEM((chunks, 2 * short, half_cols), F32),
                    pltpu.VMEM((chunks, short, width), F32),
                    pltpu.SemaphoreType.DMA((2 * chunks,)),
                ),
                out_specs=(HBM, HBM) + (place,) * len(outs),
                aliases=aliases,
            )

        peers = columns - 1
        wides = {peers: 0, peers + 1: 1}
        wide_specs = [VMEM] * peers + [HBM, HBM, VMEM]
        *sums_so_far, small_sum = unpack_call(
            unpack_first_kernel, [VMEM] * (2 * columns + 2), (small_shape,), 2 * (2 * columns + 2)
        )(*nears, far, *their_nears, their_far)
        fars, small_sum, table_grad = lax.optimization_barrier((fars, small_sum, table_grad))
        their_fars = [swap_cores(piece) for piece in fars[1:]]
        *sums_so_far, small_sum = unpack_call(
            unpack_next_kernel, wide_specs, (small_shape,), 2 * peers, aliases=wides
        )(*fars[1:], *sums_so_far, small_sum)
        small_outs = ((1, 4 * width),) + ((1, width),) * 3 + ((heads, count),) * 2
        w_uvqk_sum, w_out_sum, b_sum, g1_sum, g2_sum, bo_sum, pos_sum, time_sum = unpack_call(
            unpack_last_kernel,
            wide_specs,
            tuple(shape_of(shape, F32) for shape in small_outs),
            2 * peers,
            scratch=(
                pltpu.VMEM(small_shape.shape, F32),
                *(pltpu.VMEM(shape, F32) for shape in small_outs),
                pltpu.SemaphoreType.DMA((len(small_outs),)),
            ),
            aliases=wides,
            place=HBM,
        )(*their_fars, *sums_so_far, small_sum)
    else:
        table_grad = into_table(to_owners(home_again(dx)))
        w_uvqk_sum, w_out_sum, parts = lax.psum((dot_tn(n1, dh), dot_tn(y, go), small[0:SMALL_ROWS]), BOTH)
        at = 4 * width // LANES
        step = width // LANES
        b_sum = parts[0:at]
        g1_sum, g2_sum, bo_sum = (parts[at + n * step : at + (n + 1) * step] for n in range(3))
        at = (at + 3 * step + 7) // 8 * 8
        pos_sum = parts[at : at + heads, 0:count]
        time_sum = parts[at + heads : at + 2 * heads, 0:count]
    return (
        layer_out,
        table_grad,
        g1_sum.reshape(width),
        w_uvqk_sum,
        b_sum.reshape(4 * width),
        g2_sum.reshape(width),
        w_out_sum,
        bo_sum.reshape(width),
        pos_sum,
        time_sum,
        new_counts.reshape(rows_dev),
        log_q.reshape(rows_dev),
    )


def solution(mesh):
    split = P(("dp", "table"))
    rows_split = P(("dp", "table"), None)
    placed = (
        rows_split,
        split,
        P(("dp", "table"), None, None),
        P("table", None),
        P("table", None),
        split,
        split,
        P(),
        P(),
        P(),
        P(),
        P(),
        P(),
        P(),
        P(),
        rows_split,
    )
    return jax.shard_map(
        on_device,
        mesh=mesh,
        in_specs=placed,
        out_specs=(rows_split, rows_split, P(), P(), P(), P(), P(), P(), P(), P(), split, split),
        check_vma=False,
    )
```

```python
import functools

import jax
import jax.numpy as jnp
from jax import lax
from jax.experimental import pallas as pl
from jax.experimental.pallas import tpu as pltpu
from jax.sharding import PartitionSpec as P

EPSILON = 1e-05
MASKED = -1e30
F32 = jnp.float32
BF16 = jnp.bfloat16
I32 = jnp.int32
BOTH = ("dp", "table")
LANES = 128
VMEM = pl.BlockSpec(memory_space=pltpu.VMEM)
SMEM = pl.BlockSpec(memory_space=pltpu.SMEM)
HBM = pl.BlockSpec(memory_space=pltpu.HBM)
MIB = 1 << 20


def dot_nn(a, b):
    return lax.dot_general(a, b, (((1,), (0,)), ((), ())), preferred_element_type=F32)


def dot_nt(a, b):
    return lax.dot_general(a, b, (((1,), (1,)), ((), ())), preferred_element_type=F32)


def dot_tn(a, b):
    return lax.dot_general(a, b, (((0,), (0,)), ((), ())), preferred_element_type=F32)


def dot_exact(a, b):
    return lax.dot_general(
        a, b, (((1,), (0,)), ((), ())), precision=lax.Precision.HIGHEST, preferred_element_type=F32
    )


def iota(shape, dim):
    return lax.broadcasted_iota(I32, shape, dim)


def shape_of(shape, dtype):
    return jax.ShapeDtypeStruct(shape, dtype)


def cost(flops, moved):
    return pl.CostEstimate(flops=int(flops), bytes_accessed=int(moved), transcendentals=0)


def params(mib):
    return pltpu.CompilerParams(vmem_limit_bytes=mib * MIB)


def call(body, outs, specs, flops, moved, scratch=(), room=16, out_specs=None, aliases=None):
    if out_specs is None:
        out_specs = tuple(VMEM for _ in outs) if isinstance(outs, tuple) else VMEM
    return pl.pallas_call(
        body,
        out_shape=outs,
        in_specs=specs,
        out_specs=out_specs,
        scratch_shapes=list(scratch),
        input_output_aliases=aliases or {},
        compiler_params=params(room),
        cost_estimate=cost(flops, moved),
    )


def start_all(sources, targets, sems):
    copies = [pltpu.make_async_copy(a, b, sems.at[n]) for n, (a, b) in enumerate(zip(sources, targets))]
    for copy in copies:
        copy.start()
    return copies


def request_kernel(piece, cap, *refs):
    sources, msg_ref, held, sems = refs[:5], refs[5], refs[6:11], refs[11]
    for copy in start_all(sources, held, sems):
        copy.wait()
    rows_ref, slot_ref, len_ref, dest_ref, counts_ref = held
    owners = rows_ref.shape[1]
    tokens = slot_ref.shape[1]
    replicas = tokens // piece
    my_dp = lax.axis_index("dp")
    lens = len_ref[...].astype(F32)
    takes = dest_ref[...] == iota((replicas, dest_ref.shape[1]), 0)
    totals = jnp.sum(jnp.where(takes, lens, 0.0), axis=1, keepdims=True)
    token = iota((replicas, tokens), 1)
    target = iota((replicas, tokens), 0)
    place = (my_dp * piece + token - target * piece).astype(F32)
    here = (token >= target * piece) & (token < (target + 1) * piece) & (place < totals)
    valid = jnp.sum(jnp.where(here, 1.0, 0.0), axis=0, keepdims=True)
    slot = slot_ref[...]
    by_owner = jnp.where(slot // cap == iota((owners, tokens), 0), valid, 0.0).astype(BF16)
    by_slot = jnp.where(slot % cap + cap == iota((LANES, tokens), 0), 1.0, 0.0).astype(BF16)
    counts = dot_nt(by_owner, by_slot)
    old = jnp.sum(counts_ref[...].astype(F32), axis=0, keepdims=True)
    total = jnp.sum(old, axis=1, keepdims=True) + jnp.sum(valid, axis=1, keepdims=True)
    lane = iota((owners, LANES), 1)
    place = jnp.where(iota((cap, LANES), 0) == iota((cap, LANES), 1), 1.0, 0.0)
    wanted = dot_exact(jnp.transpose(rows_ref[...].astype(F32)), place)
    msg_ref[...] = (jnp.where(lane == 2 * cap, total, counts) + wanted).astype(I32)


def asked_column(cap, asked_ref, first):
    askers = asked_ref.shape[0]
    total = askers * cap
    ahead = iota((total, askers), 0) - iota((total, askers), 1) * cap
    spread = jnp.where((ahead >= 0) & (ahead < cap), 1.0, 0.0).astype(BF16)
    asked = asked_ref[...].astype(F32)
    high = jnp.floor(asked * (1.0 / LANES))
    low = asked - high * LANES
    each = dot_nn(spread, high.astype(BF16)) * LANES + dot_nn(spread, low.astype(BF16))
    pick = iota((total, LANES), 1) == iota((total, LANES), 0) % cap + first
    return jnp.sum(jnp.where(pick, each, 0.0), axis=1, keepdims=True)


def serve_kernel(cap, asked_ref, table_ref, served_ref):
    rows = asked_column(cap, asked_ref, 0)
    total = rows.shape[0]
    step = min(256, table_ref.shape[0])
    lane = iota((total, step), 1).astype(F32)
    acc = None
    for base in range(0, table_ref.shape[0], step):
        pick = jnp.where(rows - float(base) == lane, 1.0, 0.0).astype(BF16)
        part = dot_nn(pick, table_ref[base : base + step, :])
        acc = part if acc is None else acc + part
    served_ref[...] = acc.astype(BF16)


def counts_kernel(cap, items, asked_ref, counts_ref, new_ref, log_ref, row_ref):
    rows = asked_column(cap, asked_ref, 0)
    added = asked_column(cap, asked_ref, cap)
    total = rows.shape[0]
    lines = counts_ref.shape[0]
    line = jnp.floor(rows * (1.0 / LANES))
    lane = rows - line * LANES
    by_line = jnp.where(line == iota((total, lines), 1).astype(F32), added, 0.0).astype(BF16)
    by_lane = jnp.where(lane == iota((total, LANES), 1).astype(F32), 1.0, 0.0).astype(BF16)
    new = counts_ref[...].astype(F32) + dot_tn(by_line, by_lane)
    whole = jnp.sum(asked_ref[:, 2 * cap : 2 * cap + 1].astype(F32), axis=0, keepdims=True)
    new_ref[...] = new.astype(I32)
    log_ref[...] = jnp.log(new + 1.0) - jnp.log(whole + float(items))
    row_ref[...] = jnp.transpose(jnp.broadcast_to(rows, (total, LANES)))[0:8, :]


def take_kernel(slot_ref, fetched_ref, home_ref):
    total = fetched_ref.shape[0]
    pick = jnp.where(slot_ref[...] == iota((total, slot_ref.shape[1]), 0), 1.0, 0.0).astype(BF16)
    home_ref[...] = dot_tn(pick, fetched_ref[...]).astype(BF16)


def slot_sum_kernel(slot_ref, back_ref, sums_ref):
    total = sums_ref.shape[0]
    pick = jnp.where(slot_ref[...] == iota((total, slot_ref.shape[1]), 0), 1.0, 0.0).astype(BF16)
    sums_ref[...] = dot_nn(pick, back_ref[...]).astype(BF16)


def scatter_kernel(row_ref, got_ref, out_ref, held_ref, sems):
    parts, block, _ = held_ref.shape
    total = got_ref.shape[0]
    line = iota((block, total), 0).astype(F32)
    copies = []
    for n in range(parts):
        pick = jnp.where(row_ref[0:1, :] - float(n * block) == line, 1.0, 0.0).astype(BF16)
        held_ref[n] = dot_nn(pick, got_ref[...])
        copies += start_all(
            (held_ref.at[n],), (out_ref.at[pl.ds(n * block, block), :],), sems.at[pl.ds(n, 1)]
        )
    for copy in copies:
        copy.wait()


def segments(len_ref, dest_ref, rows):
    nhist = len_ref.shape[1]
    mine = jnp.where(dest_ref[...] == lax.axis_index("dp"), len_ref[...], 0).astype(F32)
    later = iota((nhist, nhist), 0)
    other = iota((nhist, nhist), 1)
    ends = jnp.sum(jnp.where(other <= later, mine, 0.0), axis=1, keepdims=True)
    starts = jnp.sum(jnp.where(other < later, mine, 0.0), axis=1, keepdims=True)
    place = iota((nhist, rows), 1).astype(F32)
    label = iota((nhist, rows), 0).astype(F32) + 1.0
    return jnp.sum(jnp.where((starts <= place) & (place < ends), label, 0.0), axis=0, keepdims=True)


def valid_rows(seg, rows):
    return jnp.transpose(jnp.broadcast_to(jnp.where(seg > 0.0, 1.0, 0.0), (LANES, rows)))


def masked_grad(og_ref, valid):
    wide = og_ref.shape[1] // LANES
    return (og_ref[...].astype(F32) * jnp.concatenate([valid] * wide, axis=1)).astype(BF16)


def pos_bounds(rows, count):
    return [max(1, rows // 2 ** (count - m)) for m in range(count)]


def time_bounds(count):
    return [float(4**m) for m in range(count)]


def time_gaps(time_ref, rows):
    stamp = jnp.broadcast_to(time_ref[...].astype(F32), (rows, rows))
    return jnp.transpose(stamp) - stamp


def steps_passed(value, bounds):
    total = jnp.where(value >= bounds[0], 1, 0)
    for bound in bounds[1:]:
        total = total + jnp.where(value >= bound, 1, 0)
    return total


def bias_index(seg, time_ref, rows, count):
    across = jnp.broadcast_to(seg, (rows, rows))
    down = jnp.transpose(across)
    dist = iota((rows, rows), 0) - iota((rows, rows), 1)
    near = steps_passed(dist, pos_bounds(rows, count))
    late = steps_passed(time_gaps(time_ref, rows), time_bounds(count))
    mask = (across == down) & (down > 0.0) & (dist >= 0)
    return jnp.where(mask, near * (count + 1) + late, LANES - 1)


def bias_table(pos_ref, timew_ref):
    heads, count = pos_ref.shape
    entry = iota((heads, LANES), 1)
    near = entry // (count + 1)
    late = entry - near * (count + 1)
    table = jnp.zeros((heads, LANES), F32)
    for m in range(count):
        table = table + jnp.where(near > m, pos_ref[:, m : m + 1], 0.0)
        table = table + jnp.where(late > m, timew_ref[:, m : m + 1], 0.0)
    return jnp.where(entry == LANES - 1, MASKED, table)


def look_up(table_row, index):
    rows, cols = index.shape
    spread = jnp.broadcast_to(table_row, (rows, LANES))
    return jnp.concatenate(
        [jnp.take_along_axis(spread, index[:, at : at + LANES], axis=1) for at in range(0, cols, LANES)], axis=1
    )


def norm_of(value):
    centered = value - jnp.mean(value, axis=1, keepdims=True)
    scale = lax.rsqrt(jnp.mean(centered * centered, axis=1, keepdims=True) + EPSILON)
    return centered * scale, scale


def norm_back(grad_hat, normed, scale):
    first = jnp.mean(grad_hat, axis=1, keepdims=True)
    second = jnp.mean(grad_hat * normed, axis=1, keepdims=True)
    return scale * (grad_hat - first - normed * second)


def sigmoid(value):
    return 0.5 * jnp.tanh(0.5 * value) + 0.5


def layer_kernel(
    staged,
    x_ref,
    w_ref,
    b_ref,
    g1_ref,
    g2_ref,
    wo_ref,
    bo_ref,
    len_ref,
    dest_ref,
    time_ref,
    og_ref,
    pos_ref,
    timew_ref,
    lo_out,
    n1_ref,
    y_ref,
    go_ref,
    dh_ref,
    ds_ref,
    g2g_ref,
    msg_ref,
    h_ref,
    slope_ref,
    a_ref,
    lo_ref,
    sem,
):
    rows, width = x_ref.shape
    heads, count = pos_ref.shape
    pairs = heads // 2
    seg = segments(len_ref, dest_ref, rows)
    valid = valid_rows(seg, rows)
    go_ref[...] = masked_grad(og_ref, valid)
    dmix = dot_nt(go_ref[...], wo_ref[...])
    index = bias_index(seg, time_ref, rows, count)
    table = bias_table(pos_ref, timew_ref)
    x = x_ref[...].astype(F32)
    xhat, _ = norm_of(x)
    n1 = (xhat * g1_ref[...]).astype(BF16)
    n1_ref[...] = n1
    acts = []
    for part in range(4):
        cols = slice(part * width, (part + 1) * width)
        h = dot_nn(n1, w_ref[:, cols]) + b_ref[:, cols]
        sig = sigmoid(h)
        acts.append(h * sig)
        h_ref[:, cols] = sig * (1.0 + h * (1.0 - sig))
    u = acts[0]
    v, q, k = (a.astype(BF16) for a in acts[1:])
    lane = iota((rows, LANES), 1)
    low = lane < LANES // 2
    zero = jnp.zeros((rows, LANES), BF16)

    def half(value, parity):
        return jnp.where(low if parity == 0 else ~low, value, zero)

    def stacked(value):
        return jnp.concatenate([half(value, 0), half(value, 1)], axis=0)

    def abreast(value):
        return jnp.concatenate([value[:rows], value[rows:]], axis=1)

    outs = []
    for pair in range(pairs):
        cols = slice(pair * LANES, (pair + 1) * LANES)
        bias = jnp.concatenate([look_up(table[g : g + 1, :], index) for g in (2 * pair, 2 * pair + 1)], axis=0)
        s = dot_nt(stacked(q[:, cols]), k[:, cols]) * 0.125 + bias
        sig = sigmoid(s)
        a = (s * sig).astype(BF16)
        a_ref[pair] = a
        slope_ref[pair] = sig * (1.0 + s * (1.0 - sig))
        outs.append(dot_nn(abreast(a), stacked(v[:, cols])))
    o = jnp.concatenate(outs, axis=1)
    ohat, scale2 = norm_of(o)
    g2 = g2_ref[...]
    n2 = ohat * g2
    y = (n2 * u).astype(BF16)
    y_ref[...] = y
    branch = dot_nn(y, wo_ref[...]) + bo_ref[...]
    lo_ref[...] = (jnp.concatenate([valid] * (width // LANES), axis=1) * (x + branch)).astype(BF16)
    out_copy = pltpu.make_async_copy(lo_ref, lo_out, sem)
    out_copy.start()
    du = dmix * n2
    e2 = dmix * u
    g2g_ref[...] = jnp.sum(e2 * ohat, axis=0, keepdims=True)
    do = norm_back(e2 * g2, ohat, scale2).astype(BF16)
    dh_ref[:, 0:width] = (du * h_ref[:, 0:width]).astype(BF16)
    for pair in range(pairs):
        cols = slice(pair * LANES, (pair + 1) * LANES)
        dom = stacked(do[:, cols])
        ds = (dot_nt(dom, v[:, cols]) * slope_ref[pair]).astype(BF16)
        ds_ref[2 * pair] = ds[:rows]
        ds_ref[2 * pair + 1] = ds[rows:]
        dv = dot_tn(a_ref[pair], dom)
        dq = dot_nn(abreast(ds), stacked(k[:, cols]))
        dk = dot_tn(ds, stacked(q[:, cols]))
        for part, value in ((1, dv), (2, dq * 0.125), (3, dk * 0.125)):
            at = slice(part * width + pair * LANES, part * width + (pair + 1) * LANES)
            dh_ref[:, at] = (value * h_ref[:, at]).astype(BF16)
    if staged:
        other = 1 - lax.axis_index("table")
        half_cols = 2 * width
        msg_ref[:, 0:half_cols] = dh_ref[:, pl.ds(pl.multiple_of(other * half_cols, half_cols), half_cols)]
        msg_ref[:, half_cols : half_cols + width] = n1
        half_y = width // 2
        y_half = y_ref[:, pl.ds(pl.multiple_of(other * half_y, half_y), half_y)].astype(F32)
        y_half = y_half * jnp.concatenate([valid] * (half_y // LANES), axis=1)
        msg_ref[:, half_cols + width :] = y_half.astype(BF16)
    else:
        msg_ref[...] = jnp.zeros_like(msg_ref)
    out_copy.wait()


SMALL_ROWS = 48


def prefix_ends(time_ref, rows, count):
    time_lane = 64
    row = iota((1, rows), 1).astype(F32)
    ends = [row - float(bound) for bound in pos_bounds(rows, count)]
    ends += [jnp.full((time_lane - count, rows), -1.0, F32)]
    stamp = jnp.broadcast_to(time_ref[...].astype(F32), (rows, rows))
    gaps = stamp - jnp.transpose(stamp)
    for bound in time_bounds(count):
        ends.append(jnp.sum(jnp.where(gaps >= bound, 1.0, 0.0), axis=0, keepdims=True) - 1.0)
    ends += [jnp.full((LANES - time_lane - count, rows), -1.0, F32)]
    return jnp.transpose(jnp.concatenate(ends, axis=0)).astype(I32)


def after_kernel(count, dh_ref, w_ref, x_ref, g1_ref, go_ref, ds_ref, time_ref, g2g_ref, *rest):
    dx_out, out_ref, dx_ref, sem = rest
    heads, rows, _ = ds_ref.shape
    xhat, scale = norm_of(x_ref[...].astype(F32))
    dn1 = dot_nt(dh_ref[...], w_ref[...])
    go = go_ref[...].astype(F32)
    dx_ref[...] = (norm_back(dn1 * g1_ref[...], xhat, scale) + go).astype(BF16)
    copy = pltpu.make_async_copy(dx_ref, dx_out, sem)
    copy.start()
    out_ref[...] = jnp.zeros_like(out_ref)
    g1_grad = jnp.sum(dn1 * xhat, axis=0, keepdims=True)
    b_grad = jnp.sum(dh_ref[...].astype(F32), axis=0, keepdims=True)
    go_sum = jnp.sum(go, axis=0, keepdims=True)
    at = 0
    for value in (b_grad, g1_grad, g2g_ref[...], go_sum):
        for col in range(0, value.shape[1], LANES):
            out_ref[at : at + 1, :] = value[:, col : col + LANES]
            at += 1
    at = (at + 7) // 8 * 8
    ends = prefix_ends(time_ref, rows, count)
    upto = jnp.where(iota((rows, rows), 0) <= iota((rows, rows), 1), 1.0, 0.0).astype(BF16)
    prefix = dot_nn(ds_ref[...].reshape(heads * rows, rows), upto)
    tables = [
        ((ends >= first) & (ends < first + LANES), jnp.clip(ends - first, 0, LANES - 1))
        for first in range(0, rows, LANES)
    ]
    sums = []
    for g in range(heads):
        total = jnp.zeros((1, LANES), F32)
        for n, (here, index) in enumerate(tables):
            lines = slice(n * LANES, rows)
            value = prefix[g * rows + n * LANES : (g + 1) * rows, n * LANES : (n + 1) * LANES]
            found = jnp.where(here[lines], jnp.take_along_axis(value, index[lines], axis=1), 0.0)
            total = total + jnp.sum(found, axis=0, keepdims=True)
        sums.append(total)
    sums = jnp.concatenate(sums, axis=0)
    out_ref[at : at + heads, :] = sums
    out_ref[at + heads : at + 2 * heads, 0 : LANES // 2] = sums[:, LANES // 2 :]
    copy.wait()


def place_of(columns):
    my_dp = lax.axis_index("dp")
    return lax.rem(my_dp, columns), lax.div(my_dp, columns)


def pack_kernel(planes, columns, dh_ref, n1_ref, y_ref, go_ref, got_ref, got_grad_ref, small_ref, *rest):
    nears, fars, (uv_ref, wo_ref) = rest[:columns], rest[columns : 2 * columns], rest[2 * columns :]
    width = n1_ref.shape[1]
    core = lax.axis_index("table")
    my_xy, my_z = place_of(columns)
    half_cols = 2 * width
    half_y = width // 2
    dh = jnp.concatenate(
        [dh_ref[:, pl.ds(pl.multiple_of(core * half_cols, half_cols), half_cols)], got_ref[:, 0:half_cols]],
        axis=0,
    )
    n1 = jnp.concatenate([n1_ref[...], got_ref[:, half_cols : half_cols + width]], axis=0)
    y = jnp.concatenate(
        [y_ref[:, pl.ds(pl.multiple_of(core * half_y, half_y), half_y)], got_ref[:, half_cols + width :]],
        axis=0,
    )
    go = jnp.concatenate([go_ref[...], got_grad_ref[...]], axis=0)
    uv_ref[...] = dot_tn(n1, dh)
    wo_ref[...] = dot_tn(y, go)
    short = half_y // (planes * columns)
    for rel_xy in range(columns):
        for rel_z in range(planes):
            chunk = jnp.bitwise_xor(my_xy, rel_xy) * planes + jnp.bitwise_xor(my_z, rel_z)
            out = (nears, fars)[rel_z // 2][rel_xy].at[rel_z % 2]
            for part in range(2):
                at = pl.multiple_of((2 * chunk + part) * short, short)
                out[:, part * half_cols : (part + 1) * half_cols] = uv_ref[pl.ds(at, short), :].astype(BF16)
            at = pl.multiple_of(chunk * short, short)
            out[:, 2 * half_cols : 2 * half_cols + width] = wo_ref[pl.ds(at, short), :].astype(BF16)
            out[:, 2 * half_cols + width :] = small_ref[pl.ds(at, short), :].astype(BF16)


def unpack(planes, columns, chunks, uvqk_ref, wout_ref, small_ref, held_uvqk, held_wout, sems):
    short = held_wout.shape[1]
    width = held_wout.shape[2]
    core = lax.axis_index("table")
    my_xy, my_z = place_of(columns)
    half_cols = 2 * width
    half_y = width // 2
    wout_lanes = slice(2 * half_cols, 2 * half_cols + width)
    small_lanes = slice(2 * half_cols + width, 2 * half_cols + width + LANES)
    copies = []
    for n, (rel_xy, rel_z, whose, piece) in enumerate(chunks):
        chunk = jnp.bitwise_xor(my_xy, rel_xy) * planes + jnp.bitwise_xor(my_z, rel_z)
        side = jnp.bitwise_xor(core, whose)
        for part in range(2):
            held_uvqk[n, part * short : (part + 1) * short, :] = piece[
                :, part * half_cols : (part + 1) * half_cols
            ].astype(F32)
        held_wout[n] = piece[:, wout_lanes].astype(F32)
        tall = pl.ds(pl.multiple_of(chunk * 2 * short, 2 * short), 2 * short)
        cols = pl.ds(pl.multiple_of(side * half_cols, half_cols), half_cols)
        rows = pl.ds(pl.multiple_of(side * half_y + chunk * short, short), short)
        copies += start_all(
            (held_uvqk.at[n], held_wout.at[n]),
            (uvqk_ref.at[tall, cols], wout_ref.at[rows, :]),
            sems.at[pl.ds(2 * n, 2)],
        )
        small_ref[pl.ds(pl.multiple_of(chunk * short, short), short), :] += piece[:, small_lanes].astype(F32)
    return copies


def chunks_of(planes, first_z, pieces, whose, first_xy=0):
    return [
        (first_xy + xy, first_z + z, whose, piece.at[z])
        for xy, piece in enumerate(pieces)
        for z in range(min(2, planes - first_z))
    ]


def unpack_first_kernel(planes, columns, *refs):
    mine, theirs = refs[: columns + 1], refs[columns + 1 : 2 * columns + 2]
    uvqk_ref, wout_ref, small_ref, *scratch = refs[2 * columns + 2 :]
    small_ref[...] = jnp.zeros_like(small_ref)
    chunks = []
    for whose, pieces in enumerate((mine, theirs)):
        chunks += chunks_of(planes, 0, pieces[:columns], whose) + chunks_of(planes, 2, pieces[columns:], whose)
    for copy in unpack(planes, columns, chunks, uvqk_ref, wout_ref, small_ref, *scratch):
        copy.wait()


def unpack_next_kernel(planes, columns, *refs):
    peers = columns - 1
    mine, before_ref = refs[:peers], refs[peers + 2]
    uvqk_ref, wout_ref, small_ref, *scratch = refs[peers + 3 :]
    small_ref[...] = before_ref[...]
    chunks = chunks_of(planes, 2, mine, 0, 1)
    for copy in unpack(planes, columns, chunks, uvqk_ref, wout_ref, small_ref, *scratch):
        copy.wait()


def unpack_last_kernel(planes, columns, *refs):
    peers = columns - 1
    theirs, before_ref = refs[:peers], refs[peers + 2]
    uvqk_ref, wout_ref, *small_outs = refs[peers + 3 : peers + 11]
    small_ref, *held, small_sems = refs[peers + 11 : peers + 19]
    b_ref, g1_ref, g2_ref, bo_ref, pos_ref, time_ref = held
    scratch = refs[peers + 19 :]
    small_ref[...] = before_ref[...]
    chunks = chunks_of(planes, 2, theirs, 1, 1)
    copies = unpack(planes, columns, chunks, uvqk_ref, wout_ref, small_ref, *scratch)
    at = 0
    for out in (b_ref, g1_ref, g2_ref, bo_ref):
        for col in range(0, out.shape[1], LANES):
            out[:, col : col + LANES] = small_ref[at : at + 1, :]
            at += 1
    at = (at + 7) // 8 * 8
    heads, count = pos_ref.shape
    pos_ref[...] = small_ref[at : at + heads, 0:count]
    time_ref[...] = small_ref[at + heads : at + 2 * heads, 0:count]
    for copy in copies + start_all(held, small_outs, small_sems):
        copy.wait()


def add_up(first, *rest):
    total = first.astype(F32)
    for other in rest:
        total = total + other.astype(F32)
    return total.astype(BF16)


def xor_step(value, size, step):
    return lax.ppermute(value, "dp", [(i, i ^ step) for i in range(size)])


def reduce_step(pieces, size, stride):
    return add_up(pieces[0], *(xor_step(pieces[k], size, k * stride) for k in range(1, len(pieces))))


def gather_step(own, size, stride, peers):
    return [own] + [xor_step(own, size, k * stride) for k in range(1, peers)]


def swap_cores(value):
    return lax.ppermute(value, "table", [(0, 1), (1, 0)])


def on_device(
    item_table,
    token_request_slot,
    request_rows,
    lengths,
    assignment,
    timestamps,
    item_counts,
    first_norm_gain,
    w_uvqk,
    b_uvqk,
    norm2_gain,
    w_out,
    b_out,
    pos_weight,
    time_weight,
    out_grad,
):
    rows = token_request_slot.shape[0]
    rows_dev, width = item_table.shape
    replicas = lax.axis_size("dp")
    groups = lax.axis_size("table")
    devices = replicas * groups
    cap = request_rows.shape[2]
    piece = rows // replicas
    heads, count = pos_weight.shape
    slots = devices * cap
    columns = 4
    planes = replicas // columns
    staged = (
        groups == 2
        and replicas == 16
        and width % (32 * replicas) == 0
        and (2 * heads + SMALL_ROWS - 16) <= width // 2
    )
    mb = MIB

    slot_row = token_request_slot.reshape(1, rows)
    time_row = timestamps.reshape(1, rows)
    counts_2d = item_counts.reshape(rows_dev // LANES, LANES)
    msg = call(
        functools.partial(request_kernel, piece, cap),
        shape_of((devices, LANES), I32),
        [HBM] * 5,
        mb,
        mb // 8,
        scratch=(
            pltpu.VMEM((cap, devices), I32),
            pltpu.VMEM((1, rows), I32),
            pltpu.VMEM(lengths.shape, I32),
            pltpu.VMEM(lengths.shape, I32),
            pltpu.VMEM(counts_2d.shape, I32),
            pltpu.SemaphoreType.DMA((5,)),
        ),
        room=64,
    )(request_rows.transpose(0, 2, 1).reshape(cap, devices), slot_row, lengths, assignment, counts_2d)
    if staged:
        msg, other_grad = lax.optimization_barrier((msg, out_grad))
        got_grad = swap_cores(other_grad)
    asked = lax.all_to_all(msg.reshape(devices, 1, LANES), BOTH, 0, 0, tiled=True).reshape(devices, LANES)
    if staged:
        asked, got_grad = lax.optimization_barrier((asked, got_grad))
    served = call(
        functools.partial(serve_kernel, cap), shape_of((slots, width), BF16), [VMEM] * 2, 1 << 30, 5 * mb
    )(asked, item_table)
    fetched = lax.all_to_all(served.reshape(devices, cap, width), BOTH, 0, 0, tiled=True)
    new_counts, log_q, asked_row = call(
        functools.partial(counts_kernel, cap, rows_dev * devices),
        (
            shape_of((rows_dev // LANES, LANES), I32),
            shape_of((rows_dev // LANES, LANES), F32),
            shape_of((8, slots), F32),
        ),
        [VMEM] * 2,
        64 * mb,
        mb,
    )(asked, counts_2d)
    home = call(take_kernel, shape_of((rows, width), BF16), [VMEM] * 2, 64 * mb, mb)(
        slot_row, fetched.reshape(slots, width)
    )
    x = lax.all_to_all(home.reshape(replicas, piece, width), "dp", 0, 0, tiled=True).reshape(rows, width)

    half_cols = 2 * width
    g1, g2 = first_norm_gain.reshape(1, width), norm2_gain.reshape(1, width)
    msg_cols = half_cols + width + width // 2 if staged else LANES
    layer_out, n1, y, go, dh, ds, g2_grad, to_core = call(
        functools.partial(layer_kernel, staged),
        (
            shape_of((rows, width), BF16),
            shape_of((rows, width), BF16),
            shape_of((rows, width), BF16),
            shape_of((rows, width), BF16),
            shape_of((rows, 4 * width), BF16),
            shape_of((heads, rows, rows), BF16),
            shape_of((1, width), F32),
            shape_of((rows, msg_cols), BF16),
        ),
        [VMEM] * 13,
        2 << 30,
        8 * mb,
        scratch=(
            pltpu.VMEM((rows, 4 * width), F32),
            pltpu.VMEM((heads // 2, 2 * rows, rows), F32),
            pltpu.VMEM((heads // 2, 2 * rows, rows), BF16),
            pltpu.VMEM((rows, width), BF16),
            pltpu.SemaphoreType.DMA,
        ),
        room=24,
        out_specs=(HBM,) + (VMEM,) * 7,
    )(
        x,
        w_uvqk,
        b_uvqk.reshape(1, 4 * width),
        g1,
        g2,
        w_out,
        b_out.reshape(1, width),
        lengths,
        assignment,
        time_row,
        out_grad,
        pos_weight,
        time_weight,
    )
    def home_again(dx):
        return lax.all_to_all(dx.reshape(replicas, piece, width), "dp", 0, 0, tiled=True).reshape(rows, width)

    def to_owners(back):
        return send_sums(slot_sums(back))

    def slot_sums(back):
        return call(slot_sum_kernel, shape_of((slots, width), BF16), [VMEM] * 2, 64 * mb, mb)(slot_row, back)
    def send_sums(sums):
        sums = lax.all_to_all(sums.reshape(devices, cap, width), BOTH, 0, 0, tiled=True)
        return sums.reshape(slots, width)

    def into_table(got_sums):
        block = min(512, rows_dev)
        return call(
            scatter_kernel,
            shape_of((rows_dev, width), F32),
            [VMEM] * 2,
            1 << 30,
            8 * mb,
            scratch=(
                pltpu.VMEM((rows_dev // block, block, width), F32),
                pltpu.SemaphoreType.DMA((rows_dev // block,)),
            ),
            room=24,
            out_specs=HBM,
        )(asked_row, got_sums)

    if staged:
        got = swap_cores(to_core)
    dx, small = call(
        functools.partial(after_kernel, count),
        (shape_of((rows, width), BF16), shape_of((width // 2, LANES), F32)),
        [VMEM] * 8,
        1 << 29,
        4 * mb,
        scratch=(pltpu.VMEM((rows, width), BF16), pltpu.SemaphoreType.DMA),
        out_specs=(HBM, VMEM),
    )(dh, w_uvqk, x, g1, go, ds, time_row, g2_grad)
    if staged:
        short = width // replicas // 2
        pieces = call(
            functools.partial(pack_kernel, planes, columns),
            tuple(shape_of((2, short, 5 * width + LANES), BF16) for _ in range(2 * columns)),
            [VMEM] * 7,
            1 << 30,
            6 * mb,
            scratch=(pltpu.VMEM((width, half_cols), F32), pltpu.VMEM((width // 2, width), F32)),
        )(dh, n1, y, go, got, got_grad, small)
        dx, *pieces = lax.optimization_barrier((dx, *pieces))
        nears, fars = pieces[:columns], pieces[columns:]
        back = home_again(dx)
        got_far = [xor_step(fars[k], replicas, k) for k in range(1, columns)]
        nears, got_far[0] = lax.optimization_barrier((nears, got_far[0]))
        far_line = add_up(fars[0], *got_far)
        got_line = [xor_step(far_line[k - 2], replicas, k * columns) for k in range(2, planes)]
        near_line = reduce_step(nears, replicas, 1)
        near_line, back = lax.optimization_barrier((near_line, back))
        got_next = xor_step(near_line[1], replicas, columns)
        sums = slot_sums(back)
        own = add_up(near_line[0], got_next, *got_line)
        own, sums = lax.optimization_barrier((own, sums))
        next_own = xor_step(own, replicas, columns)
        far = [xor_step(own, replicas, k * columns) for k in range(2, planes)]
        near = jnp.stack([own, next_own])
        nears = gather_step(near, replicas, 1, columns)
        far[1], sums = lax.optimization_barrier((far[1], sums))
        got_sums = send_sums(sums)
        far = jnp.stack(far)
        table_grad = into_table(got_sums)
        fars = gather_step(far, replicas, 1, columns)
        their_nears = [swap_cores(piece) for piece in nears]
        their_far = swap_cores(far)
        small_shape = shape_of((width // 2, LANES), F32)
        wide_shapes = (shape_of((width, 4 * width), F32), shape_of((width, width), F32))

        def unpack_call(body, specs, outs, chunks, scratch=(), aliases=None, place=VMEM):
            return call(
                functools.partial(body, planes, columns),
                wide_shapes + outs,
                specs,
                mb,
                3 * mb,
                scratch=scratch
                + (
                    pltpu.VMEM((chunks, 2 * short, half_cols), F32),
                    pltpu.VMEM((chunks, short, width), F32),
                    pltpu.SemaphoreType.DMA((2 * chunks,)),
                ),
                out_specs=(HBM, HBM) + (place,) * len(outs),
                aliases=aliases,
            )

        peers = columns - 1
        wides = {peers: 0, peers + 1: 1}
        wide_specs = [VMEM] * peers + [HBM, HBM, VMEM]
        *sums_so_far, small_sum = unpack_call(
            unpack_first_kernel, [VMEM] * (2 * columns + 2), (small_shape,), 2 * (2 * columns + 2)
        )(*nears, far, *their_nears, their_far)
        fars, small_sum, table_grad = lax.optimization_barrier((fars, small_sum, table_grad))
        their_fars = [swap_cores(piece) for piece in fars[1:]]
        *sums_so_far, small_sum = unpack_call(
            unpack_next_kernel, wide_specs, (small_shape,), 2 * peers, aliases=wides
        )(*fars[1:], *sums_so_far, small_sum)
        small_outs = ((1, 4 * width),) + ((1, width),) * 3 + ((heads, count),) * 2
        w_uvqk_sum, w_out_sum, b_sum, g1_sum, g2_sum, bo_sum, pos_sum, time_sum = unpack_call(
            unpack_last_kernel,
            wide_specs,
            tuple(shape_of(shape, F32) for shape in small_outs),
            2 * peers,
            scratch=(
                pltpu.VMEM(small_shape.shape, F32),
                *(pltpu.VMEM(shape, F32) for shape in small_outs),
                pltpu.SemaphoreType.DMA((len(small_outs),)),
            ),
            aliases=wides,
            place=HBM,
        )(*their_fars, *sums_so_far, small_sum)
    else:
        table_grad = into_table(to_owners(home_again(dx)))
        w_uvqk_sum, w_out_sum, parts = lax.psum((dot_tn(n1, dh), dot_tn(y, go), small[0:SMALL_ROWS]), BOTH)
        at = 4 * width // LANES
        step = width // LANES
        b_sum = parts[0:at]
        g1_sum, g2_sum, bo_sum = (parts[at + n * step : at + (n + 1) * step] for n in range(3))
        at = (at + 3 * step + 7) // 8 * 8
        pos_sum = parts[at : at + heads, 0:count]
        time_sum = parts[at + heads : at + 2 * heads, 0:count]
    return (
        layer_out,
        table_grad,
        g1_sum.reshape(width),
        w_uvqk_sum,
        b_sum.reshape(4 * width),
        g2_sum.reshape(width),
        w_out_sum,
        bo_sum.reshape(width),
        pos_sum,
        time_sum,
        new_counts.reshape(rows_dev),
        log_q.reshape(rows_dev),
    )


def solution(mesh):
    split = P(("dp", "table"))
    rows_split = P(("dp", "table"), None)
    placed = (
        rows_split,
        split,
        P(("dp", "table"), None, None),
        P("table", None),
        P("table", None),
        split,
        split,
        P(),
        P(),
        P(),
        P(),
        P(),
        P(),
        P(),
        P(),
        rows_split,
    )
    return jax.shard_map(
        on_device,
        mesh=mesh,
        in_specs=placed,
        out_specs=(rows_split, rows_split, P(), P(), P(), P(), P(), P(), P(), P(), split, split),
        check_vma=False,
    )
```

```python
import functools

import jax
import jax.numpy as jnp
from jax import lax
from jax.experimental import pallas as pl
from jax.experimental.pallas import tpu as pltpu
from jax.sharding import PartitionSpec as P

EPSILON = 1e-05
MASKED = -1e30
F32 = jnp.float32
BF16 = jnp.bfloat16
I32 = jnp.int32
BOTH = ("dp", "table")
LANES = 128
VMEM = pl.BlockSpec(memory_space=pltpu.VMEM)
SMEM = pl.BlockSpec(memory_space=pltpu.SMEM)
HBM = pl.BlockSpec(memory_space=pltpu.HBM)
MIB = 1 << 20


def dot_nn(a, b):
    return lax.dot_general(a, b, (((1,), (0,)), ((), ())), preferred_element_type=F32)


def dot_nt(a, b):
    return lax.dot_general(a, b, (((1,), (1,)), ((), ())), preferred_element_type=F32)


def dot_tn(a, b):
    return lax.dot_general(a, b, (((0,), (0,)), ((), ())), preferred_element_type=F32)


def dot_exact(a, b):
    return lax.dot_general(
        a, b, (((1,), (0,)), ((), ())), precision=lax.Precision.HIGHEST, preferred_element_type=F32
    )


def iota(shape, dim):
    return lax.broadcasted_iota(I32, shape, dim)


def shape_of(shape, dtype):
    return jax.ShapeDtypeStruct(shape, dtype)


def cost(flops, moved):
    return pl.CostEstimate(flops=int(flops), bytes_accessed=int(moved), transcendentals=0)


def params(mib):
    return pltpu.CompilerParams(vmem_limit_bytes=mib * MIB)


def call(body, outs, specs, flops, moved, scratch=(), room=16, out_specs=None, aliases=None):
    if out_specs is None:
        out_specs = tuple(VMEM for _ in outs) if isinstance(outs, tuple) else VMEM
    return pl.pallas_call(
        body,
        out_shape=outs,
        in_specs=specs,
        out_specs=out_specs,
        scratch_shapes=list(scratch),
        input_output_aliases=aliases or {},
        compiler_params=params(room),
        cost_estimate=cost(flops, moved),
    )


def start_all(sources, targets, sems):
    copies = [pltpu.make_async_copy(a, b, sems.at[n]) for n, (a, b) in enumerate(zip(sources, targets))]
    for copy in copies:
        copy.start()
    return copies


def request_kernel(piece, cap, *refs):
    sources, msg_ref, held, sems = refs[:5], refs[5], refs[6:11], refs[11]
    for copy in start_all(sources, held, sems):
        copy.wait()
    rows_ref, slot_ref, len_ref, dest_ref, counts_ref = held
    owners = rows_ref.shape[1]
    tokens = slot_ref.shape[1]
    replicas = tokens // piece
    my_dp = lax.axis_index("dp")
    lens = len_ref[...].astype(F32)
    takes = dest_ref[...] == iota((replicas, dest_ref.shape[1]), 0)
    totals = jnp.sum(jnp.where(takes, lens, 0.0), axis=1, keepdims=True)
    token = iota((replicas, tokens), 1)
    target = iota((replicas, tokens), 0)
    place = (my_dp * piece + token - target * piece).astype(F32)
    here = (token >= target * piece) & (token < (target + 1) * piece) & (place < totals)
    valid = jnp.sum(jnp.where(here, 1.0, 0.0), axis=0, keepdims=True)
    slot = slot_ref[...]
    by_owner = jnp.where(slot // cap == iota((owners, tokens), 0), valid, 0.0).astype(BF16)
    by_slot = jnp.where(slot % cap + cap == iota((LANES, tokens), 0), 1.0, 0.0).astype(BF16)
    counts = dot_nt(by_owner, by_slot)
    old = jnp.sum(counts_ref[...].astype(F32), axis=0, keepdims=True)
    total = jnp.sum(old, axis=1, keepdims=True) + jnp.sum(valid, axis=1, keepdims=True)
    lane = iota((owners, LANES), 1)
    place = jnp.where(iota((cap, LANES), 0) == iota((cap, LANES), 1), 1.0, 0.0)
    wanted = dot_exact(jnp.transpose(rows_ref[...].astype(F32)), place)
    msg_ref[...] = (jnp.where(lane == 2 * cap, total, counts) + wanted).astype(I32)


def asked_column(cap, asked_ref, first):
    askers = asked_ref.shape[0]
    total = askers * cap
    ahead = iota((total, askers), 0) - iota((total, askers), 1) * cap
    spread = jnp.where((ahead >= 0) & (ahead < cap), 1.0, 0.0).astype(BF16)
    asked = asked_ref[...].astype(F32)
    high = jnp.floor(asked * (1.0 / LANES))
    low = asked - high * LANES
    each = dot_nn(spread, high.astype(BF16)) * LANES + dot_nn(spread, low.astype(BF16))
    pick = iota((total, LANES), 1) == iota((total, LANES), 0) % cap + first
    return jnp.sum(jnp.where(pick, each, 0.0), axis=1, keepdims=True)


def serve_kernel(cap, asked_ref, table_ref, served_ref):
    rows = asked_column(cap, asked_ref, 0)
    total = rows.shape[0]
    step = min(256, table_ref.shape[0])
    lane = iota((total, step), 1).astype(F32)
    acc = None
    for base in range(0, table_ref.shape[0], step):
        pick = jnp.where(rows - float(base) == lane, 1.0, 0.0).astype(BF16)
        part = dot_nn(pick, table_ref[base : base + step, :])
        acc = part if acc is None else acc + part
    served_ref[...] = acc.astype(BF16)


def counts_kernel(cap, items, asked_ref, counts_ref, new_ref, log_ref, row_ref):
    rows = asked_column(cap, asked_ref, 0)
    added = asked_column(cap, asked_ref, cap)
    total = rows.shape[0]
    lines = counts_ref.shape[0]
    line = jnp.floor(rows * (1.0 / LANES))
    lane = rows - line * LANES
    by_line = jnp.where(line == iota((total, lines), 1).astype(F32), added, 0.0).astype(BF16)
    by_lane = jnp.where(lane == iota((total, LANES), 1).astype(F32), 1.0, 0.0).astype(BF16)
    new = counts_ref[...].astype(F32) + dot_tn(by_line, by_lane)
    whole = jnp.sum(asked_ref[:, 2 * cap : 2 * cap + 1].astype(F32), axis=0, keepdims=True)
    new_ref[...] = new.astype(I32)
    log_ref[...] = jnp.log(new + 1.0) - jnp.log(whole + float(items))
    row_ref[...] = jnp.transpose(jnp.broadcast_to(rows, (total, LANES)))[0:8, :]


def take_kernel(slot_ref, fetched_ref, home_ref):
    total = fetched_ref.shape[0]
    pick = jnp.where(slot_ref[...] == iota((total, slot_ref.shape[1]), 0), 1.0, 0.0).astype(BF16)
    home_ref[...] = dot_tn(pick, fetched_ref[...]).astype(BF16)


def slot_sum_kernel(slot_ref, back_ref, sums_ref):
    total = sums_ref.shape[0]
    pick = jnp.where(slot_ref[...] == iota((total, slot_ref.shape[1]), 0), 1.0, 0.0).astype(BF16)
    sums_ref[...] = dot_nn(pick, back_ref[...]).astype(BF16)


def scatter_kernel(row_ref, got_ref, out_ref, held_ref, sems):
    parts, block, _ = held_ref.shape
    total = got_ref.shape[0]
    line = iota((block, total), 0).astype(F32)
    copies = []
    for n in range(parts):
        pick = jnp.where(row_ref[0:1, :] - float(n * block) == line, 1.0, 0.0).astype(BF16)
        held_ref[n] = dot_nn(pick, got_ref[...])
        copies += start_all(
            (held_ref.at[n],), (out_ref.at[pl.ds(n * block, block), :],), sems.at[pl.ds(n, 1)]
        )
    for copy in copies:
        copy.wait()


def segments(len_ref, dest_ref, rows):
    nhist = len_ref.shape[1]
    mine = jnp.where(dest_ref[...] == lax.axis_index("dp"), len_ref[...], 0).astype(F32)
    later = iota((nhist, nhist), 0)
    other = iota((nhist, nhist), 1)
    ends = jnp.sum(jnp.where(other <= later, mine, 0.0), axis=1, keepdims=True)
    starts = jnp.sum(jnp.where(other < later, mine, 0.0), axis=1, keepdims=True)
    place = iota((nhist, rows), 1).astype(F32)
    label = iota((nhist, rows), 0).astype(F32) + 1.0
    return jnp.sum(jnp.where((starts <= place) & (place < ends), label, 0.0), axis=0, keepdims=True)


def valid_rows(seg, rows):
    return jnp.transpose(jnp.broadcast_to(jnp.where(seg > 0.0, 1.0, 0.0), (LANES, rows)))


def masked_grad(og_ref, valid):
    wide = og_ref.shape[1] // LANES
    return (og_ref[...].astype(F32) * jnp.concatenate([valid] * wide, axis=1)).astype(BF16)


def pos_bounds(rows, count):
    return [max(1, rows // 2 ** (count - m)) for m in range(count)]


def time_bounds(count):
    return [float(4**m) for m in range(count)]


def time_gaps(time_ref, rows):
    stamp = jnp.broadcast_to(time_ref[...].astype(F32), (rows, rows))
    return jnp.transpose(stamp) - stamp


def steps_passed(value, bounds):
    total = jnp.where(value >= bounds[0], 1, 0)
    for bound in bounds[1:]:
        total = total + jnp.where(value >= bound, 1, 0)
    return total


def bias_index(seg, time_ref, rows, count):
    across = jnp.broadcast_to(seg, (rows, rows))
    down = jnp.transpose(across)
    dist = iota((rows, rows), 0) - iota((rows, rows), 1)
    near = steps_passed(dist, pos_bounds(rows, count))
    late = steps_passed(time_gaps(time_ref, rows), time_bounds(count))
    mask = (across == down) & (down > 0.0) & (dist >= 0)
    return jnp.where(mask, near * (count + 1) + late, LANES - 1)


def bias_table(pos_ref, timew_ref):
    heads, count = pos_ref.shape
    entry = iota((heads, LANES), 1)
    near = entry // (count + 1)
    late = entry - near * (count + 1)
    table = jnp.zeros((heads, LANES), F32)
    for m in range(count):
        table = table + jnp.where(near > m, pos_ref[:, m : m + 1], 0.0)
        table = table + jnp.where(late > m, timew_ref[:, m : m + 1], 0.0)
    return jnp.where(entry == LANES - 1, MASKED, table)


def look_up(table_row, index):
    rows, cols = index.shape
    spread = jnp.broadcast_to(table_row, (rows, LANES))
    return jnp.concatenate(
        [jnp.take_along_axis(spread, index[:, at : at + LANES], axis=1) for at in range(0, cols, LANES)], axis=1
    )


def norm_of(value):
    centered = value - jnp.mean(value, axis=1, keepdims=True)
    scale = lax.rsqrt(jnp.mean(centered * centered, axis=1, keepdims=True) + EPSILON)
    return centered * scale, scale


def norm_back(grad_hat, normed, scale):
    first = jnp.mean(grad_hat, axis=1, keepdims=True)
    second = jnp.mean(grad_hat * normed, axis=1, keepdims=True)
    return scale * (grad_hat - first - normed * second)


def sigmoid(value):
    return 0.5 * jnp.tanh(0.5 * value) + 0.5


def layer_kernel(
    staged,
    x_ref,
    w_ref,
    b_ref,
    g1_ref,
    g2_ref,
    wo_ref,
    bo_ref,
    len_ref,
    dest_ref,
    time_ref,
    og_ref,
    pos_ref,
    timew_ref,
    lo_out,
    n1_ref,
    y_ref,
    go_ref,
    dh_ref,
    ds_ref,
    g2g_ref,
    msg_ref,
    h_ref,
    slope_ref,
    a_ref,
    lo_ref,
    sem,
):
    rows, width = x_ref.shape
    heads, count = pos_ref.shape
    pairs = heads // 2
    seg = segments(len_ref, dest_ref, rows)
    valid = valid_rows(seg, rows)
    go_ref[...] = masked_grad(og_ref, valid)
    dmix = dot_nt(go_ref[...], wo_ref[...])
    index = bias_index(seg, time_ref, rows, count)
    table = bias_table(pos_ref, timew_ref)
    x = x_ref[...].astype(F32)
    xhat, _ = norm_of(x)
    n1 = (xhat * g1_ref[...]).astype(BF16)
    n1_ref[...] = n1
    acts = []
    for part in range(4):
        cols = slice(part * width, (part + 1) * width)
        h = dot_nn(n1, w_ref[:, cols]) + b_ref[:, cols]
        sig = sigmoid(h)
        acts.append(h * sig)
        h_ref[:, cols] = sig * (1.0 + h * (1.0 - sig))
    u = acts[0]
    v, q, k = (a.astype(BF16) for a in acts[1:])
    lane = iota((rows, LANES), 1)
    low = lane < LANES // 2
    zero = jnp.zeros((rows, LANES), BF16)

    def half(value, parity):
        return jnp.where(low if parity == 0 else ~low, value, zero)

    def stacked(value):
        return jnp.concatenate([half(value, 0), half(value, 1)], axis=0)

    def abreast(value):
        return jnp.concatenate([value[:rows], value[rows:]], axis=1)

    outs = []
    for pair in range(pairs):
        cols = slice(pair * LANES, (pair + 1) * LANES)
        bias = jnp.concatenate([look_up(table[g : g + 1, :], index) for g in (2 * pair, 2 * pair + 1)], axis=0)
        s = dot_nt(stacked(q[:, cols]), k[:, cols]) * 0.125 + bias
        sig = sigmoid(s)
        a = (s * sig).astype(BF16)
        a_ref[pair] = a
        slope_ref[pair] = sig * (1.0 + s * (1.0 - sig))
        outs.append(dot_nn(abreast(a), stacked(v[:, cols])))
    o = jnp.concatenate(outs, axis=1)
    ohat, scale2 = norm_of(o)
    g2 = g2_ref[...]
    n2 = ohat * g2
    y = (n2 * u).astype(BF16)
    y_ref[...] = y
    branch = dot_nn(y, wo_ref[...]) + bo_ref[...]
    lo_ref[...] = (jnp.concatenate([valid] * (width // LANES), axis=1) * (x + branch)).astype(BF16)
    out_copy = pltpu.make_async_copy(lo_ref, lo_out, sem)
    out_copy.start()
    du = dmix * n2
    e2 = dmix * u
    g2g_ref[...] = jnp.sum(e2 * ohat, axis=0, keepdims=True)
    do = norm_back(e2 * g2, ohat, scale2).astype(BF16)
    dh_ref[:, 0:width] = (du * h_ref[:, 0:width]).astype(BF16)
    for pair in range(pairs):
        cols = slice(pair * LANES, (pair + 1) * LANES)
        dom = stacked(do[:, cols])
        ds = (dot_nt(dom, v[:, cols]) * slope_ref[pair]).astype(BF16)
        ds_ref[2 * pair] = ds[:rows]
        ds_ref[2 * pair + 1] = ds[rows:]
        dv = dot_tn(a_ref[pair], dom)
        dq = dot_nn(abreast(ds), stacked(k[:, cols]))
        dk = dot_tn(ds, stacked(q[:, cols]))
        for part, value in ((1, dv), (2, dq * 0.125), (3, dk * 0.125)):
            at = slice(part * width + pair * LANES, part * width + (pair + 1) * LANES)
            dh_ref[:, at] = (value * h_ref[:, at]).astype(BF16)
    if staged:
        other = 1 - lax.axis_index("table")
        half_cols = 2 * width
        msg_ref[:, 0:half_cols] = dh_ref[:, pl.ds(pl.multiple_of(other * half_cols, half_cols), half_cols)]
        msg_ref[:, half_cols : half_cols + width] = n1
        half_y = width // 2
        y_half = y_ref[:, pl.ds(pl.multiple_of(other * half_y, half_y), half_y)].astype(F32)
        y_half = y_half * jnp.concatenate([valid] * (half_y // LANES), axis=1)
        msg_ref[:, half_cols + width :] = y_half.astype(BF16)
    else:
        msg_ref[...] = jnp.zeros_like(msg_ref)
    out_copy.wait()


SMALL_ROWS = 48


def prefix_ends(time_ref, rows, count):
    time_lane = 64
    row = iota((1, rows), 1).astype(F32)
    ends = [row - float(bound) for bound in pos_bounds(rows, count)]
    ends += [jnp.full((time_lane - count, rows), -1.0, F32)]
    stamp = jnp.broadcast_to(time_ref[...].astype(F32), (rows, rows))
    gaps = stamp - jnp.transpose(stamp)
    for bound in time_bounds(count):
        ends.append(jnp.sum(jnp.where(gaps >= bound, 1.0, 0.0), axis=0, keepdims=True) - 1.0)
    ends += [jnp.full((LANES - time_lane - count, rows), -1.0, F32)]
    return jnp.transpose(jnp.concatenate(ends, axis=0)).astype(I32)


def after_kernel(count, dh_ref, w_ref, x_ref, g1_ref, go_ref, ds_ref, time_ref, g2g_ref, *rest):
    dx_out, out_ref, dx_ref, sem = rest
    heads, rows, _ = ds_ref.shape
    xhat, scale = norm_of(x_ref[...].astype(F32))
    dn1 = dot_nt(dh_ref[...], w_ref[...])
    go = go_ref[...].astype(F32)
    dx_ref[...] = (norm_back(dn1 * g1_ref[...], xhat, scale) + go).astype(BF16)
    copy = pltpu.make_async_copy(dx_ref, dx_out, sem)
    copy.start()
    out_ref[...] = jnp.zeros_like(out_ref)
    g1_grad = jnp.sum(dn1 * xhat, axis=0, keepdims=True)
    b_grad = jnp.sum(dh_ref[...].astype(F32), axis=0, keepdims=True)
    go_sum = jnp.sum(go, axis=0, keepdims=True)
    at = 0
    for value in (b_grad, g1_grad, g2g_ref[...], go_sum):
        for col in range(0, value.shape[1], LANES):
            out_ref[at : at + 1, :] = value[:, col : col + LANES]
            at += 1
    at = (at + 7) // 8 * 8
    ends = prefix_ends(time_ref, rows, count)
    upto = jnp.where(iota((rows, rows), 0) <= iota((rows, rows), 1), 1.0, 0.0).astype(BF16)
    prefix = dot_nn(ds_ref[...].reshape(heads * rows, rows), upto)
    tables = [
        ((ends >= first) & (ends < first + LANES), jnp.clip(ends - first, 0, LANES - 1))
        for first in range(0, rows, LANES)
    ]
    sums = []
    for g in range(heads):
        total = jnp.zeros((1, LANES), F32)
        for n, (here, index) in enumerate(tables):
            lines = slice(n * LANES, rows)
            value = prefix[g * rows + n * LANES : (g + 1) * rows, n * LANES : (n + 1) * LANES]
            found = jnp.where(here[lines], jnp.take_along_axis(value, index[lines], axis=1), 0.0)
            total = total + jnp.sum(found, axis=0, keepdims=True)
        sums.append(total)
    sums = jnp.concatenate(sums, axis=0)
    out_ref[at : at + heads, :] = sums
    out_ref[at + heads : at + 2 * heads, 0 : LANES // 2] = sums[:, LANES // 2 :]
    copy.wait()


def place_of(columns):
    my_dp = lax.axis_index("dp")
    return lax.rem(my_dp, columns), lax.div(my_dp, columns)


def pack_kernel(planes, columns, dh_ref, n1_ref, y_ref, go_ref, got_ref, got_grad_ref, small_ref, *rest):
    nears, fars, (uv_ref, wo_ref) = rest[:columns], rest[columns : 2 * columns], rest[2 * columns :]
    width = n1_ref.shape[1]
    core = lax.axis_index("table")
    my_xy, my_z = place_of(columns)
    half_cols = 2 * width
    half_y = width // 2
    dh = jnp.concatenate(
        [dh_ref[:, pl.ds(pl.multiple_of(core * half_cols, half_cols), half_cols)], got_ref[:, 0:half_cols]],
        axis=0,
    )
    n1 = jnp.concatenate([n1_ref[...], got_ref[:, half_cols : half_cols + width]], axis=0)
    y = jnp.concatenate(
        [y_ref[:, pl.ds(pl.multiple_of(core * half_y, half_y), half_y)], got_ref[:, half_cols + width :]],
        axis=0,
    )
    go = jnp.concatenate([go_ref[...], got_grad_ref[...]], axis=0)
    uv_ref[...] = dot_tn(n1, dh).astype(BF16)
    wo_ref[...] = dot_tn(y, go).astype(BF16)
    short = half_y // (planes * columns)
    for rel_xy in range(columns):
        for rel_z in range(planes):
            chunk = jnp.bitwise_xor(my_xy, rel_xy) * planes + jnp.bitwise_xor(my_z, rel_z)
            out = (nears, fars)[rel_z // 2][rel_xy].at[rel_z % 2]
            for part in range(2):
                at = pl.multiple_of((2 * chunk + part) * short, short)
                out[:, part * half_cols : (part + 1) * half_cols] = uv_ref[pl.ds(at, short), :]
            at = pl.multiple_of(chunk * short, short)
            out[:, 2 * half_cols : 2 * half_cols + width] = wo_ref[pl.ds(at, short), :]
            out[:, 2 * half_cols + width :] = small_ref[pl.ds(at, short), :].astype(BF16)


def unpack(planes, columns, chunks, uvqk_ref, wout_ref, small_ref, held_uvqk, held_wout, sems):
    short = held_wout.shape[1]
    width = held_wout.shape[2]
    core = lax.axis_index("table")
    my_xy, my_z = place_of(columns)
    half_cols = 2 * width
    half_y = width // 2
    wout_lanes = slice(2 * half_cols, 2 * half_cols + width)
    small_lanes = slice(2 * half_cols + width, 2 * half_cols + width + LANES)
    copies = []
    for n, (rel_xy, rel_z, whose, piece) in enumerate(chunks):
        chunk = jnp.bitwise_xor(my_xy, rel_xy) * planes + jnp.bitwise_xor(my_z, rel_z)
        side = jnp.bitwise_xor(core, whose)
        for part in range(2):
            held_uvqk[n, part * short : (part + 1) * short, :] = piece[
                :, part * half_cols : (part + 1) * half_cols
            ].astype(F32)
        held_wout[n] = piece[:, wout_lanes].astype(F32)
        tall = pl.ds(pl.multiple_of(chunk * 2 * short, 2 * short), 2 * short)
        cols = pl.ds(pl.multiple_of(side * half_cols, half_cols), half_cols)
        rows = pl.ds(pl.multiple_of(side * half_y + chunk * short, short), short)
        copies += start_all(
            (held_uvqk.at[n], held_wout.at[n]),
            (uvqk_ref.at[tall, cols], wout_ref.at[rows, :]),
            sems.at[pl.ds(2 * n, 2)],
        )
        small_ref[pl.ds(pl.multiple_of(chunk * short, short), short), :] += piece[:, small_lanes].astype(F32)
    return copies


def chunks_of(planes, first_z, pieces, whose, first_xy=0):
    return [
        (first_xy + xy, first_z + z, whose, piece.at[z])
        for xy, piece in enumerate(pieces)
        for z in range(min(2, planes - first_z))
    ]


def unpack_first_kernel(planes, columns, *refs):
    mine, theirs = refs[: columns + 1], refs[columns + 1 : 2 * columns + 2]
    uvqk_ref, wout_ref, small_ref, *scratch = refs[2 * columns + 2 :]
    small_ref[...] = jnp.zeros_like(small_ref)
    chunks = []
    for whose, pieces in enumerate((mine, theirs)):
        chunks += chunks_of(planes, 0, pieces[:columns], whose) + chunks_of(planes, 2, pieces[columns:], whose)
    for copy in unpack(planes, columns, chunks, uvqk_ref, wout_ref, small_ref, *scratch):
        copy.wait()


def unpack_next_kernel(planes, columns, *refs):
    peers = columns - 1
    mine, before_ref = refs[:peers], refs[peers + 2]
    uvqk_ref, wout_ref, small_ref, *scratch = refs[peers + 3 :]
    small_ref[...] = before_ref[...]
    chunks = chunks_of(planes, 2, mine, 0, 1)
    for copy in unpack(planes, columns, chunks, uvqk_ref, wout_ref, small_ref, *scratch):
        copy.wait()


def unpack_last_kernel(planes, columns, *refs):
    peers = columns - 1
    theirs, before_ref = refs[:peers], refs[peers + 2]
    uvqk_ref, wout_ref, *small_outs = refs[peers + 3 : peers + 11]
    small_ref, *held, small_sems = refs[peers + 11 : peers + 19]
    b_ref, g1_ref, g2_ref, bo_ref, pos_ref, time_ref = held
    scratch = refs[peers + 19 :]
    small_ref[...] = before_ref[...]
    chunks = chunks_of(planes, 2, theirs, 1, 1)
    copies = unpack(planes, columns, chunks, uvqk_ref, wout_ref, small_ref, *scratch)
    at = 0
    for out in (b_ref, g1_ref, g2_ref, bo_ref):
        for col in range(0, out.shape[1], LANES):
            out[:, col : col + LANES] = small_ref[at : at + 1, :]
            at += 1
    at = (at + 7) // 8 * 8
    heads, count = pos_ref.shape
    pos_ref[...] = small_ref[at : at + heads, 0:count]
    time_ref[...] = small_ref[at + heads : at + 2 * heads, 0:count]
    for copy in copies + start_all(held, small_outs, small_sems):
        copy.wait()


def add_up(first, *rest):
    total = first.astype(F32)
    for other in rest:
        total = total + other.astype(F32)
    return total.astype(BF16)


def xor_step(value, size, step):
    return lax.ppermute(value, "dp", [(i, i ^ step) for i in range(size)])


def reduce_step(pieces, size, stride):
    return add_up(pieces[0], *(xor_step(pieces[k], size, k * stride) for k in range(1, len(pieces))))


def gather_step(own, size, stride, peers):
    return [own] + [xor_step(own, size, k * stride) for k in range(1, peers)]


def swap_cores(value):
    return lax.ppermute(value, "table", [(0, 1), (1, 0)])


def on_device(
    item_table,
    token_request_slot,
    request_rows,
    lengths,
    assignment,
    timestamps,
    item_counts,
    first_norm_gain,
    w_uvqk,
    b_uvqk,
    norm2_gain,
    w_out,
    b_out,
    pos_weight,
    time_weight,
    out_grad,
):
    rows = token_request_slot.shape[0]
    rows_dev, width = item_table.shape
    replicas = lax.axis_size("dp")
    groups = lax.axis_size("table")
    devices = replicas * groups
    cap = request_rows.shape[2]
    piece = rows // replicas
    heads, count = pos_weight.shape
    slots = devices * cap
    columns = 4
    planes = replicas // columns
    staged = (
        groups == 2
        and replicas == 16
        and width % (32 * replicas) == 0
        and (2 * heads + SMALL_ROWS - 16) <= width // 2
    )
    mb = MIB

    slot_row = token_request_slot.reshape(1, rows)
    time_row = timestamps.reshape(1, rows)
    counts_2d = item_counts.reshape(rows_dev // LANES, LANES)
    msg = call(
        functools.partial(request_kernel, piece, cap),
        shape_of((devices, LANES), I32),
        [HBM] * 5,
        mb,
        mb // 8,
        scratch=(
            pltpu.VMEM((cap, devices), I32),
            pltpu.VMEM((1, rows), I32),
            pltpu.VMEM(lengths.shape, I32),
            pltpu.VMEM(lengths.shape, I32),
            pltpu.VMEM(counts_2d.shape, I32),
            pltpu.SemaphoreType.DMA((5,)),
        ),
        room=64,
    )(request_rows.transpose(0, 2, 1).reshape(cap, devices), slot_row, lengths, assignment, counts_2d)
    if staged:
        msg, other_grad = lax.optimization_barrier((msg, out_grad))
        got_grad = swap_cores(other_grad)
    asked = lax.all_to_all(msg.reshape(devices, 1, LANES), BOTH, 0, 0, tiled=True).reshape(devices, LANES)
    if staged:
        asked, got_grad = lax.optimization_barrier((asked, got_grad))
    served = call(
        functools.partial(serve_kernel, cap), shape_of((slots, width), BF16), [VMEM] * 2, 1 << 30, 5 * mb
    )(asked, item_table)
    fetched = lax.all_to_all(served.reshape(devices, cap, width), BOTH, 0, 0, tiled=True)
    new_counts, log_q, asked_row = call(
        functools.partial(counts_kernel, cap, rows_dev * devices),
        (
            shape_of((rows_dev // LANES, LANES), I32),
            shape_of((rows_dev // LANES, LANES), F32),
            shape_of((8, slots), F32),
        ),
        [VMEM] * 2,
        64 * mb,
        mb,
    )(asked, counts_2d)
    home = call(take_kernel, shape_of((rows, width), BF16), [VMEM] * 2, 64 * mb, mb)(
        slot_row, fetched.reshape(slots, width)
    )
    x = lax.all_to_all(home.reshape(replicas, piece, width), "dp", 0, 0, tiled=True).reshape(rows, width)

    half_cols = 2 * width
    g1, g2 = first_norm_gain.reshape(1, width), norm2_gain.reshape(1, width)
    msg_cols = half_cols + width + width // 2 if staged else LANES
    layer_out, n1, y, go, dh, ds, g2_grad, to_core = call(
        functools.partial(layer_kernel, staged),
        (
            shape_of((rows, width), BF16),
            shape_of((rows, width), BF16),
            shape_of((rows, width), BF16),
            shape_of((rows, width), BF16),
            shape_of((rows, 4 * width), BF16),
            shape_of((heads, rows, rows), BF16),
            shape_of((1, width), F32),
            shape_of((rows, msg_cols), BF16),
        ),
        [VMEM] * 13,
        2 << 30,
        8 * mb,
        scratch=(
            pltpu.VMEM((rows, 4 * width), F32),
            pltpu.VMEM((heads // 2, 2 * rows, rows), F32),
            pltpu.VMEM((heads // 2, 2 * rows, rows), BF16),
            pltpu.VMEM((rows, width), BF16),
            pltpu.SemaphoreType.DMA,
        ),
        room=24,
        out_specs=(HBM,) + (VMEM,) * 7,
    )(
        x,
        w_uvqk,
        b_uvqk.reshape(1, 4 * width),
        g1,
        g2,
        w_out,
        b_out.reshape(1, width),
        lengths,
        assignment,
        time_row,
        out_grad,
        pos_weight,
        time_weight,
    )
    def home_again(dx):
        return lax.all_to_all(dx.reshape(replicas, piece, width), "dp", 0, 0, tiled=True).reshape(rows, width)

    def to_owners(back):
        return send_sums(slot_sums(back))

    def slot_sums(back):
        return call(slot_sum_kernel, shape_of((slots, width), BF16), [VMEM] * 2, 64 * mb, mb)(slot_row, back)
    def send_sums(sums):
        sums = lax.all_to_all(sums.reshape(devices, cap, width), BOTH, 0, 0, tiled=True)
        return sums.reshape(slots, width)

    def into_table(got_sums):
        block = min(512, rows_dev)
        return call(
            scatter_kernel,
            shape_of((rows_dev, width), F32),
            [VMEM] * 2,
            1 << 30,
            8 * mb,
            scratch=(
                pltpu.VMEM((rows_dev // block, block, width), F32),
                pltpu.SemaphoreType.DMA((rows_dev // block,)),
            ),
            room=24,
            out_specs=HBM,
        )(asked_row, got_sums)

    if staged:
        got = swap_cores(to_core)
    dx, small = call(
        functools.partial(after_kernel, count),
        (shape_of((rows, width), BF16), shape_of((width // 2, LANES), F32)),
        [VMEM] * 8,
        1 << 29,
        4 * mb,
        scratch=(pltpu.VMEM((rows, width), BF16), pltpu.SemaphoreType.DMA),
        out_specs=(HBM, VMEM),
    )(dh, w_uvqk, x, g1, go, ds, time_row, g2_grad)
    if staged:
        short = width // replicas // 2
        pieces = call(
            functools.partial(pack_kernel, planes, columns),
            tuple(shape_of((2, short, 5 * width + LANES), BF16) for _ in range(2 * columns)),
            [VMEM] * 7,
            1 << 30,
            6 * mb,
            scratch=(pltpu.VMEM((width, half_cols), BF16), pltpu.VMEM((width // 2, width), BF16)),
        )(dh, n1, y, go, got, got_grad, small)
        dx, *pieces = lax.optimization_barrier((dx, *pieces))
        nears, fars = pieces[:columns], pieces[columns:]
        back = home_again(dx)
        got_far = [xor_step(fars[k], replicas, k) for k in range(1, columns)]
        nears, got_far[0] = lax.optimization_barrier((nears, got_far[0]))
        far_line = add_up(fars[0], *got_far)
        got_line = [xor_step(far_line[k - 2], replicas, k * columns) for k in range(2, planes)]
        near_line = reduce_step(nears, replicas, 1)
        near_line, back = lax.optimization_barrier((near_line, back))
        got_next = xor_step(near_line[1], replicas, columns)
        sums = slot_sums(back)
        own = add_up(near_line[0], got_next, *got_line)
        own, sums = lax.optimization_barrier((own, sums))
        next_own = xor_step(own, replicas, columns)
        far = [xor_step(own, replicas, k * columns) for k in range(2, planes)]
        near = jnp.stack([own, next_own])
        nears = gather_step(near, replicas, 1, columns)
        far[1], sums = lax.optimization_barrier((far[1], sums))
        got_sums = send_sums(sums)
        far = jnp.stack(far)
        table_grad = into_table(got_sums)
        fars = gather_step(far, replicas, 1, columns)
        their_nears = [swap_cores(piece) for piece in nears]
        their_far = swap_cores(far)
        small_shape = shape_of((width // 2, LANES), F32)
        wide_shapes = (shape_of((width, 4 * width), F32), shape_of((width, width), F32))

        def unpack_call(body, specs, outs, chunks, scratch=(), aliases=None, place=VMEM):
            return call(
                functools.partial(body, planes, columns),
                wide_shapes + outs,
                specs,
                mb,
                3 * mb,
                scratch=scratch
                + (
                    pltpu.VMEM((chunks, 2 * short, half_cols), F32),
                    pltpu.VMEM((chunks, short, width), F32),
                    pltpu.SemaphoreType.DMA((2 * chunks,)),
                ),
                out_specs=(HBM, HBM) + (place,) * len(outs),
                aliases=aliases,
            )

        peers = columns - 1
        wides = {peers: 0, peers + 1: 1}
        wide_specs = [VMEM] * peers + [HBM, HBM, VMEM]
        *sums_so_far, small_sum = unpack_call(
            unpack_first_kernel, [VMEM] * (2 * columns + 2), (small_shape,), 2 * (2 * columns + 2)
        )(*nears, far, *their_nears, their_far)
        fars, small_sum, table_grad = lax.optimization_barrier((fars, small_sum, table_grad))
        their_fars = [swap_cores(piece) for piece in fars[1:]]
        *sums_so_far, small_sum = unpack_call(
            unpack_next_kernel, wide_specs, (small_shape,), 2 * peers, aliases=wides
        )(*fars[1:], *sums_so_far, small_sum)
        small_outs = ((1, 4 * width),) + ((1, width),) * 3 + ((heads, count),) * 2
        w_uvqk_sum, w_out_sum, b_sum, g1_sum, g2_sum, bo_sum, pos_sum, time_sum = unpack_call(
            unpack_last_kernel,
            wide_specs,
            tuple(shape_of(shape, F32) for shape in small_outs),
            2 * peers,
            scratch=(
                pltpu.VMEM(small_shape.shape, F32),
                *(pltpu.VMEM(shape, F32) for shape in small_outs),
                pltpu.SemaphoreType.DMA((len(small_outs),)),
            ),
            aliases=wides,
            place=HBM,
        )(*their_fars, *sums_so_far, small_sum)
    else:
        table_grad = into_table(to_owners(home_again(dx)))
        w_uvqk_sum, w_out_sum, parts = lax.psum((dot_tn(n1, dh), dot_tn(y, go), small[0:SMALL_ROWS]), BOTH)
        at = 4 * width // LANES
        step = width // LANES
        b_sum = parts[0:at]
        g1_sum, g2_sum, bo_sum = (parts[at + n * step : at + (n + 1) * step] for n in range(3))
        at = (at + 3 * step + 7) // 8 * 8
        pos_sum = parts[at : at + heads, 0:count]
        time_sum = parts[at + heads : at + 2 * heads, 0:count]
    return (
        layer_out,
        table_grad,
        g1_sum.reshape(width),
        w_uvqk_sum,
        b_sum.reshape(4 * width),
        g2_sum.reshape(width),
        w_out_sum,
        bo_sum.reshape(width),
        pos_sum,
        time_sum,
        new_counts.reshape(rows_dev),
        log_q.reshape(rows_dev),
    )


def solution(mesh):
    split = P(("dp", "table"))
    rows_split = P(("dp", "table"), None)
    placed = (
        rows_split,
        split,
        P(("dp", "table"), None, None),
        P("table", None),
        P("table", None),
        split,
        split,
        P(),
        P(),
        P(),
        P(),
        P(),
        P(),
        P(),
        P(),
        rows_split,
    )
    return jax.shard_map(
        on_device,
        mesh=mesh,
        in_specs=placed,
        out_specs=(rows_split, rows_split, P(), P(), P(), P(), P(), P(), P(), P(), split, split),
        check_vma=False,
    )
```
